128 devices in a mesh: dom: 128 (over y, z, x, core).
Axes of the slice: x: 4, y: 4, z: 4, core: 2. Of those that a mesh axis runs over, the one named last changes fastest.
Arguments:
- rest_pos: float32 [3, 524288], P(None, 'dom'), may hold values from -6 to 6
- displacement: float32 [3, 524288], P(None, 'dom'), may hold values from -3 to 3
- velocity: float32 [3, 524288], P(None, 'dom'), may hold values from -6 to 6
- ext_force: float32 [3, 524288], P(None, 'dom'), may hold values from -6 to 6
- node_mass: float32 [524288], P('dom'), may hold values from 0.5 to 2
- body_accel: float32 [3], replicated, may hold values from -2 to 2
- connectivity: int32 [8, 524288], P(None, 'dom'), may hold values from 0 to 4095
- elem_material: int32 [4096], P('dom'), may hold values from 0 to 7
- stiffness: float32 [8, 24, 24], replicated, may hold values from -1.25 to 1.25
- shared_nodes: int32 [128, 5, 128], P('dom'), may hold values from 0 to 4095, as said below
- contact_slave: int32 [262144], P('dom'), may hold values from 0 to 4095
- contact_owner: int32 [262144, 1], P('dom'), may hold values from 0 to 127; in each aligned block of 2048 rows (0 to 2047, 2048 to 4095, ...) at most 64 rows name the same one
- contact_master: int32 [262144], P('dom'), may hold values from 0 to 4095
- contact_normal: float32 [3, 262144], P(None, 'dom'), may hold values from -4 to 4
- part_of_node: int32 [524288], P('dom'), may hold values from 0 to 799
- part_mass: float32 [400], replicated, may hold values from 327 to 1310
- part_center: float32 [3, 400], replicated, may hold values from -1 to 1
- part_inertia: float32 [3, 400], replicated, may hold values from 327 to 1310
Outputs:
- nodal_velocity: float32 [3, 524288], P(None, 'dom')
- part_motion: float32 [6, 400], replicated
The draws below stay inside these ranges and needn't reach their ends.
Inputs may be any that keep to these rules, and one draw needn't show every extreme that they name: `connectivity`: offsets are taken modulo 4096 after adding the element's own local number. `shared_nodes`: on each partition d the 5 x 128 entries are distinct interface copies; entry k of list b on d and entry k of list b on d XOR 2**b are copies of one node. `contact_slave`: slave indices are local copies of the contact's own partition. `contact_owner`: among the 2048 contacts of one partition no owner appears more than 64 times, and some owner appears exactly 64 times. `contact_master`: master indices are local copies of the owner partition. `part_of_node`: values of 400 or more mark copies of no rigid part.
All inputs are finite; a program needn't handle non-finite values.
Results may differ from the reference program's by a relative error of at most 0.0001.
Values sent between devices are 32-bit elements; how exact they have to be, the bound alone decides.
No kernel may reach another device: no remote copies, remote signals or barrier semaphores. Data moves between devices by JAX's collectives and lax.ppermute only.
A program may use at most 128 MiB of HBM per device.

```python
import math
import jax
import jax.numpy as jnp
import numpy as np
from jax import lax

NODE_DEV = 4096
E_DEV = 4096
SH = 128
NBR = 5
C_DEV = 2048
CAP = 64
CYCLES = 3
MATS = 8
PARTS_SIZE = 400
DOMS = 128
NODES = 524288
ELEMS = 524288
BLOCKS = 4096
CONTACTS = 262144


def draw_shared_nodes(key, part):
    domain_keys = jax.random.split(key, DOMS)
    orders = jax.vmap(lambda one_key: jax.random.permutation(one_key, NODE_DEV))(domain_keys)
    return orders[:, :NBR * SH].reshape(DOMS, NBR, SH).astype(jnp.int32)


def with_ends(drawn, stream_key, low, largest):
    longest = drawn.shape.index(max(drawn.shape))
    spots = []
    for shift in (0, 1):
        where = [jax.random.randint(jax.random.fold_in(stream_key, axis), (), 0, length) for axis, length in enumerate(drawn.shape)]
        where[longest] = (where[longest] + shift) % drawn.shape[longest]
        spots.append(tuple(where))
    return drawn.at[spots[0]].set(low).at[spots[1]].set(largest)


def levels(key, shape, cuts, smallest, largest):
    level = 1.0
    for dim, shards_of in cuts:
        steps = jax.random.uniform(jax.random.fold_in(jax.random.fold_in(key, 6), dim), (shards_of,), jnp.float32, smallest / len(cuts), largest / len(cuts))
        level = level * jnp.repeat(jnp.exp(steps), shape[dim] // shards_of).reshape((-1,) + (1,) * (len(shape) - 1 - dim))
    return level


def assign_block(key, own, number, rows, count, top, bound, lean):
    ranking = jax.random.permutation(key, count)
    heavy_load, common = load_shares(count, rows * top, bound, lean, True), load_shares(count, rows * top, bound, lean, False)
    places = jnp.arange(count)

    def named(tallies, rotation):
        used = int((tallies > 0).sum())
        fixed = max(1, used // 4)
        shifted = fixed + (places - fixed + rotation * (used - fixed)) % max(1, count - fixed)
        return jnp.zeros((count,), jnp.int32).at[ranking[jnp.where(places < fixed, places, shifted)]].set(jnp.asarray(tallies, jnp.int32))

    tallies = jnp.where(number % 4 == 0, named(heavy_load, number // 4), named(common, number - number // 4 - 1))
    mixed = jax.random.permutation(jax.random.fold_in(own, 3), count)
    donor, receiver = mixed[0:count // 2 * 2:2], mixed[1:count // 2 * 2:2]
    slack = jnp.minimum(tallies[donor] - 1, bound - tallies[receiver]) // 2
    slack = jnp.where((donor == ranking[0]) | (receiver == ranking[0]) | (tallies[receiver] == 0), 0, jnp.maximum(slack, 0))
    shifted = jax.random.randint(jax.random.fold_in(own, 4), (count // 2,), 0, 1 << 20) % (slack + 1)
    tallies = tallies.at[donor].add(-shifted).at[receiver].add(shifted)
    labels = jnp.searchsorted(jnp.cumsum(tallies), jnp.arange(rows * top), side="right").astype(jnp.int32)
    listing = labels.reshape(top, rows).T
    listing = listing[jax.random.permutation(jax.random.fold_in(own, 1), rows)]
    rotation = jax.random.randint(jax.random.fold_in(own, 2), (rows, 1), 0, top)
    return jnp.take_along_axis(listing, (jnp.arange(top)[None, :] + rotation) % top, axis=1)


def load_shares(amount, total, most, lean, full):
    loads = [(1 << 20) // math.isqrt(standing ** lean) + 1 for standing in range(1, amount + 1)]
    largest = most if full else min(most, max(-(-total // amount), total * loads[0] // sum(loads)))
    least = 1 if total - largest >= amount - 1 else 0
    given, surplus = [largest] + [least] * (amount - 1), total - largest - least * (amount - 1)
    while surplus > 0:
        movable = [i for i in range(1, amount) if given[i] < largest] or [i for i in range(1, amount) if given[i] < most]
        pool, budget = sum([loads[i] for i in movable]), surplus
        for i in movable:
            more = min(most - given[i], max(1, budget * loads[i] // pool), surplus)
            given[i] = given[i] + more
            surplus = surplus - more
    return np.array(given)


def centred(rng, shape, spread, bound, cuts=(), kind=jnp.bfloat16):
    result = spread * jax.random.normal(rng, shape, jnp.float32)
    if cuts:
        result = result * levels(rng, shape, cuts, -0.22, 0.18)
    return jnp.clip(result, -bound, bound).astype(kind)


def setup_inputs(seed: int = 0) -> dict:
    keys = jax.random.split(jax.random.key(seed), 19)
    rest_pos = centred(keys[0], (3, NODES), 1.0, 6.0, ((1, 128),), jnp.float32)
    displacement = centred(keys[1], (3, NODES), 0.2, 3.0, ((1, 128),), jnp.float32)
    velocity = centred(keys[2], (3, NODES), 1.0, 6.0, ((1, 128),), jnp.float32)
    ext_force = centred(keys[3], (3, NODES), 1.0, 6.0, ((1, 128),), jnp.float32)
    node_mass = jnp.clip(jnp.exp(math.log(2.0) - 1.3862944 * jax.random.uniform(keys[4], (NODES,), jnp.float32) ** levels(keys[4], (NODES,), ((0, 128),), -0.2, 0.2)), 0.5, 2.0)
    body_accel = jnp.clip(jax.random.uniform(keys[5], (3,), jnp.float32, -2.0, 2.0), -2.0, 2.0)
    connectivity = with_ends(jax.random.randint(keys[6], (8, ELEMS), 0, min(NODE_DEV, 16368)), jax.random.fold_in(keys[6], 1), 0, (min(NODE_DEV, 16368)) - 1).astype(jnp.int32)
    elem_material = with_ends(jax.random.randint(keys[7], (BLOCKS,), 0, MATS), jax.random.fold_in(keys[7], 1), 0, MATS - 1).astype(jnp.int32)
    stiffness = centred(keys[8], (MATS, 24, 24), 24 ** -0.5, 1.25, (), jnp.float32)
    shared_nodes = draw_shared_nodes(jax.random.fold_in(keys[18], 71), 0)
    contact_slave = with_ends(jax.random.randint(keys[10], (CONTACTS,), 0, NODE_DEV), jax.random.fold_in(keys[10], 1), 0, NODE_DEV - 1).astype(jnp.int32)
    contact_owner_keys = jax.random.split(jax.random.fold_in(keys[11], 1), CONTACTS // C_DEV)
    contact_owner_turns = jax.random.permutation(jax.random.fold_in(keys[11], 3), CONTACTS // C_DEV)
    contact_owner = jax.vmap(lambda own, number: assign_block(jax.random.fold_in(keys[11], 2), own, number, C_DEV, DOMS, 1, CAP, 2))(contact_owner_keys, contact_owner_turns).reshape((CONTACTS, 1))
    contact_master = with_ends(jax.random.randint(keys[12], (CONTACTS,), 0, NODE_DEV), jax.random.fold_in(keys[12], 1), 0, NODE_DEV - 1).astype(jnp.int32)
    contact_normal = centred(keys[13], (3, CONTACTS), 0.6, 4.0, ((1, 128),), jnp.float32)
    part_of_node = with_ends(jax.random.randint(keys[14], (NODES,), 0, 2 * PARTS_SIZE), jax.random.fold_in(keys[14], 1), 0, (2 * PARTS_SIZE) - 1).astype(jnp.int32)
    part_mass = jnp.clip(jnp.exp(jax.random.uniform(keys[15], (PARTS_SIZE,), jnp.float32, math.log(327.0), math.log(1310.0))), 327.0, 1310.0)
    part_center = jnp.clip(jax.random.uniform(keys[16], (3, PARTS_SIZE), jnp.float32, -1.0, 1.0), -1.0, 1.0)
    part_inertia = jnp.clip(jnp.exp(jax.random.uniform(keys[17], (3, PARTS_SIZE), jnp.float32, math.log(327.0), math.log(1310.0))), 327.0, 1310.0)
    return dict(rest_pos=rest_pos, displacement=displacement, velocity=velocity, ext_force=ext_force, node_mass=node_mass, body_accel=body_accel, connectivity=connectivity, elem_material=elem_material, stiffness=stiffness, shared_nodes=shared_nodes, contact_slave=contact_slave, contact_owner=contact_owner, contact_master=contact_master, contact_normal=contact_normal, part_of_node=part_of_node, part_mass=part_mass, part_center=part_center, part_inertia=part_inertia)


TIME_STEP = 0.1
DAMP_RATIO = 0.05
PENALTY = 2.0
GAP_WIDTH = 0.5
CONTACT_DAMP = 0.2


def element_forces(corners, material, stiffness, nodal_field):
    blocks = corners.shape[1] // 128
    gathered = nodal_field[:, corners].reshape(24, blocks, 128)
    block_matrix = stiffness[material]
    forces = jnp.einsum("bij,jbk->ibk", block_matrix, gathered, precision=lax.Precision.HIGHEST)
    return jnp.zeros_like(nodal_field).at[:, corners.reshape(-1)].add(forces.reshape(3, 8 * corners.shape[1]))


def contact_push(slave_pos, slave_vel, master_pos, master_vel, normal):
    gap_size = jnp.sum((slave_pos - master_pos) * normal, axis=0)
    closing = jnp.sum((slave_vel - master_vel) * normal, axis=0)
    push_size = PENALTY * GAP_WIDTH * jax.nn.softplus(-gap_size / GAP_WIDTH) - CONTACT_DAMP * closing
    return push_size[None] * normal


def cross_product(left, right):
    return jnp.stack([left[1] * right[2] - left[2] * right[1], left[2] * right[0] - left[0] * right[2], left[0] * right[1] - left[1] * right[0]])


def by_domain(array_in):
    return array_in.reshape(array_in.shape[0], DOMS, NODE_DEV).transpose(1, 0, 2)


def to_global(array_in):
    return array_in.transpose(1, 0, 2).reshape(array_in.shape[1], NODES)


def take_columns(values_one, index_one):
    return values_one[:, index_one]


def add_columns(values_one, index_one, added_one):
    return values_one.at[:, index_one].add(added_one)


def reference(rest_pos, displacement, velocity, ext_force, node_mass, body_accel, connectivity, elem_material, stiffness, shared_nodes, contact_slave, contact_owner, contact_master, contact_normal, part_of_node, part_mass, part_center, part_inertia):
    displaced = by_domain(displacement)
    speeds = by_domain(velocity)
    applied = by_domain(ext_force)
    masses = node_mass.reshape(DOMS, 1, NODE_DEV)
    local_elem = jnp.arange(E_DEV, dtype=jnp.int32)
    corners = (connectivity.reshape(8, DOMS, E_DEV).transpose(1, 0, 2) + local_elem[None, None, :]) % NODE_DEV
    material = elem_material.reshape(DOMS, E_DEV // 128)
    shared_flat = shared_nodes.reshape(DOMS, NBR * SH)
    domain_ids = jnp.arange(DOMS, dtype=jnp.int32)
    accel_column = body_accel[None, :, None]

    def one_domain(inputs):
        return element_forces(inputs[0], inputs[1], stiffness, inputs[2])

    assembled = jnp.zeros_like(displaced)
    for cycle_index in range(CYCLES):
        internal = lax.map(one_domain, (corners, material, displaced + DAMP_RATIO * speeds))
        own_values = jax.vmap(take_columns)(internal, shared_flat).reshape(DOMS, 3, NBR, SH)
        pieces = [own_values[domain_ids ^ (1 << bit_number), :, bit_number] for bit_number in range(NBR)]
        received = jnp.stack(pieces, axis=2).reshape(DOMS, 3, NBR * SH)
        assembled = jax.vmap(add_columns)(internal, shared_flat, received)
        speeds = speeds + TIME_STEP * ((applied - assembled) / masses - accel_column)
        displaced = displaced + TIME_STEP * speeds

    positions = to_global(by_domain(rest_pos) + displaced)
    speeds_all = to_global(speeds)
    last_internal = to_global(assembled)
    contact_domain = jnp.arange(CONTACTS, dtype=jnp.int32) // C_DEV
    slave_node = contact_domain * NODE_DEV + contact_slave
    master_node = contact_owner[:, 0] * NODE_DEV + contact_master
    pushed = contact_push(positions[:, slave_node], speeds_all[:, slave_node], positions[:, master_node], speeds_all[:, master_node], contact_normal)
    contact = jnp.zeros_like(positions).at[:, slave_node].add(pushed).at[:, master_node].add(-pushed)
    nodal_velocity = speeds_all + TIME_STEP * contact / node_mass[None]
    net_force = ext_force - last_internal + contact - node_mass[None] * body_accel[:, None]

    part_index = jnp.minimum(part_of_node, PARTS_SIZE)

    def segment_rows(columns_in):
        return jax.ops.segment_sum(columns_in.T, part_index, PARTS_SIZE + 1)[:PARTS_SIZE].T

    mass_moments = segment_rows(jnp.concatenate([node_mass[None], node_mass[None] * positions], 0))
    mass_total = part_mass + mass_moments[0]
    centre = (part_mass[None] * part_center + mass_moments[1:4]) / mass_total[None]
    centre_ext = jnp.concatenate([centre, jnp.zeros((3, 1), centre.dtype)], 1)
    lever_arm = positions - centre_ext[:, part_index]
    load_sums = segment_rows(jnp.concatenate([net_force, cross_product(lever_arm, net_force)], 0))
    part_motion = jnp.concatenate([load_sums[0:3] / mass_total[None], load_sums[3:6] / part_inertia], 0)
    return nodal_velocity, part_motion
```

```python
import jax
import jax.numpy as jnp
from jax import lax
from jax.experimental import pallas as pl
from jax.experimental.pallas import tpu as pltpu
from jax.sharding import PartitionSpec as P

CYCLES = 3
PARTS_SIZE = 400

TIME_STEP = 0.1
DAMP_RATIO = 0.05
PENALTY = 2.0
GAP_WIDTH = 0.5
CONTACT_DAMP = 0.2

BF = jnp.bfloat16
F32 = jnp.float32
NT = (((1,), (1,)), ((), ()))
LANES = 128
ROWS = 32
NBR = 5
TOGETHER = 4

VMEM = pl.BlockSpec(memory_space=pltpu.VMEM)
SMEM = pl.BlockSpec(memory_space=pltpu.SMEM)


def call(body, outs, in_specs, name, scratch=(), flops=0):
    return pl.pallas_call(
        body,
        out_shape=[jax.ShapeDtypeStruct(s, d) for s, d in outs],
        in_specs=in_specs,
        out_specs=[VMEM] * len(outs),
        scratch_shapes=list(scratch),
        compiler_params=pltpu.CompilerParams(vmem_limit_bytes=40 << 20),
        cost_estimate=pl.CostEstimate(flops=flops, bytes_accessed=1 << 20, transcendentals=0),
        name=name,
    )


def lanes_of(row, idx):
    return jnp.take_along_axis(row, idx, axis=1, mode="promise_in_bounds")


def gather(tab, bases, lo, hi):
    acc = [None] * len(bases)
    for h in range(ROWS):
        here = hi == h
        for c, base in enumerate(bases):
            row = jnp.broadcast_to(tab[base + h : base + h + 1, :], (8, LANES))
            val = lanes_of(row, lo)
            acc[c] = val if h == 0 else jnp.where(here, val, acc[c])
    return acc


def halves(x):
    first = x.astype(BF)
    return first, (x - first.astype(F32)).astype(BF)


def wide(x, a, n):
    row = jnp.broadcast_to(x[a : a + 1, :].astype(F32), (16, LANES)).astype(BF)
    return jnp.concatenate([row] * (n // 16), 0)


def iota_rows(n):
    return lax.broadcasted_iota(jnp.int32, (n, LANES), 0).astype(F32).astype(BF)


def place(lo, hi, vals):
    lof, hif = lo.astype(F32), hi.astype(F32)
    it = iota_rows(LANES)
    split = [halves(v) for v in vals]
    one, zero = jnp.ones((LANES, LANES), BF), jnp.zeros((LANES, LANES), BF)
    left, right = [], []
    for a in range(8):
        right.append(jnp.where(wide(lof, a, LANES) == it, one, zero))
        mask = wide(hif, a, ROWS) == it[:ROWS]
        left.append(
            jnp.concatenate(
                [
                    jnp.where(mask, wide(split[c][s], a, ROWS), zero[:ROWS])
                    for s in range(2)
                    for c in range(len(vals))
                ],
                0,
            )
        )
    return jnp.concatenate(left, 1), jnp.concatenate(right, 1)


def add_placed(acc, lo, hi, vals):
    left, right = place(lo, hi, vals)
    acc[...] += lax.dot_general(left, right, NT, preferred_element_type=F32)


def to_rows(src, dst):
    for c in range(3):
        for h in range(ROWS):
            dst[c * ROWS + h : c * ROWS + h + 1, :] = src[c : c + 1, h * LANES : (h + 1) * LANES]


def shared_split(shared):
    idx = jnp.concatenate([shared[...], jnp.zeros((8 - NBR, LANES), jnp.int32)], 0)
    return idx & 127, idx >> 7


def elements(conn, mat, tab, cols, g, acc):
    acc[...] = jnp.zeros_like(acc)
    lane = lax.broadcasted_iota(jnp.int32, (8, LANES), 1)

    def step(i, carry):
        for q in range(TOGETHER):
            b = i * TOGETHER + q
            off = pl.multiple_of(b * LANES, LANES)
            idx = (conn[:, pl.ds(off, LANES)] + lane + off) & 4095
            lo, hi = idx & 127, idx >> 7
            vals = gather(tab, (0, ROWS, 2 * ROWS), lo, hi)
            for c in range(3):
                g[q * 24 + 8 * c : q * 24 + 8 * c + 8, :] = vals[c]
            first = mat[b] * 24
            force = [jnp.zeros((8, LANES), F32)] * 3
            for j in range(24):
                col = cols.at[first + j]
                row = jnp.broadcast_to(g[q * 24 + j : q * 24 + j + 1, :], (8, LANES))
                force = [force[c] + col[8 * c : 8 * c + 8, :] * row for c in range(3)]
            add_placed(acc, lo, hi, force)
        return carry

    lax.fori_loop(0, ROWS // TOGETHER, step, 0)


def finish_internal(acc, internal, shared, own):
    internal[...] = acc[0:96, :] + acc[96:192, :]
    lo, hi = shared_split(shared)
    vals = gather(internal, (0, ROWS, 2 * ROWS), lo, hi)
    for b in range(NBR):
        for c in range(3):
            own[b][c : c + 1, :] = vals[c][b : b + 1, :]


def first_kernel(disp, vel, force, conn, mat, stiff, shared, *rest):
    u, v, f, internal, inv, cols = rest[:6]
    own = rest[6:11]
    tab, g, acc, small = rest[11:]
    to_rows(disp, u)
    to_rows(vel, v)
    to_rows(force, f)
    tab[...] = u[...] + DAMP_RATIO * v[...]
    for m in range(8):
        for j in range(24):
            cols[m * 24 + j] = jnp.broadcast_to(stiff[m * 24 : (m + 1) * 24, j : j + 1], (24, LANES))
    lo, hi = shared_split(shared)
    lane = lax.broadcasted_iota(jnp.int32, (8, LANES), 1).astype(F32)
    row = lax.broadcasted_iota(jnp.int32, (8, LANES), 0).astype(F32)
    small[...] = jnp.zeros_like(small)
    held = row < NBR
    add_placed(small, lo, hi, [jnp.where(held, lane, 0.0), jnp.where(held, row + 1.0, 0.0)])
    inv[...] = (small[0:64, :] + small[64:128, :]).astype(jnp.int32)
    elements(conn, mat, tab, cols, g, acc)
    finish_internal(acc, internal, shared, own)


def update(u, v, internal, inv, f, mass, accel, recv, c, r):
    at = slice(c * ROWS + r, c * ROWS + r + 8)
    slot, which = inv[r : r + 8, :], inv[ROWS + r : ROWS + r + 8, :]
    total = internal[at, :]
    for b in range(NBR):
        row = jnp.broadcast_to(recv[b][c : c + 1, :], (8, LANES))
        total = total + jnp.where(which == b + 1, lanes_of(row, slot), 0.0)
    speed = v[at, :] + TIME_STEP * ((f[at, :] - total) / mass[r : r + 8, :] - accel[c])
    return at, u[at, :] + TIME_STEP * speed, speed, total


def next_kernel(u, v, internal, inv, f, mass, accel, conn, mat, cols, shared, *rest):
    recv = rest[:5]
    u2, v2, internal2 = rest[5:8]
    own = rest[8:13]
    tab, g, acc = rest[13:]
    for c in range(3):
        for r in range(0, ROWS, 8):
            at, disp, speed, _ = update(u, v, internal, inv, f, mass, accel, recv, c, r)
            u2[at, :] = disp
            v2[at, :] = speed
            tab[at, :] = disp + DAMP_RATIO * speed
    elements(conn, mat, tab, cols, g, acc)
    finish_internal(acc, internal2, shared, own)


def slot_kernel(slave, owner, master, normal, send, sidx, acc):
    acc[...] = jnp.zeros_like(acc)
    down = lax.broadcasted_iota(jnp.int32, (LANES, LANES), 0)
    across = lax.broadcasted_iota(jnp.int32, (LANES, LANES), 1)
    before = jnp.where(down < across, 1.0, 0.0).astype(BF)
    carry = jnp.zeros((LANES, 1), F32)
    for t in range(16):
        hit = jnp.where(jnp.broadcast_to(owner[t : t + 1, :], (LANES, LANES)) == down, 1.0, 0.0)
        hitb = hit.astype(BF)
        count = jnp.dot(hitb, before, preferred_element_type=F32) + carry
        rank = jnp.sum(hit * count, axis=0, keepdims=True)
        carry = carry + jnp.sum(hit, axis=1, keepdims=True)
        mine = jnp.broadcast_to(rank, (64, LANES)) == down[:64].astype(F32)
        vals = [normal[c : c + 1, t * LANES : (t + 1) * LANES] for c in range(3)]
        vals += [master[t : t + 1, :].astype(F32), slave[t : t + 1, :].astype(F32)]
        left = [jnp.broadcast_to(x, (64, LANES)) for x in vals]
        for s in range(3):
            piece = [jnp.where(mine, x, 0.0).astype(BF) for x in left]
            left = [x - x.astype(BF).astype(F32) for x in left]
            acc[:, 0:320] += lax.dot_general(
                hitb, jnp.concatenate(piece, 0), NT, preferred_element_type=F32
            )
    send[...] = acc[:, 0:256]
    sidx[...] = acc[:, 256:384]


def dots_kernel(u, v, internal, inv, f, mass, accel, pos, send, sidx, got, *rest):
    recv = rest[:5]
    x2, v2, net, dots, idx, nrm = rest[5:11]
    tab = rest[11]
    to_rows(pos, x2)
    for c in range(3):
        for r in range(0, ROWS, 8):
            at, disp, speed, total = update(u, v, internal, inv, f, mass, accel, recv, c, r)
            place_now = x2[at, :] + disp
            x2[at, :] = place_now
            v2[at, :] = speed
            net[at, :] = f[at, :] - total - mass[r : r + 8, :] * accel[c]
            tab[at, :] = place_now
            tab[c * ROWS + 96 + r : c * ROWS + 96 + r + 8, :] = speed
    left = lax.broadcasted_iota(jnp.int32, (LANES, LANES), 1) < 64
    own0, own1 = send[:, 0:128], send[:, 128:256]
    got0, got1 = got[:, 0:128], got[:, 128:256]
    nrm[0] = jnp.where(left, own0, pltpu.roll(got0, 64, 1))
    nrm[1] = jnp.where(left, pltpu.roll(own0, 64, 1), got0)
    nrm[2] = jnp.where(left, own1, pltpu.roll(got1, 64, 1))
    idx[...] = jnp.where(left, sidx[...], got1).astype(jnp.int32)

    def step(i, carry):
        for q in range(2):
            off = pl.multiple_of(i * 16 + q * 8, 8)
            here = idx[pl.ds(off, 8), :]
            vals = gather(tab, tuple(range(0, 192, ROWS)), here & 127, here >> 7)
            w = [nrm[c, pl.ds(off, 8), :] for c in range(3)]
            dots[pl.ds(off, 8), 0:128] = vals[0] * w[0] + vals[1] * w[1] + vals[2] * w[2]
            dots[pl.ds(off, 8), 128:256] = vals[3] * w[0] + vals[4] * w[1] + vals[5] * w[2]
        return carry

    lax.fori_loop(0, 8, step, 0)


def part_sums(part, vals, acc):
    it = iota_rows(LANES)
    it8 = (lax.broadcasted_iota(jnp.int32, (16, LANES), 0) & 7).astype(F32).astype(BF)
    one, zero = jnp.ones((LANES, LANES), BF), jnp.zeros((LANES, LANES), BF)
    for r in range(0, ROWS, 8):
        here = part[r : r + 8, :]
        lof, hif = (here & 127).astype(F32), (here >> 7).astype(F32)
        val = vals(r)
        first = [x.astype(BF).astype(F32) for x in val]
        split = (first, [x - y for x, y in zip(val, first)])
        left, right = [], []
        for a in range(8):
            right.append(jnp.where(wide(lof, a, LANES) == it, one, zero))
            mask = wide(hif, a, 16) == it8
            rows = []
            for s in range(2):
                for k in range(0, len(val), 2):
                    two = [jnp.broadcast_to(split[s][k + d][a : a + 1, :], (8, LANES)) for d in range(2)]
                    rows.append(jnp.where(mask, jnp.concatenate(two, 0).astype(BF), zero[:16]))
            left.append(jnp.concatenate(rows, 0))
        acc[...] += lax.dot_general(
            jnp.concatenate(left, 1), jnp.concatenate(right, 1), NT, preferred_element_type=F32
        )


def contact_kernel(dots, got, idx, nrm, x, v, net, mass, part, nodal, sums, acc, tot, acc2):
    acc[...] = jnp.zeros_like(acc)
    acc2[...] = jnp.zeros_like(acc2)
    sign = jnp.where(lax.broadcasted_iota(jnp.int32, (8, LANES), 1) < 64, 1.0, -1.0)

    def step(i, carry):
        for q in range(4):
            off = pl.multiple_of(i * 32 + q * 8, 8)
            at = pl.ds(off, 8)
            gap = sign * (dots[at, 0:128] - pltpu.roll(got[at, 0:128], 64, 1))
            closing = sign * (dots[at, 128:256] - pltpu.roll(got[at, 128:256], 64, 1))
            z = -gap / GAP_WIDTH
            soft = jnp.maximum(z, 0.0) + jnp.log1p(jnp.exp(-jnp.abs(z)))
            push = sign * (PENALTY * GAP_WIDTH * soft - CONTACT_DAMP * closing)
            here = idx[at, :]
            add_placed(acc, here & 127, here >> 7, [push * nrm[c, at, :] for c in range(3)])
        return carry

    lax.fori_loop(0, 4, step, 0)
    contact = acc[0:96, :] + acc[96:192, :]
    tot[...] = net[...] + contact
    for c in range(3):
        speed = v[c * ROWS : (c + 1) * ROWS, :] + TIME_STEP * contact[c * ROWS : (c + 1) * ROWS, :] / mass[...]
        for h in range(ROWS):
            nodal[c : c + 1, h * LANES : (h + 1) * LANES] = speed[h : h + 1, :]

    def vals(r):
        m = mass[r : r + 8, :]
        p = [x[c * ROWS + r : c * ROWS + r + 8, :] for c in range(3)]
        n = [tot[c * ROWS + r : c * ROWS + r + 8, :] for c in range(3)]
        return [
            m,
            *[m * y for y in p],
            *n,
            p[1] * n[2] - p[2] * n[1],
            p[2] * n[0] - p[0] * n[2],
            p[0] * n[1] - p[1] * n[0],
        ]

    part_sums(part, vals, acc2)
    all_sums = acc2[0:80, :] + acc2[80:160, :]
    sums[...] = jnp.concatenate([all_sums, jnp.zeros((48, LANES), F32)], 0).T


def total_kernel(got, out):
    out[...] = jnp.broadcast_to(jnp.sum(got[...], axis=0, keepdims=True), (LANES, LANES))


def motion_kernel(got, pmass, pcenter, pinertia, out, pm, pc, pi):
    spans = [(h, min(LANES, PARTS_SIZE - h * LANES)) for h in range(4)]
    for ref in (pm, pc, pi):
        ref[...] = jnp.ones_like(ref)
    for h, n in spans:
        lanes = slice(h * LANES, h * LANES + n)
        pm[h : h + 1, 0:n] = pmass[0:1, lanes]
        for c in range(3):
            pc[8 * c + h : 8 * c + h + 1, 0:n] = pcenter[c : c + 1, lanes]
            pi[8 * c + h : 8 * c + h + 1, 0:n] = pinertia[c : c + 1, lanes]
    by = got[...].T
    val = [by[8 * k : 8 * k + 8, :] for k in range(10)]
    mass = pm[...] + val[0]
    centre = [(pm[...] * pc[8 * c : 8 * c + 8, :] + val[1 + c]) / mass for c in range(3)]
    force, turn = val[4:7], val[7:10]
    rows = [y / mass for y in force]
    for c in range(3):
        a, b = (c + 1) % 3, (c + 2) % 3
        moment = turn[c] - (centre[a] * force[b] - centre[b] * force[a])
        rows.append(moment / pi[8 * c : 8 * c + 8, :])
    for r, row in enumerate(rows):
        for h, n in spans:
            out[r : r + 1, h * LANES : h * LANES + n] = row[h : h + 1, 0:n]


def partner(block, apart):
    count = lax.axis_size("dom")
    return lax.ppermute(block, "dom", [(i, i ^ (1 << apart)) for i in range(count)])


def swap(block):
    return lax.all_to_all(block, "dom", 0, 0, tiled=True)


def per_device(
    rest_pos,
    displacement,
    velocity,
    ext_force,
    node_mass,
    body_accel,
    connectivity,
    elem_material,
    stiffness,
    shared_nodes,
    contact_slave,
    contact_owner,
    contact_master,
    contact_normal,
    part_of_node,
    part_mass,
    part_center,
    part_inertia,
):
    mass = node_mass.reshape(ROWS, LANES)
    shared = shared_nodes.reshape(NBR, LANES)
    state = ((96, LANES), F32)
    own = [((3, LANES), F32)] * NBR
    square = ((LANES, LANES), F32)
    double = ((LANES, 2 * LANES), F32)

    send, sidx = call(
        slot_kernel,
        [double, square],
        [VMEM] * 4,
        "contact_slots",
        [pltpu.VMEM((LANES, 384), F32)],
    )(
        contact_slave.reshape(16, LANES),
        contact_owner.reshape(16, LANES),
        contact_master.reshape(16, LANES),
        contact_normal,
    )
    got = swap(send)

    work = [
        pltpu.VMEM((96, LANES), F32),
        pltpu.VMEM((24 * TOGETHER, LANES), F32),
        pltpu.VMEM((192, LANES), F32),
    ]
    u, v, f, internal, inv, cols, *mine = call(
        first_kernel,
        [state, state, state, state, ((64, LANES), jnp.int32), ((192, 24, LANES), F32), *own],
        [VMEM] * 4 + [SMEM] + [VMEM] * 2,
        "first_cycle",
        [*work, pltpu.VMEM((128, LANES), F32)],
    )(displacement, velocity, ext_force, connectivity, elem_material, stiffness.reshape(192, 24), shared)
    recv = [partner(mine[b], b) for b in range(NBR)]
    for _ in range(CYCLES - 1):
        u, v, internal, *mine = call(
            next_kernel,
            [state, state, state, *own],
            [VMEM] * 6 + [SMEM, VMEM, SMEM] + [VMEM] * 7,
            "next_cycle",
            work,
        )(u, v, internal, inv, f, mass, body_accel, connectivity, elem_material, cols, shared, *recv)
        recv = [partner(mine[b], b) for b in range(NBR)]

    x, v, net, dots, idx, nrm = call(
        dots_kernel,
        [state, state, state, double, ((LANES, LANES), jnp.int32), ((3, LANES, LANES), F32)],
        [VMEM] * 6 + [SMEM] + [VMEM] * 9,
        "contact_dots",
        [pltpu.VMEM((192, LANES), F32)],
    )(u, v, internal, inv, f, mass, body_accel, rest_pos, send, sidx, got, *recv)
    other = swap(dots)
    nodal_velocity, sums = call(
        contact_kernel,
        [((3, 4096), F32), square],
        [VMEM] * 9,
        "contact_forces",
        [pltpu.VMEM((192, LANES), F32), pltpu.VMEM((96, LANES), F32), pltpu.VMEM((160, LANES), F32)],
    )(dots, other, idx, nrm, x, v, net, mass, part_of_node.reshape(ROWS, LANES))
    (total,) = call(total_kernel, [square], [VMEM], "part_totals")(swap(sums))
    (motion,) = call(
        motion_kernel,
        [((6, PARTS_SIZE), F32)],
        [VMEM] * 4,
        "part_motion",
        [pltpu.VMEM((8, LANES), F32), pltpu.VMEM((24, LANES), F32), pltpu.VMEM((24, LANES), F32)],
    )(swap(total), part_mass.reshape(1, PARTS_SIZE), part_center, part_inertia)
    return nodal_velocity, motion


def solution(mesh):
    placed = (
        P(None, "dom"),
        P(None, "dom"),
        P(None, "dom"),
        P(None, "dom"),
        P("dom"),
        P(),
        P(None, "dom"),
        P("dom"),
        P(),
        P("dom", None, None),
        P("dom"),
        P("dom", None),
        P("dom"),
        P(None, "dom"),
        P("dom"),
        P(),
        P(),
        P(),
    )
    return jax.shard_map(
        per_device, mesh=mesh, in_specs=placed, out_specs=(P(None, "dom"), P()), check_vma=False
    )
```

```python
import functools

import jax
import jax.numpy as jnp
from jax import lax
from jax.experimental import pallas as pl
from jax.experimental.pallas import tpu as pltpu
from jax.sharding import PartitionSpec as P

CYCLES = 3
PARTS_SIZE = 400

TIME_STEP = 0.1
DAMP_RATIO = 0.05
PENALTY = 2.0
GAP_WIDTH = 0.5
CONTACT_DAMP = 0.2

BF = jnp.bfloat16
F32 = jnp.float32
NT = (((1,), (1,)), ((), ()))
LANES = 128
ROWS = 32
NBR = 5
TOGETHER = 4

VMEM = pl.BlockSpec(memory_space=pltpu.VMEM)
SMEM = pl.BlockSpec(memory_space=pltpu.SMEM)
HBM = pl.BlockSpec(memory_space=pltpu.HBM)


def call(body, outs, in_specs, name, scratch=(), flops=0):
    return pl.pallas_call(
        body,
        out_shape=[jax.ShapeDtypeStruct(s, d) for s, d in outs],
        in_specs=in_specs,
        out_specs=[VMEM] * len(outs),
        scratch_shapes=list(scratch),
        compiler_params=pltpu.CompilerParams(vmem_limit_bytes=40 << 20),
        cost_estimate=pl.CostEstimate(flops=flops, bytes_accessed=1 << 20, transcendentals=0),
        name=name,
    )


def lanes_of(row, idx):
    return jnp.take_along_axis(row, idx, axis=1, mode="promise_in_bounds")


def gather(tab, bases, lo, hi):
    acc = [None] * len(bases)
    for h in range(ROWS):
        here = hi == h
        for c, base in enumerate(bases):
            row = jnp.broadcast_to(tab[base + h : base + h + 1, :], (8, LANES))
            val = lanes_of(row, lo)
            acc[c] = val if h == 0 else jnp.where(here, val, acc[c])
    return acc


def halves(x):
    first = x.astype(BF)
    return first, (x - first.astype(F32)).astype(BF)


def wide(x, a, n):
    row = jnp.broadcast_to(x[a : a + 1, :].astype(F32), (16, LANES)).astype(BF)
    return jnp.concatenate([row] * (n // 16), 0)


def iota_rows(n):
    return lax.broadcasted_iota(jnp.int32, (n, LANES), 0).astype(F32).astype(BF)


def place(lo, hi, vals):
    lof, hif = lo.astype(F32), hi.astype(F32)
    it = iota_rows(LANES)
    split = [halves(v) for v in vals]
    one, zero = jnp.ones((LANES, LANES), BF), jnp.zeros((LANES, LANES), BF)
    left, right = [], []
    for a in range(8):
        right.append(jnp.where(wide(lof, a, LANES) == it, one, zero))
        mask = wide(hif, a, ROWS) == it[:ROWS]
        left.append(
            jnp.concatenate(
                [
                    jnp.where(mask, wide(split[c][s], a, ROWS), zero[:ROWS])
                    for s in range(2)
                    for c in range(len(vals))
                ],
                0,
            )
        )
    return jnp.concatenate(left, 1), jnp.concatenate(right, 1)


def add_placed(acc, lo, hi, vals):
    left, right = place(lo, hi, vals)
    acc[...] += lax.dot_general(left, right, NT, preferred_element_type=F32)


def to_rows(src, dst):
    for c in range(3):
        for h in range(ROWS):
            dst[c * ROWS + h : c * ROWS + h + 1, :] = src[c : c + 1, h * LANES : (h + 1) * LANES]


def elements(idx, mat, tab, cols, g, acc):
    acc[...] = jnp.zeros_like(acc)
    steps = ROWS // TOGETHER

    def corners(i, q):
        here = idx[:, pl.ds(pl.multiple_of((i * TOGETHER + q) * LANES, LANES), LANES)]
        return here & 127, here >> 7

    def fetch(i):
        vals = []
        for q in range(TOGETHER):
            vals += gather(tab, (0, ROWS, 2 * ROWS), *corners(i, q))
        return tuple(vals)

    def step(i, vals):
        upcoming = fetch((i + 1) & (steps - 1))
        left, right = [], []
        for q in range(TOGETHER):
            for c in range(3):
                g[q * 24 + 8 * c : q * 24 + 8 * c + 8, :] = vals[q * 3 + c]
            first = mat[i * TOGETHER + q] * 24
            force = [jnp.zeros((8, LANES), F32)] * 3
            for j in range(24):
                col = cols.at[first + j]
                row = jnp.broadcast_to(g[q * 24 + j : q * 24 + j + 1, :], (8, LANES))
                force = [force[c] + col[8 * c : 8 * c + 8, :] * row for c in range(3)]
            one, two = place(*corners(i, q), force)
            left.append(one)
            right.append(two)
        acc[...] += lax.dot_general(
            jnp.concatenate(left, 1), jnp.concatenate(right, 1), NT, preferred_element_type=F32
        )
        return upcoming

    lax.fori_loop(0, steps, step, fetch(0))


def finish_internal(acc, internal, shared):
    internal[...] = acc[0:96, :] + acc[96:192, :]
    return gather(internal, (0, ROWS, 2 * ROWS), shared[...] & 127, shared[...] >> 7)


def slots(slave, owner, master, normal, acc):
    acc[...] = jnp.zeros_like(acc)
    down = lax.broadcasted_iota(jnp.int32, (LANES, LANES), 0)
    across = lax.broadcasted_iota(jnp.int32, (LANES, LANES), 1)
    before = jnp.where(down < across, 1.0, 0.0).astype(BF)
    carry = jnp.zeros((LANES, 1), F32)
    for t in range(16):
        hit = jnp.where(jnp.broadcast_to(owner[t : t + 1, :], (LANES, LANES)) == down, 1.0, 0.0)
        hitb = hit.astype(BF)
        count = jnp.dot(hitb, before, preferred_element_type=F32) + carry
        rank = jnp.sum(hit * count, axis=0, keepdims=True)
        carry = carry + jnp.sum(hit, axis=1, keepdims=True)
        mine = jnp.broadcast_to(rank, (64, LANES)) == down[:64].astype(F32)
        vals = [normal[c : c + 1, t * LANES : (t + 1) * LANES] for c in range(3)]
        vals += [master[t : t + 1, :].astype(F32), slave[t : t + 1, :].astype(F32)]
        left = [jnp.broadcast_to(x, (64, LANES)) for x in vals]
        for s in range(3):
            piece = [jnp.where(mine, x, 0.0).astype(BF) for x in left]
            left = [x - x.astype(BF).astype(F32) for x in left]
            acc[:, 0:320] += lax.dot_general(
                hitb, jnp.concatenate(piece, 0), NT, preferred_element_type=F32
            )


def spans():
    return [(h, min(LANES, PARTS_SIZE - h * LANES)) for h in range(4)]


def row_of_tile(row):
    here = lax.broadcasted_iota(jnp.int32, (8, LANES), 0) == (row & 7)
    return pl.ds(pl.multiple_of((row >> 3) << 3, 8), 8), here


def first_kernel(*refs):
    srcs = refs[:18]
    (u, v, fm, mass, pos, idx, inv, cols, part, shared, internal, send, sidx, rigid) = refs[18:32]
    work = refs[32:]
    (disp0, vel0, force0, pos0, shared0, slave, owner, master, normal, stiff) = work[:10]
    pmass, pcenter, pinertia, mat, accel, conn = work[10:16]
    tab, g, acc, small, table, sems = work[16:]
    dsts = (stiff, disp0, vel0, conn, mat, shared0, force0, mass, accel, slave, owner, master, normal)
    dsts = dsts + (pos0, part, pmass, pcenter, pinertia)
    copies = [pltpu.make_async_copy(a, b, sems.at[i]) for i, (a, b) in enumerate(zip(srcs, dsts))]
    for copy in copies:
        copy.start()
    small[...] = jnp.zeros_like(small)
    copies[0].wait()
    for m in range(8):
        for j in range(24):
            cols[m * 24 + j] = jnp.broadcast_to(stiff[m, :, j : j + 1], (24, LANES))
    for copy in copies[1:]:
        copy.wait()
    to_rows(disp0, u)
    to_rows(vel0, v)
    to_rows(force0, fm)
    to_rows(pos0, pos)
    tab[...] = u[...] + DAMP_RATIO * v[...]
    for c in range(3):
        at = slice(c * ROWS, (c + 1) * ROWS)
        fm[at, :] = fm[at, :] / mass[...] - accel[c]
    lane = lax.broadcasted_iota(jnp.int32, (8, LANES), 1)
    for b in range(ROWS):
        at = slice(b * LANES, (b + 1) * LANES)
        idx[:, at] = (conn[:, at] + lane + b * LANES) & 4095
    shared[...] = jnp.zeros_like(shared)
    for b in range(NBR):
        shared[b : b + 1, :] = shared0[b]
    row = lax.broadcasted_iota(jnp.int32, (8, LANES), 0).astype(F32)
    held = row < NBR
    kept = [jnp.where(held, lane.astype(F32), 0.0), jnp.where(held, row + 1.0, 0.0)]
    add_placed(small, shared[...] & 127, shared[...] >> 7, kept)
    inv[...] = (small[0:64, :] + small[64:128, :]).astype(jnp.int32)
    rigid[...] = jnp.ones_like(rigid)
    for h, n in spans():
        at = slice(h * LANES, h * LANES + n)
        rigid[h : h + 1, 0:n] = pmass[0:1, at]
        for c in range(3):
            rigid[8 + 8 * c + h : 9 + 8 * c + h, 0:n] = pcenter[c : c + 1, at]
            rigid[32 + 8 * c + h : 33 + 8 * c + h, 0:n] = pinertia[c : c + 1, at]
    slots(slave, owner, master, normal, table)
    send[:, 0:256] = table[:, 0:256]
    sidx[...] = table[:, 256:384]
    send[:, 256:640] = jnp.zeros((LANES, 384), F32)
    elements(idx, mat, tab, cols, g, acc)
    own = finish_internal(acc, internal, shared)
    me = lax.axis_index("dom")
    for b in range(NBR):
        tile, here = row_of_tile(me ^ (1 << b))
        for c in range(3):
            row = jnp.broadcast_to(own[c][b : b + 1, :], (8, LANES))
            send[tile, 256 + c * LANES : 256 + (c + 1) * LANES] += jnp.where(here, row, 0.0)


def update(u, v, internal, inv, fm, mass, recv, c, r):
    at = slice(c * ROWS + r, c * ROWS + r + 8)
    slot, which = inv[r : r + 8, :], inv[ROWS + r : ROWS + r + 8, :]
    total = internal[at, :]
    for b in range(NBR):
        row = jnp.broadcast_to(recv[b][c], (8, LANES))
        total = total + jnp.where(which == b + 1, lanes_of(row, slot), 0.0)
    speed = v[at, :] + TIME_STEP * (fm[at, :] - total / mass[r : r + 8, :])
    return at, u[at, :] + TIME_STEP * speed, speed, total


def rows_of(refs):
    return [[ref[c : c + 1, :] for c in range(3)] for ref in refs]


def next_kernel(from_table, u, v, internal, inv, fm, mass, idx, mat, cols, shared, *rest):
    if from_table:
        got, rest = rest[0], rest[1:]
        me = lax.axis_index("dom")
        recv = []
        for b in range(NBR):
            tile, here = row_of_tile(me ^ (1 << b))
            picked = [
                jnp.where(here, got[tile, 256 + c * LANES : 256 + (c + 1) * LANES], 0.0) for c in range(3)
            ]
            recv.append([jnp.sum(x, axis=0, keepdims=True) for x in picked])
    else:
        recv, rest = rows_of(rest[:NBR]), rest[NBR:]
    u2, v2, internal2 = rest[:3]
    own = rest[3:8]
    tab, g, acc = rest[8:]
    for c in range(3):
        for r in range(0, ROWS, 8):
            at, disp, speed, _ = update(u, v, internal, inv, fm, mass, recv, c, r)
            u2[at, :] = disp
            v2[at, :] = speed
            tab[at, :] = disp + DAMP_RATIO * speed
    elements(idx, mat, tab, cols, g, acc)
    vals = finish_internal(acc, internal2, shared)
    for b in range(NBR):
        for c in range(3):
            own[b][c : c + 1, :] = vals[c][b : b + 1, :]


def dots_kernel(u, v, internal, inv, fm, mass, pos, part, send, sidx, got, *rest):
    recv = rows_of(rest[:5])
    x2, v2, net, dots, idx, nrm, tab, acc = rest[5:]
    for c in range(3):
        for r in range(0, ROWS, 8):
            at, disp, speed, total = update(u, v, internal, inv, fm, mass, recv, c, r)
            place_now = pos[at, :] + disp
            x2[at, :] = place_now
            v2[at, :] = speed
            net[at, :] = mass[r : r + 8, :] * fm[at, :] - total
            tab[at, :] = place_now
            tab[c * ROWS + 96 + r : c * ROWS + 96 + r + 8, :] = speed
    left = lax.broadcasted_iota(jnp.int32, (LANES, LANES), 1) < 64
    own0, own1 = send[:, 0:128], send[:, 128:256]
    got0, got1 = got[:, 0:128], got[:, 128:256]
    nrm[0] = jnp.where(left, own0, pltpu.roll(got0, 64, 1))
    nrm[1] = jnp.where(left, pltpu.roll(own0, 64, 1), got0)
    nrm[2] = jnp.where(left, own1, pltpu.roll(got1, 64, 1))
    idx[...] = jnp.where(left, sidx[...], got1).astype(jnp.int32)

    def vals(r):
        m = mass[r : r + 8, :]
        return [m, *[m * tab[c * ROWS + r : c * ROWS + r + 8, :] for c in range(3)]]

    acc[...] = jnp.zeros_like(acc)
    part_sums(part, vals, acc, True)
    moments = jnp.concatenate([acc[0:32, :] + acc[32:64, :], jnp.zeros((96, LANES), F32)], 0)
    dots[:, 256:384] = moments.T

    def step(i, carry):
        for q in range(2):
            off = pl.multiple_of(i * 16 + q * 8, 8)
            here = idx[pl.ds(off, 8), :]
            vals = gather(tab, tuple(range(0, 192, ROWS)), here & 127, here >> 7)
            w = [nrm[c, pl.ds(off, 8), :] for c in range(3)]
            dots[pl.ds(off, 8), 0:128] = vals[0] * w[0] + vals[1] * w[1] + vals[2] * w[2]
            dots[pl.ds(off, 8), 128:256] = vals[3] * w[0] + vals[4] * w[1] + vals[5] * w[2]
        return carry

    lax.fori_loop(0, 8, step, 0)


def part_sums(part, vals, acc, by_device):
    it = iota_rows(LANES)
    it8 = (lax.broadcasted_iota(jnp.int32, (16, LANES), 0) & 7).astype(F32).astype(BF)
    one, zero = jnp.ones((LANES, LANES), BF), jnp.zeros((LANES, LANES), BF)
    for r in range(0, ROWS, 8):
        here = part[r : r + 8, :]
        lo = here & 127
        if by_device:
            lo = ((lo & 63) << 1) | (lo >> 6)
        lof, hif = lo.astype(F32), (here >> 7).astype(F32)
        val = vals(r)
        first = [x.astype(BF).astype(F32) for x in val]
        split = (first, [x - y for x, y in zip(val, first)])
        left, right = [], []
        for a in range(8):
            right.append(jnp.where(wide(lof, a, LANES) == it, one, zero))
            mask = wide(hif, a, 16) == it8
            rows = []
            for s in range(2):
                for k in range(0, len(val), 2):
                    two = [jnp.broadcast_to(split[s][k + d][a : a + 1, :], (8, LANES)) for d in range(2)]
                    rows.append(jnp.where(mask, jnp.concatenate(two, 0).astype(BF), zero[:16]))
            left.append(jnp.concatenate(rows, 0))
        acc[...] += lax.dot_general(
            jnp.concatenate(left, 1), jnp.concatenate(right, 1), NT, preferred_element_type=F32
        )


def contact_kernel(dots, got, idx, nrm, x, v, net, mass, part, nodal, keep, give, acc, tot, acc2):
    acc[...] = jnp.zeros_like(acc)
    acc2[...] = jnp.zeros_like(acc2)
    sign = jnp.where(lax.broadcasted_iota(jnp.int32, (8, LANES), 1) < 64, 1.0, -1.0)

    def step(i, carry):
        left, right = [], []
        for q in range(4):
            at = pl.ds(pl.multiple_of(i * 32 + q * 8, 8), 8)
            gap = sign * (dots[at, 0:128] - pltpu.roll(got[at, 0:128], 64, 1))
            closing = sign * (dots[at, 128:256] - pltpu.roll(got[at, 128:256], 64, 1))
            z = -gap / GAP_WIDTH
            soft = jnp.maximum(z, 0.0) + jnp.log1p(jnp.exp(-jnp.abs(z)))
            push = sign * (PENALTY * GAP_WIDTH * soft - CONTACT_DAMP * closing)
            here = idx[at, :]
            one, two = place(here & 127, here >> 7, [push * nrm[c, at, :] for c in range(3)])
            left.append(one)
            right.append(two)
        acc[...] += lax.dot_general(
            jnp.concatenate(left, 1), jnp.concatenate(right, 1), NT, preferred_element_type=F32
        )
        return carry

    lax.fori_loop(0, 4, step, 0)
    contact = acc[0:96, :] + acc[96:192, :]
    tot[...] = net[...] + contact
    for c in range(3):
        speed = v[c * ROWS : (c + 1) * ROWS, :] + TIME_STEP * contact[c * ROWS : (c + 1) * ROWS, :] / mass[...]
        for h in range(ROWS):
            nodal[c : c + 1, h * LANES : (h + 1) * LANES] = speed[h : h + 1, :]

    def vals(r):
        p = [x[c * ROWS + r : c * ROWS + r + 8, :] for c in range(3)]
        n = [tot[c * ROWS + r : c * ROWS + r + 8, :] for c in range(3)]
        return [
            *n,
            p[1] * n[2] - p[2] * n[1],
            p[2] * n[0] - p[0] * n[2],
            p[0] * n[1] - p[1] * n[0],
        ]

    part_sums(part, vals, acc2, False)
    acc2[0:48, :] = acc2[0:48, :] + acc2[48:96, :]
    even = lax.axis_index("dom") & 1 == 0
    for k in range(6):
        low, high = acc2[8 * k : 8 * k + 2, :], acc2[8 * k + 2 : 8 * k + 4, :]
        keep[2 * k : 2 * k + 2, :] = jnp.where(even, low, high)
        give[2 * k : 2 * k + 2, :] = jnp.where(even, high, low)
    keep[12:16, :] = jnp.zeros((4, LANES), F32)
    give[12:16, :] = jnp.zeros((4, LANES), F32)
    keep[12:13, :] = jnp.sum(got[:, 256:384], axis=0, keepdims=True)


def spread_kernel(keep, given, out):
    tile = keep[...] + given[...]
    for k in range(64):
        out[16 * k : 16 * k + 16, :] = tile


def total_kernel(got, out):
    total = got[0:16, :]
    for k in range(1, 64):
        total = total + got[16 * k : 16 * k + 16, :]
    out[0:16, :] = total
    for k in range(64):
        out[16 + k : 17 + k, :] = got[16 * k + 12 : 16 * k + 13, :]


def motion_kernel(mine, other, rigid, out):
    even = lax.axis_index("dom") & 1 == 0
    low = jnp.where(even, mine[...], other[...])
    high = jnp.where(even, other[...], mine[...])
    by = jnp.concatenate([low[16:80, :], high[16:80, :]], 0).T
    moments = [by[8 * k : 8 * k + 4, :] for k in range(4)]
    sums = [jnp.concatenate([low[2 * k : 2 * k + 2, :], high[2 * k : 2 * k + 2, :]], 0) for k in range(6)]
    own = rigid[0:4, :]
    mass = own + moments[0]
    centre = [(own * rigid[8 + 8 * c : 12 + 8 * c, :] + moments[1 + c]) / mass for c in range(3)]
    force, turn = sums[0:3], sums[3:6]
    rows = [y / mass for y in force]
    for c in range(3):
        a, b = (c + 1) % 3, (c + 2) % 3
        moment = turn[c] - (centre[a] * force[b] - centre[b] * force[a])
        rows.append(moment / rigid[32 + 8 * c : 36 + 8 * c, :])
    for r, row in enumerate(rows):
        for h, n in spans():
            out[r : r + 1, h * LANES : h * LANES + n] = row[h : h + 1, 0:n]


def partner(block, apart):
    count = lax.axis_size("dom")
    return lax.ppermute(block, "dom", [(i, i ^ (1 << apart)) for i in range(count)])


def swap(block, groups=None):
    return lax.all_to_all(block, "dom", 0, 0, tiled=True, axis_index_groups=groups)


def per_device(
    rest_pos,
    displacement,
    velocity,
    ext_force,
    node_mass,
    body_accel,
    connectivity,
    elem_material,
    stiffness,
    shared_nodes,
    contact_slave,
    contact_owner,
    contact_master,
    contact_normal,
    part_of_node,
    part_mass,
    part_center,
    part_inertia,
):
    state = ((96, LANES), F32)
    square = ((LANES, LANES), F32)
    table = ((LANES, 5 * LANES), F32)
    own = [((3, LANES), F32)] * NBR
    work = [
        pltpu.VMEM((96, LANES), F32),
        pltpu.VMEM((24 * TOGETHER, LANES), F32),
        pltpu.VMEM((192, LANES), F32),
    ]
    inputs = (
        stiffness,
        displacement,
        velocity,
        connectivity,
        elem_material,
        shared_nodes.transpose(1, 0, 2),
        ext_force,
        node_mass.reshape(ROWS, LANES),
        body_accel,
        contact_slave.reshape(16, LANES),
        contact_owner.reshape(16, LANES),
        contact_master.reshape(16, LANES),
        contact_normal,
        rest_pos,
        part_of_node.reshape(ROWS, LANES),
        part_mass.reshape(1, PARTS_SIZE),
        part_center,
        part_inertia,
    )
    rows, ints = ((ROWS, LANES), F32), jnp.int32
    u, v, fm, mass, pos, idx, inv, cols, part, shared, internal, send, sidx, rigid = call(
        first_kernel,
        [
            state,
            state,
            state,
            rows,
            state,
            ((8, 4096), ints),
            ((64, LANES), ints),
            ((192, 24, LANES), F32),
            ((ROWS, LANES), ints),
            ((8, LANES), ints),
            state,
            table,
            square,
            ((56, LANES), F32),
        ],
        [HBM] * 18,
        "first_cycle",
        [
            *[pltpu.VMEM((3, 4096), F32)] * 4,
            pltpu.VMEM((NBR, 1, LANES), ints),
            *[pltpu.VMEM((16, LANES), ints)] * 3,
            pltpu.VMEM((3, 2048), F32),
            pltpu.VMEM((8, 24, 24), F32),
            pltpu.VMEM((1, PARTS_SIZE), F32),
            pltpu.VMEM((3, PARTS_SIZE), F32),
            pltpu.VMEM((3, PARTS_SIZE), F32),
            pltpu.SMEM((ROWS,), ints),
            pltpu.SMEM((3,), F32),
            pltpu.VMEM((8, 4096), ints),
            *work,
            pltpu.VMEM((LANES, LANES), F32),
            pltpu.VMEM((LANES, 3 * LANES), F32),
            pltpu.SemaphoreType.DMA((18,)),
        ],
    )(*inputs)
    got = swap(send)
    recv = [got]
    for n in range(CYCLES - 1):
        u, v, internal, *mine = call(
            functools.partial(next_kernel, n == 0),
            [state, state, state, *own],
            [VMEM] * 7 + [SMEM] + [VMEM] * (2 + len(recv)),
            "next_cycle",
            work,
        )(u, v, internal, inv, fm, mass, idx, elem_material, cols, shared, *recv)
        recv = [partner(mine[b], b) for b in range(NBR)]

    trio = ((LANES, 3 * LANES), F32)
    x, v, net, dots, ends, nrm = call(
        dots_kernel,
        [state, state, state, trio, ((LANES, LANES), ints), ((3, LANES, LANES), F32)],
        [VMEM] * 16,
        "contact_dots",
        [pltpu.VMEM((192, LANES), F32), pltpu.VMEM((64, LANES), F32)],
    )(u, v, internal, inv, fm, mass, pos, part, send, sidx, got, *recv)
    half = ((16, LANES), F32)
    nodal_velocity, keep, give = call(
        contact_kernel,
        [((3, 4096), F32), half, half],
        [VMEM] * 9,
        "contact_forces",
        [pltpu.VMEM((192, LANES), F32), pltpu.VMEM((96, LANES), F32), pltpu.VMEM((96, LANES), F32)],
    )(dots, swap(dots), ends, nrm, x, v, net, mass, part)
    (spread,) = call(spread_kernel, [((1024, LANES), F32)], [VMEM] * 2, "part_spread")(keep, partner(give, 0))
    chips = lax.axis_size("dom") // 2
    groups = [[2 * i + core for i in range(chips)] for core in range(2)]
    (total,) = call(total_kernel, [((80, LANES), F32)], [VMEM], "part_totals")(swap(spread, groups))
    (motion,) = call(motion_kernel, [((6, PARTS_SIZE), F32)], [VMEM] * 3, "part_motion")(
        total, partner(total, 0), rigid
    )
    return nodal_velocity, motion


def solution(mesh):
    placed = (
        P(None, "dom"),
        P(None, "dom"),
        P(None, "dom"),
        P(None, "dom"),
        P("dom"),
        P(),
        P(None, "dom"),
        P("dom"),
        P(),
        P("dom", None, None),
        P("dom"),
        P("dom", None),
        P("dom"),
        P(None, "dom"),
        P("dom"),
        P(),
        P(),
        P(),
    )
    return jax.shard_map(
        per_device, mesh=mesh, in_specs=placed, out_specs=(P(None, "dom"), P()), check_vma=False
    )
```

```python
import functools

import jax
import jax.numpy as jnp
from jax import lax
from jax.experimental import pallas as pl
from jax.experimental.pallas import tpu as pltpu
from jax.sharding import PartitionSpec as P

CYCLES = 3
PARTS_SIZE = 400

TIME_STEP = 0.1
DAMP_RATIO = 0.05
PENALTY = 2.0
GAP_WIDTH = 0.5
CONTACT_DAMP = 0.2

BF = jnp.bfloat16
F32 = jnp.float32
NT = (((1,), (1,)), ((), ()))
LANES = 128
ROWS = 32
NBR = 5
TOGETHER = 4

VMEM = pl.BlockSpec(memory_space=pltpu.VMEM)
SMEM = pl.BlockSpec(memory_space=pltpu.SMEM)
HBM = pl.BlockSpec(memory_space=pltpu.HBM)


def call(body, outs, in_specs, name, scratch=(), flops=0):
    return pl.pallas_call(
        body,
        out_shape=[jax.ShapeDtypeStruct(s, d) for s, d in outs],
        in_specs=in_specs,
        out_specs=[VMEM] * len(outs),
        scratch_shapes=list(scratch),
        compiler_params=pltpu.CompilerParams(vmem_limit_bytes=40 << 20),
        cost_estimate=pl.CostEstimate(flops=flops, bytes_accessed=1 << 20, transcendentals=0),
        name=name,
    )


def lanes_of(row, idx):
    return jnp.take_along_axis(row, idx, axis=1, mode="promise_in_bounds")


def gather(tab, bases, lo, hi):
    acc = [None] * len(bases)
    for h in range(ROWS):
        here = hi == h
        for c, base in enumerate(bases):
            row = jnp.broadcast_to(tab[base + h : base + h + 1, :], (8, LANES))
            val = lanes_of(row, lo)
            acc[c] = val if h == 0 else jnp.where(here, val, acc[c])
    return acc


def halves(x):
    first = x.astype(BF)
    return first, (x - first.astype(F32)).astype(BF)


def wide(x, a, n):
    row = jnp.broadcast_to(x[a : a + 1, :].astype(F32), (16, LANES)).astype(BF)
    return jnp.concatenate([row] * (n // 16), 0)


def iota_rows(n):
    return lax.broadcasted_iota(jnp.int32, (n, LANES), 0).astype(F32).astype(BF)


def place(lo, hi, vals):
    lof, hif = lo.astype(F32), hi.astype(F32)
    it = iota_rows(LANES)
    split = [halves(v) for v in vals]
    one, zero = jnp.ones((LANES, LANES), BF), jnp.zeros((LANES, LANES), BF)
    left, right = [], []
    for a in range(8):
        right.append(jnp.where(wide(lof, a, LANES) == it, one, zero))
        mask = wide(hif, a, ROWS) == it[:ROWS]
        left.append(
            jnp.concatenate(
                [
                    jnp.where(mask, wide(split[c][s], a, ROWS), zero[:ROWS])
                    for s in range(2)
                    for c in range(len(vals))
                ],
                0,
            )
        )
    return jnp.concatenate(left, 1), jnp.concatenate(right, 1)


def add_placed(acc, lo, hi, vals):
    left, right = place(lo, hi, vals)
    acc[...] += lax.dot_general(left, right, NT, preferred_element_type=F32)


def to_rows(src, dst):
    for c in range(3):
        for h in range(ROWS):
            dst[c * ROWS + h : c * ROWS + h + 1, :] = src[c : c + 1, h * LANES : (h + 1) * LANES]


def elements(idx, mat, tab, cols, g, acc):
    acc[...] = jnp.zeros_like(acc)
    steps = ROWS // TOGETHER

    def corners(i, q):
        here = idx[:, pl.ds(pl.multiple_of((i * TOGETHER + q) * LANES, LANES), LANES)]
        return here & 127, here >> 7

    def fetch(i):
        vals = []
        for q in range(TOGETHER):
            vals += gather(tab, (0, ROWS, 2 * ROWS), *corners(i, q))
        return tuple(vals)

    def step(i, vals):
        upcoming = fetch((i + 1) & (steps - 1))
        left, right = [], []
        for q in range(TOGETHER):
            for c in range(3):
                g[q * 24 + 8 * c : q * 24 + 8 * c + 8, :] = vals[q * 3 + c]
            first = mat[i * TOGETHER + q] * 24
            force = [jnp.zeros((8, LANES), F32)] * 3
            for j in range(24):
                col = cols.at[first + j]
                row = jnp.broadcast_to(g[q * 24 + j : q * 24 + j + 1, :], (8, LANES))
                force = [force[c] + col[8 * c : 8 * c + 8, :] * row for c in range(3)]
            one, two = place(*corners(i, q), force)
            left.append(one)
            right.append(two)
        acc[...] += lax.dot_general(
            jnp.concatenate(left, 1), jnp.concatenate(right, 1), NT, preferred_element_type=F32
        )
        return upcoming

    lax.fori_loop(0, steps, step, fetch(0))


def finish_internal(acc, internal, shared):
    internal[...] = acc[0:96, :] + acc[96:192, :]
    return gather(internal, (0, ROWS, 2 * ROWS), shared[...] & 127, shared[...] >> 7)


def slots(slave, owner, master, normal, acc, between):
    acc[...] = jnp.zeros_like(acc)
    down = lax.broadcasted_iota(jnp.int32, (LANES, LANES), 0)
    across = lax.broadcasted_iota(jnp.int32, (LANES, LANES), 1)
    before = jnp.where(down < across, 1.0, 0.0).astype(BF)
    carry = jnp.zeros((LANES, 1), F32)
    for pair in range(8):
        hits, pieces = [], []
        for t in (2 * pair, 2 * pair + 1):
            hit = jnp.where(jnp.broadcast_to(owner[t : t + 1, :], (LANES, LANES)) == down, 1.0, 0.0)
            hitb = hit.astype(BF)
            count = jnp.dot(hitb, before, preferred_element_type=F32) + carry
            rank = jnp.sum(hit * count, axis=0, keepdims=True)
            carry = carry + jnp.sum(hit, axis=1, keepdims=True)
            mine = jnp.broadcast_to(rank, (64, LANES)) == down[:64].astype(F32)
            vals = [normal[c : c + 1, t * LANES : (t + 1) * LANES] for c in range(3)]
            vals += [master[t : t + 1, :].astype(F32), slave[t : t + 1, :].astype(F32)]
            left = [jnp.broadcast_to(x, (64, LANES)) for x in vals]
            for s in range(3):
                hits.append(hitb)
                pieces.append(jnp.concatenate([jnp.where(mine, x, 0.0).astype(BF) for x in left], 0))
                left = [x - x.astype(BF).astype(F32) for x in left]
        between(pair)
        acc[:, 0:320] += lax.dot_general(
            jnp.concatenate(hits, 1), jnp.concatenate(pieces, 1), NT, preferred_element_type=F32
        )


def spans():
    return [(h, min(LANES, PARTS_SIZE - h * LANES)) for h in range(4)]


def row_of_tile(row):
    here = lax.broadcasted_iota(jnp.int32, (8, LANES), 0) == (row & 7)
    return pl.ds(pl.multiple_of((row >> 3) << 3, 8), 8), here


def first_kernel(*refs):
    srcs = refs[:18]
    (u, v, fm, mass, pos, idx, inv, cols, part, shared, internal, send, sidx, rigid) = refs[18:32]
    work = refs[32:]
    (disp0, vel0, force0, pos0, shared0, slave, owner, master, normal, stiff) = work[:10]
    pmass, pcenter, pinertia, mat, accel, conn = work[10:16]
    tab, g, acc, small, table, sems = work[16:]
    dsts = (stiff, disp0, vel0, conn, mat, shared0, force0, mass, accel, slave, owner, master, normal)
    dsts = dsts + (pos0, part, pmass, pcenter, pinertia)
    copies = [pltpu.make_async_copy(a, b, sems.at[i]) for i, (a, b) in enumerate(zip(srcs, dsts))]
    for copy in copies:
        copy.start()
    small[...] = jnp.zeros_like(small)
    for copy in copies:
        copy.wait()

    def columns(m):
        for j in range(24):
            cols[m * 24 + j] = jnp.broadcast_to(stiff[m, :, j : j + 1], (24, LANES))

    to_rows(disp0, u)
    to_rows(vel0, v)
    to_rows(force0, fm)
    to_rows(pos0, pos)
    tab[...] = u[...] + DAMP_RATIO * v[...]
    for c in range(3):
        at = slice(c * ROWS, (c + 1) * ROWS)
        fm[at, :] = fm[at, :] / mass[...] - accel[c]
    lane = lax.broadcasted_iota(jnp.int32, (8, LANES), 1)
    for b in range(ROWS):
        at = slice(b * LANES, (b + 1) * LANES)
        idx[:, at] = (conn[:, at] + lane + b * LANES) & 4095
    shared[...] = jnp.zeros_like(shared)
    for b in range(NBR):
        shared[b : b + 1, :] = shared0[b]
    row = lax.broadcasted_iota(jnp.int32, (8, LANES), 0).astype(F32)
    held = row < NBR
    kept = [jnp.where(held, lane.astype(F32), 0.0), jnp.where(held, row + 1.0, 0.0)]
    add_placed(small, shared[...] & 127, shared[...] >> 7, kept)
    inv[...] = (small[0:64, :] + small[64:128, :]).astype(jnp.int32)
    rigid[...] = jnp.ones_like(rigid)
    for h, n in spans():
        at = slice(h * LANES, h * LANES + n)
        rigid[h : h + 1, 0:n] = pmass[0:1, at]
        for c in range(3):
            rigid[8 + 8 * c + h : 9 + 8 * c + h, 0:n] = pcenter[c : c + 1, at]
            rigid[32 + 8 * c + h : 33 + 8 * c + h, 0:n] = pinertia[c : c + 1, at]
    slots(slave, owner, master, normal, table, columns)
    send[:, 0:256] = table[:, 0:256]
    sidx[...] = table[:, 256:384]
    send[:, 256:640] = jnp.zeros((LANES, 384), F32)
    elements(idx, mat, tab, cols, g, acc)
    own = finish_internal(acc, internal, shared)
    me = lax.axis_index("dom")
    for b in range(NBR):
        tile, here = row_of_tile(me ^ (1 << b))
        for c in range(3):
            row = jnp.broadcast_to(own[c][b : b + 1, :], (8, LANES))
            send[tile, 256 + c * LANES : 256 + (c + 1) * LANES] += jnp.where(here, row, 0.0)


def update(u, v, internal, inv, fm, mass, recv, c, r):
    at = slice(c * ROWS + r, c * ROWS + r + 8)
    slot, which = inv[r : r + 8, :], inv[ROWS + r : ROWS + r + 8, :]
    total = internal[at, :]
    for b in range(NBR):
        row = jnp.broadcast_to(recv[b][c], (8, LANES))
        total = total + jnp.where(which == b + 1, lanes_of(row, slot), 0.0)
    speed = v[at, :] + TIME_STEP * (fm[at, :] - total / mass[r : r + 8, :])
    return at, u[at, :] + TIME_STEP * speed, speed, total


def rows_of(refs):
    return [[ref[c : c + 1, :] for c in range(3)] for ref in refs]


def next_kernel(from_table, u, v, internal, inv, fm, mass, idx, mat, cols, shared, *rest):
    if from_table:
        got, rest = rest[0], rest[1:]
        me = lax.axis_index("dom")
        recv = []
        for b in range(NBR):
            tile, here = row_of_tile(me ^ (1 << b))
            picked = [
                jnp.where(here, got[tile, 256 + c * LANES : 256 + (c + 1) * LANES], 0.0) for c in range(3)
            ]
            recv.append([jnp.sum(x, axis=0, keepdims=True) for x in picked])
    else:
        recv, rest = rows_of(rest[:NBR]), rest[NBR:]
    u2, v2, internal2 = rest[:3]
    own = rest[3:8]
    tab, g, acc = rest[8:]
    for c in range(3):
        for r in range(0, ROWS, 8):
            at, disp, speed, _ = update(u, v, internal, inv, fm, mass, recv, c, r)
            u2[at, :] = disp
            v2[at, :] = speed
            tab[at, :] = disp + DAMP_RATIO * speed
    elements(idx, mat, tab, cols, g, acc)
    vals = finish_internal(acc, internal2, shared)
    for b in range(NBR):
        for c in range(3):
            own[b][c : c + 1, :] = vals[c][b : b + 1, :]


def dots_kernel(u, v, internal, inv, fm, mass, pos, part, send, sidx, got, *rest):
    recv = rows_of(rest[:5])
    x2, v2, net, dots, idx, nrm, tab, acc = rest[5:]
    for c in range(3):
        for r in range(0, ROWS, 8):
            at, disp, speed, total = update(u, v, internal, inv, fm, mass, recv, c, r)
            place_now = pos[at, :] + disp
            x2[at, :] = place_now
            v2[at, :] = speed
            net[at, :] = mass[r : r + 8, :] * fm[at, :] - total
            tab[at, :] = place_now
            tab[c * ROWS + 96 + r : c * ROWS + 96 + r + 8, :] = speed
    left = lax.broadcasted_iota(jnp.int32, (LANES, LANES), 1) < 64
    own0, own1 = send[:, 0:128], send[:, 128:256]
    got0, got1 = got[:, 0:128], got[:, 128:256]
    nrm[0] = jnp.where(left, own0, pltpu.roll(got0, 64, 1))
    nrm[1] = jnp.where(left, pltpu.roll(own0, 64, 1), got0)
    nrm[2] = jnp.where(left, own1, pltpu.roll(got1, 64, 1))
    idx[...] = jnp.where(left, sidx[...], got1).astype(jnp.int32)

    def vals(r):
        m = mass[r : r + 8, :]
        return [m, *[m * tab[c * ROWS + r : c * ROWS + r + 8, :] for c in range(3)]]

    acc[...] = jnp.zeros_like(acc)
    part_sums(part, vals, acc, True)
    moments = jnp.concatenate([acc[0:32, :] + acc[32:64, :], jnp.zeros((96, LANES), F32)], 0)
    dots[:, 256:384] = moments.T

    def step(i, carry):
        for q in range(2):
            off = pl.multiple_of(i * 16 + q * 8, 8)
            here = idx[pl.ds(off, 8), :]
            vals = gather(tab, tuple(range(0, 192, ROWS)), here & 127, here >> 7)
            w = [nrm[c, pl.ds(off, 8), :] for c in range(3)]
            dots[pl.ds(off, 8), 0:128] = vals[0] * w[0] + vals[1] * w[1] + vals[2] * w[2]
            dots[pl.ds(off, 8), 128:256] = vals[3] * w[0] + vals[4] * w[1] + vals[5] * w[2]
        return carry

    lax.fori_loop(0, 8, step, 0)


def part_sums(part, vals, acc, by_device):
    it = iota_rows(LANES)
    it8 = (lax.broadcasted_iota(jnp.int32, (16, LANES), 0) & 7).astype(F32).astype(BF)
    one, zero = jnp.ones((LANES, LANES), BF), jnp.zeros((LANES, LANES), BF)
    for r in range(0, ROWS, 8):
        here = part[r : r + 8, :]
        lo = here & 127
        if by_device:
            lo = ((lo & 63) << 1) | (lo >> 6)
        lof, hif = lo.astype(F32), (here >> 7).astype(F32)
        val = vals(r)
        first = [x.astype(BF).astype(F32) for x in val]
        split = (first, [x - y for x, y in zip(val, first)])
        left, right = [], []
        for a in range(8):
            right.append(jnp.where(wide(lof, a, LANES) == it, one, zero))
            mask = wide(hif, a, 16) == it8
            rows = []
            for s in range(2):
                for k in range(0, len(val), 2):
                    two = [jnp.broadcast_to(split[s][k + d][a : a + 1, :], (8, LANES)) for d in range(2)]
                    rows.append(jnp.where(mask, jnp.concatenate(two, 0).astype(BF), zero[:16]))
            left.append(jnp.concatenate(rows, 0))
        acc[...] += lax.dot_general(
            jnp.concatenate(left, 1), jnp.concatenate(right, 1), NT, preferred_element_type=F32
        )


def contact_kernel(dots, got, idx, nrm, x, v, net, mass, part, nodal, keep, give, acc, tot, acc2):
    acc[...] = jnp.zeros_like(acc)
    acc2[...] = jnp.zeros_like(acc2)
    sign = jnp.where(lax.broadcasted_iota(jnp.int32, (8, LANES), 1) < 64, 1.0, -1.0)

    def step(i, carry):
        left, right = [], []
        for q in range(4):
            at = pl.ds(pl.multiple_of(i * 32 + q * 8, 8), 8)
            gap = sign * (dots[at, 0:128] - pltpu.roll(got[at, 0:128], 64, 1))
            closing = sign * (dots[at, 128:256] - pltpu.roll(got[at, 128:256], 64, 1))
            z = -gap / GAP_WIDTH
            soft = jnp.maximum(z, 0.0) + jnp.log1p(jnp.exp(-jnp.abs(z)))
            push = sign * (PENALTY * GAP_WIDTH * soft - CONTACT_DAMP * closing)
            here = idx[at, :]
            one, two = place(here & 127, here >> 7, [push * nrm[c, at, :] for c in range(3)])
            left.append(one)
            right.append(two)
        acc[...] += lax.dot_general(
            jnp.concatenate(left, 1), jnp.concatenate(right, 1), NT, preferred_element_type=F32
        )
        return carry

    lax.fori_loop(0, 4, step, 0)
    contact = acc[0:96, :] + acc[96:192, :]
    tot[...] = net[...] + contact
    for c in range(3):
        speed = v[c * ROWS : (c + 1) * ROWS, :] + TIME_STEP * contact[c * ROWS : (c + 1) * ROWS, :] / mass[...]
        for h in range(ROWS):
            nodal[c : c + 1, h * LANES : (h + 1) * LANES] = speed[h : h + 1, :]

    def vals(r):
        p = [x[c * ROWS + r : c * ROWS + r + 8, :] for c in range(3)]
        n = [tot[c * ROWS + r : c * ROWS + r + 8, :] for c in range(3)]
        return [
            *n,
            p[1] * n[2] - p[2] * n[1],
            p[2] * n[0] - p[0] * n[2],
            p[0] * n[1] - p[1] * n[0],
        ]

    part_sums(part, vals, acc2, False)
    acc2[0:48, :] = acc2[0:48, :] + acc2[48:96, :]
    even = lax.axis_index("dom") & 1 == 0
    for k in range(6):
        low, high = acc2[8 * k : 8 * k + 2, :], acc2[8 * k + 2 : 8 * k + 4, :]
        keep[2 * k : 2 * k + 2, :] = jnp.where(even, low, high)
        give[2 * k : 2 * k + 2, :] = jnp.where(even, high, low)
    keep[12:16, :] = jnp.zeros((4, LANES), F32)
    give[12:16, :] = jnp.zeros((4, LANES), F32)
    keep[12:13, :] = jnp.sum(got[:, 256:384], axis=0, keepdims=True)


def spread_kernel(keep, given, out):
    tile = keep[...] + given[...]
    for k in range(64):
        out[16 * k : 16 * k + 16, :] = tile


def total_kernel(got, out):
    total = got[0:16, :]
    for k in range(1, 64):
        total = total + got[16 * k : 16 * k + 16, :]
    out[0:16, :] = total
    for k in range(64):
        out[16 + k : 17 + k, :] = got[16 * k + 12 : 16 * k + 13, :]


def motion_kernel(mine, other, rigid, out):
    even = lax.axis_index("dom") & 1 == 0
    low = jnp.where(even, mine[...], other[...])
    high = jnp.where(even, other[...], mine[...])
    by = jnp.concatenate([low[16:80, :], high[16:80, :]], 0).T
    moments = [by[8 * k : 8 * k + 4, :] for k in range(4)]
    sums = [jnp.concatenate([low[2 * k : 2 * k + 2, :], high[2 * k : 2 * k + 2, :]], 0) for k in range(6)]
    own = rigid[0:4, :]
    mass = own + moments[0]
    centre = [(own * rigid[8 + 8 * c : 12 + 8 * c, :] + moments[1 + c]) / mass for c in range(3)]
    force, turn = sums[0:3], sums[3:6]
    rows = [y / mass for y in force]
    for c in range(3):
        a, b = (c + 1) % 3, (c + 2) % 3
        moment = turn[c] - (centre[a] * force[b] - centre[b] * force[a])
        rows.append(moment / rigid[32 + 8 * c : 36 + 8 * c, :])
    for r, row in enumerate(rows):
        for h, n in spans():
            out[r : r + 1, h * LANES : h * LANES + n] = row[h : h + 1, 0:n]


def partner(block, apart):
    count = lax.axis_size("dom")
    return lax.ppermute(block, "dom", [(i, i ^ (1 << apart)) for i in range(count)])


def swap(block, groups=None):
    return lax.all_to_all(block, "dom", 0, 0, tiled=True, axis_index_groups=groups)


def per_device(
    rest_pos,
    displacement,
    velocity,
    ext_force,
    node_mass,
    body_accel,
    connectivity,
    elem_material,
    stiffness,
    shared_nodes,
    contact_slave,
    contact_owner,
    contact_master,
    contact_normal,
    part_of_node,
    part_mass,
    part_center,
    part_inertia,
):
    state = ((96, LANES), F32)
    square = ((LANES, LANES), F32)
    table = ((LANES, 5 * LANES), F32)
    own = [((3, LANES), F32)] * NBR
    work = [
        pltpu.VMEM((96, LANES), F32),
        pltpu.VMEM((24 * TOGETHER, LANES), F32),
        pltpu.VMEM((192, LANES), F32),
    ]
    inputs = (
        stiffness,
        displacement,
        velocity,
        connectivity,
        elem_material,
        shared_nodes.transpose(1, 0, 2),
        ext_force,
        node_mass.reshape(ROWS, LANES),
        body_accel,
        contact_slave.reshape(16, LANES),
        contact_owner.reshape(16, LANES),
        contact_master.reshape(16, LANES),
        contact_normal,
        rest_pos,
        part_of_node.reshape(ROWS, LANES),
        part_mass.reshape(1, PARTS_SIZE),
        part_center,
        part_inertia,
    )
    rows, ints = ((ROWS, LANES), F32), jnp.int32
    u, v, fm, mass, pos, idx, inv, cols, part, shared, internal, send, sidx, rigid = call(
        first_kernel,
        [
            state,
            state,
            state,
            rows,
            state,
            ((8, 4096), ints),
            ((64, LANES), ints),
            ((192, 24, LANES), F32),
            ((ROWS, LANES), ints),
            ((8, LANES), ints),
            state,
            table,
            square,
            ((56, LANES), F32),
        ],
        [HBM] * 18,
        "first_cycle",
        [
            *[pltpu.VMEM((3, 4096), F32)] * 4,
            pltpu.VMEM((NBR, 1, LANES), ints),
            *[pltpu.VMEM((16, LANES), ints)] * 3,
            pltpu.VMEM((3, 2048), F32),
            pltpu.VMEM((8, 24, 24), F32),
            pltpu.VMEM((1, PARTS_SIZE), F32),
            pltpu.VMEM((3, PARTS_SIZE), F32),
            pltpu.VMEM((3, PARTS_SIZE), F32),
            pltpu.SMEM((ROWS,), ints),
            pltpu.SMEM((3,), F32),
            pltpu.VMEM((8, 4096), ints),
            *work,
            pltpu.VMEM((LANES, LANES), F32),
            pltpu.VMEM((LANES, 3 * LANES), F32),
            pltpu.SemaphoreType.DMA((18,)),
        ],
    )(*[pltpu.with_memory_space_constraint(x, pltpu.HBM) for x in inputs])
    got = swap(send)
    recv = [got]
    for n in range(CYCLES - 1):
        u, v, internal, *mine = call(
            functools.partial(next_kernel, n == 0),
            [state, state, state, *own],
            [VMEM] * 7 + [SMEM] + [VMEM] * (2 + len(recv)),
            "next_cycle",
            work,
        )(u, v, internal, inv, fm, mass, idx, elem_material, cols, shared, *recv)
        recv = [partner(mine[b], b) for b in range(NBR)]

    trio = ((LANES, 3 * LANES), F32)
    x, v, net, dots, ends, nrm = call(
        dots_kernel,
        [state, state, state, trio, ((LANES, LANES), ints), ((3, LANES, LANES), F32)],
        [VMEM] * 16,
        "contact_dots",
        [pltpu.VMEM((192, LANES), F32), pltpu.VMEM((64, LANES), F32)],
    )(u, v, internal, inv, fm, mass, pos, part, send, sidx, got, *recv)
    half = ((16, LANES), F32)
    nodal_velocity, keep, give = call(
        contact_kernel,
        [((3, 4096), F32), half, half],
        [VMEM] * 9,
        "contact_forces",
        [pltpu.VMEM((192, LANES), F32), pltpu.VMEM((96, LANES), F32), pltpu.VMEM((96, LANES), F32)],
    )(dots, swap(dots), ends, nrm, x, v, net, mass, part)
    (spread,) = call(spread_kernel, [((1024, LANES), F32)], [VMEM] * 2, "part_spread")(keep, partner(give, 0))
    chips = lax.axis_size("dom") // 2
    groups = [[2 * i + core for i in range(chips)] for core in range(2)]
    (total,) = call(total_kernel, [((80, LANES), F32)], [VMEM], "part_totals")(swap(spread, groups))
    (motion,) = call(motion_kernel, [((6, PARTS_SIZE), F32)], [VMEM] * 3, "part_motion")(
        total, partner(total, 0), rigid
    )
    return nodal_velocity, motion


def solution(mesh):
    placed = (
        P(None, "dom"),
        P(None, "dom"),
        P(None, "dom"),
        P(None, "dom"),
        P("dom"),
        P(),
        P(None, "dom"),
        P("dom"),
        P(),
        P("dom", None, None),
        P("dom"),
        P("dom", None),
        P("dom"),
        P(None, "dom"),
        P("dom"),
        P(),
        P(),
        P(),
    )
    return jax.shard_map(
        per_device, mesh=mesh, in_specs=placed, out_specs=(P(None, "dom"), P()), check_vma=False
    )
```

```python
import functools

import jax
import jax.numpy as jnp
from jax import lax
from jax.experimental import pallas as pl
from jax.experimental.pallas import tpu as pltpu
from jax.sharding import PartitionSpec as P

CYCLES = 3
PARTS_SIZE = 400

TIME_STEP = 0.1
DAMP_RATIO = 0.05
PENALTY = 2.0
GAP_WIDTH = 0.5
CONTACT_DAMP = 0.2

BF = jnp.bfloat16
F32 = jnp.float32
NT = (((1,), (1,)), ((), ()))
LANES = 128
ROWS = 32
NBR = 5
TOGETHER = 4

VMEM = pl.BlockSpec(memory_space=pltpu.VMEM)
SMEM = pl.BlockSpec(memory_space=pltpu.SMEM)
HBM = pl.BlockSpec(memory_space=pltpu.HBM)


def call(body, outs, in_specs, name, scratch=(), flops=0):
    return pl.pallas_call(
        body,
        out_shape=[jax.ShapeDtypeStruct(s, d) for s, d in outs],
        in_specs=in_specs,
        out_specs=[VMEM] * len(outs),
        scratch_shapes=list(scratch),
        compiler_params=pltpu.CompilerParams(vmem_limit_bytes=40 << 20),
        cost_estimate=pl.CostEstimate(flops=flops, bytes_accessed=1 << 20, transcendentals=0),
        name=name,
    )


def lanes_of(row, idx):
    return jnp.take_along_axis(row, idx, axis=1, mode="promise_in_bounds")


def gather(tab, bases, lo, hi, rows=ROWS):
    acc = [None] * len(bases)
    for h in range(rows):
        here = hi == h
        for c, base in enumerate(bases):
            row = jnp.broadcast_to(tab[base + h : base + h + 1, :], (8, LANES))
            val = lanes_of(row, lo)
            acc[c] = val if h == 0 else jnp.where(here, val, acc[c])
    return acc


def halves(x):
    first = x.astype(BF)
    return first, (x - first.astype(F32)).astype(BF)


def wide(x, a, n):
    row = jnp.broadcast_to(x[a : a + 1, :].astype(F32), (16, LANES)).astype(BF)
    return jnp.concatenate([row] * (n // 16), 0)


def iota_rows(n):
    return lax.broadcasted_iota(jnp.int32, (n, LANES), 0).astype(F32).astype(BF)


def place(lo, hi, vals):
    lof, hif = lo.astype(F32), hi.astype(F32)
    it = iota_rows(LANES)
    split = [halves(v) for v in vals]
    one, zero = jnp.ones((LANES, LANES), BF), jnp.zeros((LANES, LANES), BF)
    left, right = [], []
    for a in range(8):
        right.append(jnp.where(wide(lof, a, LANES) == it, one, zero))
        mask = wide(hif, a, ROWS) == it[:ROWS]
        left.append(
            jnp.concatenate(
                [
                    jnp.where(mask, wide(split[c][s], a, ROWS), zero[:ROWS])
                    for s in range(2)
                    for c in range(len(vals))
                ],
                0,
            )
        )
    return jnp.concatenate(left, 1), jnp.concatenate(right, 1)


def add_placed(acc, lo, hi, vals):
    left, right = place(lo, hi, vals)
    acc[...] += lax.dot_general(left, right, NT, preferred_element_type=F32)


def to_rows(src, dst):
    for c in range(3):
        for h in range(ROWS):
            dst[c * ROWS + h : c * ROWS + h + 1, :] = src[c : c + 1, h * LANES : (h + 1) * LANES]


def elements(idx, mat, tab, cols, g, acc):
    acc[...] = jnp.zeros_like(acc)
    steps = ROWS // TOGETHER

    def corners(i, q):
        here = idx[:, pl.ds(pl.multiple_of((i * TOGETHER + q) * LANES, LANES), LANES)]
        return here & 127, here >> 7

    def fetch(i):
        vals = []
        for q in range(TOGETHER):
            vals += gather(tab, (0, ROWS, 2 * ROWS), *corners(i, q))
        return tuple(vals)

    def step(i, vals):
        upcoming = fetch((i + 1) & (steps - 1))
        left, right = [], []
        for q in range(TOGETHER):
            for c in range(3):
                g[q * 24 + 8 * c : q * 24 + 8 * c + 8, :] = vals[q * 3 + c]
            first = mat[i * TOGETHER + q] * 24
            force = [jnp.zeros((8, LANES), F32)] * 3
            for j in range(24):
                col = cols.at[first + j]
                row = jnp.broadcast_to(g[q * 24 + j : q * 24 + j + 1, :], (8, LANES))
                force = [force[c] + col[8 * c : 8 * c + 8, :] * row for c in range(3)]
            one, two = place(*corners(i, q), force)
            left.append(one)
            right.append(two)
        acc[...] += lax.dot_general(
            jnp.concatenate(left, 1), jnp.concatenate(right, 1), NT, preferred_element_type=F32
        )
        return upcoming

    lax.fori_loop(0, steps, step, fetch(0))


def finish_internal(acc, internal, shared):
    internal[...] = acc[0:96, :] + acc[96:192, :]
    return gather(internal, (0, ROWS, 2 * ROWS), shared[...] & 127, shared[...] >> 7)


def slotted(hitb, rank, vals):
    rows = lax.broadcasted_iota(jnp.int32, (64, LANES), 0).astype(F32)
    mine = jnp.broadcast_to(rank, (64, LANES)) == rows
    left = [jnp.broadcast_to(x, (64, LANES)) for x in vals]
    pieces = []
    for s in range(3):
        pieces.append(jnp.concatenate([jnp.where(mine, x, 0.0).astype(BF) for x in left], 0))
        left = [x - x.astype(BF).astype(F32) for x in left]
    return [hitb] * 3, pieces


def hits_of(owner_row):
    down = lax.broadcasted_iota(jnp.int32, (LANES, LANES), 0)
    return jnp.where(jnp.broadcast_to(owner_row, (LANES, LANES)) == down, 1.0, 0.0)


def slots(owner, master, normal, slot, acc, between):
    acc[...] = jnp.zeros_like(acc)
    down = lax.broadcasted_iota(jnp.int32, (LANES, LANES), 0)
    across = lax.broadcasted_iota(jnp.int32, (LANES, LANES), 1)
    before = jnp.where(down < across, 1.0, 0.0).astype(BF)
    carry = jnp.zeros((LANES, 1), F32)
    for pair in range(8):
        hits, pieces = [], []
        for t in (2 * pair, 2 * pair + 1):
            hit = hits_of(owner[t : t + 1, :])
            hitb = hit.astype(BF)
            count = jnp.dot(hitb, before, preferred_element_type=F32) + carry
            rank = jnp.sum(hit * count, axis=0, keepdims=True)
            carry = carry + jnp.sum(hit, axis=1, keepdims=True)
            slot[t : t + 1, :] = owner[t : t + 1, :] * 64 + rank.astype(jnp.int32)
            vals = [normal[c : c + 1, t * LANES : (t + 1) * LANES] for c in range(3)]
            one, two = slotted(hitb, rank, [*vals, master[t : t + 1, :].astype(F32)])
            hits += one
            pieces += two
        between(pair)
        acc[...] += lax.dot_general(
            jnp.concatenate(hits, 1), jnp.concatenate(pieces, 1), NT, preferred_element_type=F32
        )


def spans():
    return [(h, min(LANES, PARTS_SIZE - h * LANES)) for h in range(4)]


def row_of_tile(row):
    here = lax.broadcasted_iota(jnp.int32, (8, LANES), 0) == (row & 7)
    return pl.ds(pl.multiple_of((row >> 3) << 3, 8), 8), here


def first_kernel(*refs):
    srcs = refs[:18]
    (u, v, fm, mass, pos, idx, inv, cols, part, shared, internal, send, slave, slot, nrm, rigid) = refs[18:34]
    work = refs[34:]
    (disp0, vel0, force0, pos0, shared0, owner, master, normal, stiff) = work[:9]
    pmass, pcenter, pinertia, mat, accel, conn = work[9:15]
    tab, g, acc, small, table, sems = work[15:]
    dsts = (stiff, disp0, vel0, conn, mat, shared0, force0, mass, accel, slave, owner, master, normal)
    dsts = dsts + (pos0, part, pmass, pcenter, pinertia)
    copies = [pltpu.make_async_copy(a, b, sems.at[i]) for i, (a, b) in enumerate(zip(srcs, dsts))]
    for copy in copies:
        copy.start()
    small[...] = jnp.zeros_like(small)
    for copy in copies:
        copy.wait()

    def columns(m):
        for j in range(24):
            cols[m * 24 + j] = jnp.broadcast_to(stiff[m, :, j : j + 1], (24, LANES))

    to_rows(disp0, u)
    to_rows(vel0, v)
    to_rows(force0, fm)
    to_rows(pos0, pos)
    tab[...] = u[...] + DAMP_RATIO * v[...]
    for c in range(3):
        at = slice(c * ROWS, (c + 1) * ROWS)
        fm[at, :] = fm[at, :] / mass[...] - accel[c]
    lane = lax.broadcasted_iota(jnp.int32, (8, LANES), 1)
    for b in range(ROWS):
        at = slice(b * LANES, (b + 1) * LANES)
        idx[:, at] = (conn[:, at] + lane + b * LANES) & 4095
    shared[...] = jnp.zeros_like(shared)
    for b in range(NBR):
        shared[b : b + 1, :] = shared0[b]
    row = lax.broadcasted_iota(jnp.int32, (8, LANES), 0).astype(F32)
    held = row < NBR
    kept = [jnp.where(held, lane.astype(F32), 0.0), jnp.where(held, row + 1.0, 0.0)]
    add_placed(small, shared[...] & 127, shared[...] >> 7, kept)
    inv[...] = (small[0:64, :] + small[64:128, :]).astype(jnp.int32)
    rigid[...] = jnp.ones_like(rigid)
    for h, n in spans():
        at = slice(h * LANES, h * LANES + n)
        rigid[h : h + 1, 0:n] = pmass[0:1, at]
        for c in range(3):
            rigid[8 + 8 * c + h : 9 + 8 * c + h, 0:n] = pcenter[c : c + 1, at]
            rigid[32 + 8 * c + h : 33 + 8 * c + h, 0:n] = pinertia[c : c + 1, at]
    for t in range(16):
        for c in range(3):
            nrm[16 * c + t : 16 * c + t + 1, :] = normal[c : c + 1, t * LANES : (t + 1) * LANES]
    slots(owner, master, normal, slot, table, columns)
    send[:, 0:256] = table[...]
    send[:, 256:640] = jnp.zeros((LANES, 384), F32)
    elements(idx, mat, tab, cols, g, acc)
    own = finish_internal(acc, internal, shared)
    me = lax.axis_index("dom")
    for b in range(NBR):
        tile, here = row_of_tile(me ^ (1 << b))
        for c in range(3):
            row = jnp.broadcast_to(own[c][b : b + 1, :], (8, LANES))
            send[tile, 256 + c * LANES : 256 + (c + 1) * LANES] += jnp.where(here, row, 0.0)


def update(u, v, internal, inv, fm, mass, recv, c, r):
    at = slice(c * ROWS + r, c * ROWS + r + 8)
    slot, which = inv[r : r + 8, :], inv[ROWS + r : ROWS + r + 8, :]
    total = internal[at, :]
    for b in range(NBR):
        row = jnp.broadcast_to(recv[b][c], (8, LANES))
        total = total + jnp.where(which == b + 1, lanes_of(row, slot), 0.0)
    speed = v[at, :] + TIME_STEP * (fm[at, :] - total / mass[r : r + 8, :])
    return at, u[at, :] + TIME_STEP * speed, speed, total


def rows_of(refs):
    return [[ref[c : c + 1, :] for c in range(3)] for ref in refs]


def next_kernel(from_table, u, v, internal, inv, fm, mass, idx, mat, cols, shared, *rest):
    if from_table:
        got, rest = rest[0], rest[1:]
        me = lax.axis_index("dom")
        recv = []
        for b in range(NBR):
            tile, here = row_of_tile(me ^ (1 << b))
            picked = [
                jnp.where(here, got[tile, 256 + c * LANES : 256 + (c + 1) * LANES], 0.0) for c in range(3)
            ]
            recv.append([jnp.sum(x, axis=0, keepdims=True) for x in picked])
    else:
        recv, rest = rows_of(rest[:NBR]), rest[NBR:]
    u2, v2, internal2 = rest[:3]
    own = rest[3:8]
    tab, g, acc = rest[8:]
    for c in range(3):
        for r in range(0, ROWS, 8):
            at, disp, speed, _ = update(u, v, internal, inv, fm, mass, recv, c, r)
            u2[at, :] = disp
            v2[at, :] = speed
            tab[at, :] = disp + DAMP_RATIO * speed
    elements(idx, mat, tab, cols, g, acc)
    vals = finish_internal(acc, internal2, shared)
    for b in range(NBR):
        for c in range(3):
            own[b][c : c + 1, :] = vals[c][b : b + 1, :]


def dots_kernel(u, v, internal, inv, fm, mass, pos, part, slave, slot, nrm, got, *rest):
    recv = rows_of(rest[:5])
    x2, v2, net, dots, midx, mnrm, tab, acc, table, ab, dense = rest[5:]
    for c in range(3):
        for r in range(0, ROWS, 8):
            at, disp, speed, total = update(u, v, internal, inv, fm, mass, recv, c, r)
            place_now = pos[at, :] + disp
            x2[at, :] = place_now
            v2[at, :] = speed
            net[at, :] = mass[r : r + 8, :] * fm[at, :] - total
            tab[at, :] = place_now
            tab[c * ROWS + 96 + r : c * ROWS + 96 + r + 8, :] = speed
    left = lax.broadcasted_iota(jnp.int32, (64, LANES), 1) < 64
    for k, out in ((0, mnrm.at[0]), (1, mnrm.at[1]), (2, mnrm.at[2]), (3, midx)):
        at = slice(LANES * (k // 2), LANES * (k // 2) + LANES)
        top, low = got[0:64, at], got[64:128, at]
        if k % 2:
            out[...] = jnp.where(left, pltpu.roll(top, 64, 1), low).astype(out.dtype)
        else:
            out[...] = jnp.where(left, top, pltpu.roll(low, 64, 1))

    def vals(r):
        m = mass[r : r + 8, :]
        return [m, *[m * tab[c * ROWS + r : c * ROWS + r + 8, :] for c in range(3)]]

    def both(here, w):
        y = gather(tab, tuple(range(0, 192, ROWS)), here & 127, here >> 7)
        return y[0] * w[0] + y[1] * w[1] + y[2] * w[2], y[3] * w[0] + y[4] * w[1] + y[5] * w[2]

    for r in (0, 8):
        w = [nrm[16 * c + r : 16 * c + r + 8, :] for c in range(3)]
        ab[r : r + 8, :], ab[16 + r : 24 + r, :] = both(slave[r : r + 8, :], w)
    acc[...] = jnp.zeros_like(acc)
    part_sums(part, vals, acc, True)
    moments = jnp.concatenate([acc[0:32, :] + acc[32:64, :], jnp.zeros((96, LANES), F32)], 0)
    dots[:, 256:384] = moments.T
    table[...] = jnp.zeros_like(table)

    def step(i, carry):
        for q in range(2):
            at = pl.ds(pl.multiple_of(i * 16 + q * 8, 8), 8)
            dense[0, at, :], dense[1, at, :] = both(midx[at, :], [mnrm[c, at, :] for c in range(3)])
        hits, pieces = [], []
        for q in range(4):
            at = pl.ds(i * 4 + q, 1)
            here = slot[at, :]
            rows = [ab[at, :], ab[pl.ds(16 + i * 4 + q, 1), :]]
            one, two = slotted(hits_of(here >> 6).astype(BF), (here & 63).astype(F32), rows)
            hits += one
            pieces += two
        table[...] += lax.dot_general(
            jnp.concatenate(hits, 1), jnp.concatenate(pieces, 1), NT, preferred_element_type=F32
        )
        return carry

    lax.fori_loop(0, 4, step, 0)
    dots[:, 0:128] = table[...]
    dots[0:64, 128:256] = jnp.where(left, dense[0], pltpu.roll(dense[1], 64, 1))
    dots[64:128, 128:256] = jnp.where(left, pltpu.roll(dense[0], 64, 1), dense[1])


def part_sums(part, vals, acc, by_device):
    it = iota_rows(LANES)
    it8 = (lax.broadcasted_iota(jnp.int32, (16, LANES), 0) & 7).astype(F32).astype(BF)
    one, zero = jnp.ones((LANES, LANES), BF), jnp.zeros((LANES, LANES), BF)
    for r in range(0, ROWS, 8):
        here = part[r : r + 8, :]
        lo = here & 127
        if by_device:
            lo = ((lo & 63) << 1) | (lo >> 6)
        lof, hif = lo.astype(F32), (here >> 7).astype(F32)
        val = vals(r)
        first = [x.astype(BF).astype(F32) for x in val]
        split = (first, [x - y for x, y in zip(val, first)])
        left, right = [], []
        for a in range(8):
            right.append(jnp.where(wide(lof, a, LANES) == it, one, zero))
            mask = wide(hif, a, 16) == it8
            rows = []
            for s in range(2):
                for k in range(0, len(val), 2):
                    two = [jnp.broadcast_to(split[s][k + d][a : a + 1, :], (8, LANES)) for d in range(2)]
                    rows.append(jnp.where(mask, jnp.concatenate(two, 0).astype(BF), zero[:16]))
            left.append(jnp.concatenate(rows, 0))
        acc[...] += lax.dot_general(
            jnp.concatenate(left, 1), jnp.concatenate(right, 1), NT, preferred_element_type=F32
        )


def contact_kernel(
    dots, got, slave, slot, nrm, midx, mnrm, x, v, net, mass, part, nodal, keep, give, acc, tot, acc2, push, mine
):
    acc[...] = jnp.zeros_like(acc)
    acc2[...] = jnp.zeros_like(acc2)
    left = lax.broadcasted_iota(jnp.int32, (LANES, LANES), 1) < 64
    as_slave = dots[:, 0:128] - got[:, 128:256]
    as_master = got[:, 0:128] - dots[:, 128:256]
    gap = jnp.where(left, as_slave, pltpu.roll(as_master, 64, 1))
    closing = jnp.where(left, pltpu.roll(as_slave, 64, 1), as_master)
    z = -gap / GAP_WIDTH
    soft = jnp.maximum(z, 0.0) + jnp.log1p(jnp.exp(-jnp.abs(z)))
    size = PENALTY * GAP_WIDTH * soft - CONTACT_DAMP * closing
    top, low = size[0:64, :], size[64:128, :]
    mine[...] = jnp.where(left[0:64, :], top, pltpu.roll(low, 64, 1))
    push[...] = -jnp.where(left[0:64, :], pltpu.roll(top, 64, 1), low)

    def step(i, carry):
        one, two = [], []
        for q in range(4):
            at = pl.ds(pl.multiple_of(i * 32 + q * 8, 8), 8)
            here, size = midx[at, :], push[at, :]
            pair = place(here & 127, here >> 7, [size * mnrm[c, at, :] for c in range(3)])
            one.append(pair[0])
            two.append(pair[1])
        acc[...] += lax.dot_general(
            jnp.concatenate(one, 1), jnp.concatenate(two, 1), NT, preferred_element_type=F32
        )
        return carry

    lax.fori_loop(0, 2, step, 0)
    one, two = [], []
    for r in (0, 8):
        here, at = slave[r : r + 8, :], slot[r : r + 8, :]
        (size,) = gather(mine, (0,), ((at >> 12) << 6) + (at & 63), (at >> 6) & 63, 64)
        pair = place(here & 127, here >> 7, [size * nrm[16 * c + r : 16 * c + r + 8, :] for c in range(3)])
        one.append(pair[0])
        two.append(pair[1])
    acc[...] += lax.dot_general(
        jnp.concatenate(one, 1), jnp.concatenate(two, 1), NT, preferred_element_type=F32
    )
    contact = acc[0:96, :] + acc[96:192, :]
    tot[...] = net[...] + contact
    for c in range(3):
        speed = v[c * ROWS : (c + 1) * ROWS, :] + TIME_STEP * contact[c * ROWS : (c + 1) * ROWS, :] / mass[...]
        for h in range(ROWS):
            nodal[c : c + 1, h * LANES : (h + 1) * LANES] = speed[h : h + 1, :]

    def vals(r):
        p = [x[c * ROWS + r : c * ROWS + r + 8, :] for c in range(3)]
        n = [tot[c * ROWS + r : c * ROWS + r + 8, :] for c in range(3)]
        return [
            *n,
            p[1] * n[2] - p[2] * n[1],
            p[2] * n[0] - p[0] * n[2],
            p[0] * n[1] - p[1] * n[0],
        ]

    part_sums(part, vals, acc2, False)
    acc2[0:48, :] = acc2[0:48, :] + acc2[48:96, :]
    lane = lax.broadcasted_iota(jnp.int32, (8, LANES), 1)
    last = jnp.zeros((8, LANES), F32)
    for k in range(6):
        piece = jnp.where(lane < 16, acc2[8 * k : 8 * k + 8, :], 0.0)
        last = last + (pltpu.roll(piece, 16 * k, 1) if k else piece)
    even = lax.axis_index("dom") & 1 == 0
    pairs = [(acc2[8 * k : 8 * k + 1, :], acc2[8 * k + 2 : 8 * k + 3, :]) for k in range(6)]
    pairs += [(acc2[8 * k + 1 : 8 * k + 2, :], acc2[8 * k + 25 : 8 * k + 26, :]) for k in range(3)]
    pairs += [(jnp.zeros((1, LANES), F32), last[3:4, :])]
    for k, (low, high) in enumerate(pairs):
        keep[k : k + 1, :] = jnp.where(even, low, high)
        give[k : k + 1, :] = jnp.where(even, high, low)
    keep[10:16, :] = jnp.zeros((6, LANES), F32)
    give[10:16, :] = jnp.zeros((6, LANES), F32)
    moments = jnp.broadcast_to(jnp.sum(got[:, 256:384], axis=0, keepdims=True), (8, LANES))
    moments = jnp.where(lane < 96, 0.0, pltpu.roll(moments, 96, 1))
    keep[9:10, :] = keep[9:10, :] + moments[0:1, :]


def spread_kernel(keep, given, out):
    tile = keep[...] + given[...]
    for k in range(10):
        out[:, k * LANES : (k + 1) * LANES] = jnp.broadcast_to(tile[k : k + 1, :], (64, LANES))


def total_kernel(got, out):
    for k in range(10):
        out[k : k + 1, :] = jnp.sum(got[:, k * LANES : (k + 1) * LANES], axis=0, keepdims=True)
    out[10:16, :] = jnp.zeros((6, LANES), F32)
    out[16:80, :] = pltpu.roll(got[:, 9 * LANES : 10 * LANES], 32, 1)


def motion_kernel(mine, other, rigid, out):
    even = lax.axis_index("dom") & 1 == 0
    low = jnp.where(even, mine[...], other[...])
    high = jnp.where(even, other[...], mine[...])
    by = jnp.concatenate([low[16:80, :], high[16:80, :]], 0).T
    moments = [by[8 * k : 8 * k + 4, :] for k in range(4)]
    sums = []
    for k in range(6):
        second = low[6 + k : 7 + k, :] if k < 3 else high[3 + k : 4 + k, :]
        last = pltpu.roll(high[8:16, :], LANES - 16 * k, 1) if k else high[8:16, :]
        sums.append(jnp.concatenate([low[k : k + 1, :], second, high[k : k + 1, :], last[1:2, :]], 0))
    own = rigid[0:4, :]
    mass = own + moments[0]
    centre = [(own * rigid[8 + 8 * c : 12 + 8 * c, :] + moments[1 + c]) / mass for c in range(3)]
    force, turn = sums[0:3], sums[3:6]
    rows = [y / mass for y in force]
    for c in range(3):
        a, b = (c + 1) % 3, (c + 2) % 3
        moment = turn[c] - (centre[a] * force[b] - centre[b] * force[a])
        rows.append(moment / rigid[32 + 8 * c : 36 + 8 * c, :])
    for r, row in enumerate(rows):
        for h, n in spans():
            out[r : r + 1, h * LANES : h * LANES + n] = row[h : h + 1, 0:n]


def partner(block, apart):
    count = lax.axis_size("dom")
    return lax.ppermute(block, "dom", [(i, i ^ (1 << apart)) for i in range(count)])


def swap(block, groups=None):
    return lax.all_to_all(block, "dom", 0, 0, tiled=True, axis_index_groups=groups)


def per_device(
    rest_pos,
    displacement,
    velocity,
    ext_force,
    node_mass,
    body_accel,
    connectivity,
    elem_material,
    stiffness,
    shared_nodes,
    contact_slave,
    contact_owner,
    contact_master,
    contact_normal,
    part_of_node,
    part_mass,
    part_center,
    part_inertia,
):
    state = ((96, LANES), F32)
    table = ((LANES, 5 * LANES), F32)
    own = [((3, LANES), F32)] * NBR
    work = [
        pltpu.VMEM((96, LANES), F32),
        pltpu.VMEM((24 * TOGETHER, LANES), F32),
        pltpu.VMEM((192, LANES), F32),
    ]
    inputs = (
        stiffness,
        displacement,
        velocity,
        connectivity,
        elem_material,
        shared_nodes.transpose(1, 0, 2),
        ext_force,
        node_mass.reshape(ROWS, LANES),
        body_accel,
        contact_slave.reshape(16, LANES),
        contact_owner.reshape(16, LANES),
        contact_master.reshape(16, LANES),
        contact_normal,
        rest_pos,
        part_of_node.reshape(ROWS, LANES),
        part_mass.reshape(1, PARTS_SIZE),
        part_center,
        part_inertia,
    )
    rows, ints = ((ROWS, LANES), F32), jnp.int32
    u, v, fm, mass, pos, idx, inv, cols, part, shared, internal, send, slave, slot, nrm, rigid = call(
        first_kernel,
        [
            state,
            state,
            state,
            rows,
            state,
            ((8, 4096), ints),
            ((64, LANES), ints),
            ((192, 24, LANES), F32),
            ((ROWS, LANES), ints),
            ((8, LANES), ints),
            state,
            table,
            ((16, LANES), ints),
            ((16, LANES), ints),
            ((48, LANES), F32),
            ((56, LANES), F32),
        ],
        [HBM] * 18,
        "first_cycle",
        [
            *[pltpu.VMEM((3, 4096), F32)] * 4,
            pltpu.VMEM((NBR, 1, LANES), ints),
            *[pltpu.VMEM((16, LANES), ints)] * 2,
            pltpu.VMEM((3, 2048), F32),
            pltpu.VMEM((8, 24, 24), F32),
            pltpu.VMEM((1, PARTS_SIZE), F32),
            pltpu.VMEM((3, PARTS_SIZE), F32),
            pltpu.VMEM((3, PARTS_SIZE), F32),
            pltpu.SMEM((ROWS,), ints),
            pltpu.SMEM((3,), F32),
            pltpu.VMEM((8, 4096), ints),
            *work,
            pltpu.VMEM((LANES, LANES), F32),
            pltpu.VMEM((LANES, 2 * LANES), F32),
            pltpu.SemaphoreType.DMA((18,)),
        ],
    )(*[pltpu.with_memory_space_constraint(x, pltpu.HBM) for x in inputs])
    got = swap(send)
    recv = [got]
    for n in range(CYCLES - 1):
        u, v, internal, *mine = call(
            functools.partial(next_kernel, n == 0),
            [state, state, state, *own],
            [VMEM] * 7 + [SMEM] + [VMEM] * (2 + len(recv)),
            "next_cycle",
            work,
        )(u, v, internal, inv, fm, mass, idx, elem_material, cols, shared, *recv)
        recv = [partner(mine[b], b) for b in range(NBR)]

    trio = ((LANES, 3 * LANES), F32)
    x, v, net, dots, midx, mnrm = call(
        dots_kernel,
        [state, state, state, trio, ((64, LANES), ints), ((3, 64, LANES), F32)],
        [VMEM] * 17,
        "contact_dots",
        [
            pltpu.VMEM((192, LANES), F32),
            pltpu.VMEM((64, LANES), F32),
            pltpu.VMEM((LANES, LANES), F32),
            pltpu.VMEM((32, LANES), F32),
            pltpu.VMEM((2, 64, LANES), F32),
        ],
    )(u, v, internal, inv, fm, mass, pos, part, slave, slot, nrm, got, *recv)
    half = ((16, LANES), F32)
    nodal_velocity, keep, give = call(
        contact_kernel,
        [((3, 4096), F32), half, half],
        [VMEM] * 12,
        "contact_forces",
        [
            pltpu.VMEM((192, LANES), F32),
            pltpu.VMEM((96, LANES), F32),
            pltpu.VMEM((96, LANES), F32),
            pltpu.VMEM((64, LANES), F32),
            pltpu.VMEM((64, LANES), F32),
        ],
    )(dots, swap(dots), slave, slot, nrm, midx, mnrm, x, v, net, mass, part)
    (spread,) = call(spread_kernel, [((64, 10 * LANES), F32)], [VMEM] * 2, "part_spread")(keep, partner(give, 0))
    chips = lax.axis_size("dom") // 2
    groups = [[2 * i + core for i in range(chips)] for core in range(2)]
    (total,) = call(total_kernel, [((80, LANES), F32)], [VMEM], "part_totals")(swap(spread, groups))
    (motion,) = call(motion_kernel, [((6, PARTS_SIZE), F32)], [VMEM] * 3, "part_motion")(
        total, partner(total, 0), rigid
    )
    return nodal_velocity, motion


def solution(mesh):
    placed = (
        P(None, "dom"),
        P(None, "dom"),
        P(None, "dom"),
        P(None, "dom"),
        P("dom"),
        P(),
        P(None, "dom"),
        P("dom"),
        P(),
        P("dom", None, None),
        P("dom"),
        P("dom", None),
        P("dom"),
        P(None, "dom"),
        P("dom"),
        P(),
        P(),
        P(),
    )
    return jax.shard_map(
        per_device, mesh=mesh, in_specs=placed, out_specs=(P(None, "dom"), P()), check_vma=False
    )
```

```python
import functools

import jax
import jax.numpy as jnp
from jax import lax
from jax.experimental import pallas as pl
from jax.experimental.pallas import tpu as pltpu
from jax.sharding import PartitionSpec as P

CYCLES = 3
PARTS_SIZE = 400

TIME_STEP = 0.1
DAMP_RATIO = 0.05
PENALTY = 2.0
GAP_WIDTH = 0.5
CONTACT_DAMP = 0.2

BF = jnp.bfloat16
F32 = jnp.float32
NT = (((1,), (1,)), ((), ()))
LANES = 128
ROWS = 32
NBR = 5
TOGETHER = 4

VMEM = pl.BlockSpec(memory_space=pltpu.VMEM)
SMEM = pl.BlockSpec(memory_space=pltpu.SMEM)
HBM = pl.BlockSpec(memory_space=pltpu.HBM)


def call(body, outs, in_specs, name, scratch=(), flops=0):
    return pl.pallas_call(
        body,
        out_shape=[jax.ShapeDtypeStruct(s, d) for s, d in outs],
        in_specs=in_specs,
        out_specs=[VMEM] * len(outs),
        scratch_shapes=list(scratch),
        compiler_params=pltpu.CompilerParams(vmem_limit_bytes=40 << 20),
        cost_estimate=pl.CostEstimate(flops=flops, bytes_accessed=1 << 20, transcendentals=0),
        name=name,
    )


def lanes_of(row, idx):
    return jnp.take_along_axis(row, idx, axis=1, mode="promise_in_bounds")


def gather(tab, bases, lo, hi, rows=ROWS):
    acc = [None] * len(bases)
    for h in range(rows):
        here = hi == h
        for c, base in enumerate(bases):
            row = jnp.broadcast_to(tab[base + h : base + h + 1, :], (8, LANES))
            val = lanes_of(row, lo)
            acc[c] = val if h == 0 else jnp.where(here, val, acc[c])
    return acc


def halves(x):
    first = x.astype(BF)
    return first, (x - first.astype(F32)).astype(BF)


def wide(x, a, n):
    row = jnp.broadcast_to(x[a : a + 1, :].astype(F32), (16, LANES)).astype(BF)
    return jnp.concatenate([row] * (n // 16), 0)


def iota_rows(n):
    return lax.broadcasted_iota(jnp.int32, (n, LANES), 0).astype(F32).astype(BF)


def place(lo, hi, vals):
    lof, hif = lo.astype(F32), hi.astype(F32)
    it = iota_rows(LANES)
    split = [halves(v) for v in vals]
    one, zero = jnp.ones((LANES, LANES), BF), jnp.zeros((LANES, LANES), BF)
    left, right = [], []
    for a in range(8):
        right.append(jnp.where(wide(lof, a, LANES) == it, one, zero))
        mask = wide(hif, a, ROWS) == it[:ROWS]
        left.append(
            jnp.concatenate(
                [
                    jnp.where(mask, wide(split[c][s], a, ROWS), zero[:ROWS])
                    for s in range(2)
                    for c in range(len(vals))
                ],
                0,
            )
        )
    return jnp.concatenate(left, 1), jnp.concatenate(right, 1)


def add_placed(acc, lo, hi, vals):
    left, right = place(lo, hi, vals)
    acc[...] += lax.dot_general(left, right, NT, preferred_element_type=F32)


def to_rows(src, dst):
    for c in range(3):
        for h in range(ROWS):
            dst[c * ROWS + h : c * ROWS + h + 1, :] = src[c : c + 1, h * LANES : (h + 1) * LANES]


def elements(idx, mat, tab, cols, g, acc):
    acc[...] = jnp.zeros_like(acc)
    steps = ROWS // TOGETHER

    def corners(i, q):
        here = idx[:, pl.ds(pl.multiple_of((i * TOGETHER + q) * LANES, LANES), LANES)]
        return here & 127, here >> 7

    def fetch(i):
        vals = []
        for q in range(TOGETHER):
            vals += gather(tab, (0, ROWS, 2 * ROWS), *corners(i, q))
        return tuple(vals)

    def step(i, vals):
        upcoming = fetch((i + 1) & (steps - 1))
        left, right = [], []
        for q in range(TOGETHER):
            for c in range(3):
                g[q * 24 + 8 * c : q * 24 + 8 * c + 8, :] = vals[q * 3 + c]
            first = mat[i * TOGETHER + q] * 24
            force = [jnp.zeros((8, LANES), F32)] * 3
            for j in range(24):
                col = cols.at[first + j]
                row = jnp.broadcast_to(g[q * 24 + j : q * 24 + j + 1, :], (8, LANES))
                force = [force[c] + col[8 * c : 8 * c + 8, :] * row for c in range(3)]
            one, two = place(*corners(i, q), force)
            left.append(one)
            right.append(two)
        acc[...] += lax.dot_general(
            jnp.concatenate(left, 1), jnp.concatenate(right, 1), NT, preferred_element_type=F32
        )
        return upcoming

    lax.fori_loop(0, steps, step, fetch(0))


def finish_internal(acc, internal, shared):
    internal[...] = acc[0:96, :] + acc[96:192, :]
    return gather(internal, (0, ROWS, 2 * ROWS), shared[...] & 127, shared[...] >> 7)


def slotted(hitb, rank, vals):
    rows = lax.broadcasted_iota(jnp.int32, (64, LANES), 0).astype(F32)
    mine = jnp.broadcast_to(rank, (64, LANES)) == rows
    left = [jnp.broadcast_to(x, (64, LANES)) for x in vals]
    pieces = []
    for s in range(3):
        pieces.append(jnp.concatenate([jnp.where(mine, x, 0.0).astype(BF) for x in left], 0))
        left = [x - x.astype(BF).astype(F32) for x in left]
    return [hitb] * 3, pieces


def hits_of(owner_row):
    down = lax.broadcasted_iota(jnp.int32, (LANES, LANES), 0)
    return jnp.where(jnp.broadcast_to(owner_row, (LANES, LANES)) == down, 1.0, 0.0)


def slots(owner, master, normal, slot, acc, between):
    acc[...] = jnp.zeros_like(acc)
    down = lax.broadcasted_iota(jnp.int32, (LANES, LANES), 0)
    across = lax.broadcasted_iota(jnp.int32, (LANES, LANES), 1)
    before = jnp.where(down < across, 1.0, 0.0).astype(BF)
    carry = jnp.zeros((LANES, 1), F32)
    for pair in range(8):
        hits, pieces = [], []
        for t in (2 * pair, 2 * pair + 1):
            hit = hits_of(owner[t : t + 1, :])
            hitb = hit.astype(BF)
            count = jnp.dot(hitb, before, preferred_element_type=F32) + carry
            rank = jnp.sum(hit * count, axis=0, keepdims=True)
            carry = carry + jnp.sum(hit, axis=1, keepdims=True)
            slot[t : t + 1, :] = owner[t : t + 1, :] * 64 + rank.astype(jnp.int32)
            vals = [normal[c : c + 1, t * LANES : (t + 1) * LANES] for c in range(3)]
            one, two = slotted(hitb, rank, [*vals, master[t : t + 1, :].astype(F32)])
            hits += one
            pieces += two
        between(pair)
        acc[...] += lax.dot_general(
            jnp.concatenate(hits, 1), jnp.concatenate(pieces, 1), NT, preferred_element_type=F32
        )


def spans():
    return [(h, min(LANES, PARTS_SIZE - h * LANES)) for h in range(4)]


def row_of_tile(row):
    here = lax.broadcasted_iota(jnp.int32, (8, LANES), 0) == (row & 7)
    return pl.ds(pl.multiple_of((row >> 3) << 3, 8), 8), here


def copy_all(srcs, dsts, sems):
    copies = [pltpu.make_async_copy(a, b, sems.at[i]) for i, (a, b) in enumerate(zip(srcs, dsts))]
    for copy in copies:
        copy.start()
    return copies


def first_kernel(*refs):
    srcs = refs[:13]
    u, v, fm, mass, idx, cols, shared, internal, send, slave, slot, normal = refs[13:25]
    disp0, vel0, force0, shared0, owner, master, stiff, mat, accel, conn, tab, g, acc, table, sems = refs[25:]
    dsts = (stiff, owner, master, normal, disp0, vel0, conn, mat, shared0, force0, mass, accel, slave)
    copies = copy_all(srcs, dsts, sems)

    def columns(m):
        for j in range(24):
            cols[m * 24 + j] = jnp.broadcast_to(stiff[m, :, j : j + 1], (24, LANES))

    for copy in copies[:4]:
        copy.wait()
    slots(owner, master, normal, slot, table, columns)
    send[:, 0:256] = table[...]
    send[:, 256:640] = jnp.zeros((LANES, 384), F32)
    for copy in copies[4:]:
        copy.wait()
    to_rows(disp0, u)
    to_rows(vel0, v)
    to_rows(force0, fm)
    tab[...] = u[...] + DAMP_RATIO * v[...]
    for c in range(3):
        at = slice(c * ROWS, (c + 1) * ROWS)
        fm[at, :] = fm[at, :] / mass[...] - accel[c]
    lane = lax.broadcasted_iota(jnp.int32, (8, LANES), 1)
    for b in range(ROWS):
        at = slice(b * LANES, (b + 1) * LANES)
        idx[:, at] = (conn[:, at] + lane + b * LANES) & 4095
    shared[...] = jnp.zeros_like(shared)
    for b in range(NBR):
        shared[b : b + 1, :] = shared0[b]
    elements(idx, mat, tab, cols, g, acc)
    own = finish_internal(acc, internal, shared)
    me = lax.axis_index("dom")
    for b in range(NBR):
        tile, here = row_of_tile(me ^ (1 << b))
        for c in range(3):
            row = jnp.broadcast_to(own[c][b : b + 1, :], (8, LANES))
            send[tile, 256 + c * LANES : 256 + (c + 1) * LANES] += jnp.where(here, row, 0.0)


def fixed_kernel(*refs):
    pos0, part0, pmass0, pcenter0, pinertia0, normal, shared, mass, pos, part, inv, nrm, light, rigid = refs[:14]
    pos1, pmass, pcenter, pinertia, small, sems = refs[14:]
    copies = copy_all(
        (pos0, part0, pmass0, pcenter0, pinertia0), (pos1, part, pmass, pcenter, pinertia), sems
    )
    small[...] = jnp.zeros_like(small)
    lane = lax.broadcasted_iota(jnp.int32, (8, LANES), 1)
    row = lax.broadcasted_iota(jnp.int32, (8, LANES), 0)
    held = row < NBR
    lo, hi = shared[...] & 127, shared[...] >> 7
    kept = [jnp.where(held, lane, 0).astype(F32), jnp.where(held, row + 1, 0).astype(F32)]
    add_placed(small, lo, hi, kept)
    found = (small[0:64, :] + small[64:128, :]).astype(jnp.int32)
    inv[...] = found[0:ROWS, :] + found[ROWS : 2 * ROWS, :] * LANES
    (weight,) = gather(mass, (0,), lo, hi)
    light[...] = -TIME_STEP / weight
    for t in range(16):
        for c in range(3):
            nrm[16 * c + t : 16 * c + t + 1, :] = normal[c : c + 1, t * LANES : (t + 1) * LANES]
    rigid[...] = jnp.ones_like(rigid)
    for copy in copies:
        copy.wait()
    to_rows(pos1, pos)
    for h, n in spans():
        at = slice(h * LANES, h * LANES + n)
        rigid[h : h + 1, 0:n] = pmass[0:1, at]
        for c in range(3):
            rigid[8 + 8 * c + h : 9 + 8 * c + h, 0:n] = pcenter[c : c + 1, at]
            rigid[32 + 8 * c + h : 33 + 8 * c + h, 0:n] = pinertia[c : c + 1, at]


def from_shared(code, rows):
    total = 0.0
    for b in range(NBR):
        row = jnp.broadcast_to(rows[b], (8, LANES))
        total = total + jnp.where(code >> 7 == b + 1, lanes_of(row, code & 127), 0.0)
    return total


def update(u, v, internal, inv, fm, mass, recv, c, r):
    at = slice(c * ROWS + r, c * ROWS + r + 8)
    total = internal[at, :] + from_shared(inv[r : r + 8, :], [recv[b][c] for b in range(NBR)])
    speed = v[at, :] + TIME_STEP * (fm[at, :] - total / mass[r : r + 8, :])
    return at, u[at, :] + TIME_STEP * speed, speed, total


def rows_of(refs):
    return [[ref[c : c + 1, :] for c in range(3)] for ref in refs]


def next_kernel(from_table, u, v, internal, inv, fm, mass, idx, mat, cols, shared, *rest):
    if from_table:
        got, rest = rest[0], rest[1:]
        me = lax.axis_index("dom")
        recv = []
        for b in range(NBR):
            tile, here = row_of_tile(me ^ (1 << b))
            picked = [
                jnp.where(here, got[tile, 256 + c * LANES : 256 + (c + 1) * LANES], 0.0) for c in range(3)
            ]
            recv.append([jnp.sum(x, axis=0, keepdims=True) for x in picked])
    else:
        recv, rest = rows_of(rest[:NBR]), rest[NBR:]
    u2, v2, internal2 = rest[:3]
    own = rest[3:8]
    tab, g, acc = rest[8:]
    for c in range(3):
        for r in range(0, ROWS, 8):
            at, disp, speed, _ = update(u, v, internal, inv, fm, mass, recv, c, r)
            u2[at, :] = disp
            v2[at, :] = speed
            tab[at, :] = disp + DAMP_RATIO * speed
    elements(idx, mat, tab, cols, g, acc)
    vals = finish_internal(acc, internal2, shared)
    for b in range(NBR):
        for c in range(3):
            own[b][c : c + 1, :] = vals[c][b : b + 1, :]


def ends_kernel(got, slave, inv, midx, mnrm, code):
    left = lax.broadcasted_iota(jnp.int32, (64, LANES), 1) < 64
    for k, out in ((0, mnrm.at[0]), (1, mnrm.at[1]), (2, mnrm.at[2]), (3, midx)):
        at = slice(LANES * (k // 2), LANES * (k // 2) + LANES)
        top, low = got[0:64, at], got[64:128, at]
        if k % 2:
            out[...] = jnp.where(left, pltpu.roll(top, 64, 1), low).astype(out.dtype)
        else:
            out[...] = jnp.where(left, top, pltpu.roll(low, 64, 1))
    for r in range(0, 80, 8):
        here = slave[r : r + 8, :] if r < 16 else midx[r - 16 : r - 8, :]
        (code[r : r + 8, :],) = gather(inv, (0,), here & 127, here >> 7)


def base_kernel(u, v, internal, fm, mass, pos, slave, nrm, midx, mnrm, x2, v2, ab, tab):
    for c in range(3):
        for r in range(0, ROWS, 8):
            at = slice(c * ROWS + r, c * ROWS + r + 8)
            speed = v[at, :] + TIME_STEP * (fm[at, :] - internal[at, :] / mass[r : r + 8, :])
            place_now = pos[at, :] + (u[at, :] + TIME_STEP * speed)
            x2[at, :] = place_now
            v2[at, :] = speed
            tab[at, :] = place_now
            tab[c * ROWS + 96 + r : c * ROWS + 96 + r + 8, :] = speed

    def both(here, w):
        y = gather(tab, tuple(range(0, 192, ROWS)), here & 127, here >> 7)
        return y[0] * w[0] + y[1] * w[1] + y[2] * w[2], y[3] * w[0] + y[4] * w[1] + y[5] * w[2]

    for r in (0, 8):
        w = [nrm[16 * c + r : 16 * c + r + 8, :] for c in range(3)]
        ab[0, r : r + 8, :], ab[1, r : r + 8, :] = both(slave[r : r + 8, :], w)

    def step(i, carry):
        for q in range(2):
            at = pl.ds(pl.multiple_of(i * 16 + q * 8, 8), 8)
            to = pl.ds(pl.multiple_of(i * 16 + q * 8 + 16, 8), 8)
            ab[0, to, :], ab[1, to, :] = both(midx[at, :], [mnrm[c, at, :] for c in range(3)])
        return carry

    lax.fori_loop(0, 4, step, 0)


def dots_kernel(x1, v1, ab1, internal, inv, light, fm, mass, part, slot, nrm, mnrm, code, *rest):
    recv = rows_of(rest[:5])
    x2, v2, net, dots, acc, table, ab = rest[5:]
    for c in range(3):
        for r in range(0, ROWS, 8):
            at = slice(c * ROWS + r, c * ROWS + r + 8)
            m = mass[r : r + 8, :]
            more = from_shared(inv[r : r + 8, :], [recv[b][c] for b in range(NBR)])
            change = -TIME_STEP * (more / m)
            x2[at, :] = x1[at, :] + TIME_STEP * change
            v2[at, :] = v1[at, :] + change
            net[at, :] = m * fm[at, :] - internal[at, :] - more
    moved = [[recv[b][c] * light[b : b + 1, :] for b in range(NBR)] for c in range(3)]
    for r in range(0, 80, 8):
        here = code[r : r + 8, :]
        if r < 16:
            w = [nrm[16 * c + r : 16 * c + r + 8, :] for c in range(3)]
        else:
            w = [mnrm[c, r - 16 : r - 8, :] for c in range(3)]
        d = [from_shared(here, moved[c]) for c in range(3)]
        change = d[0] * w[0] + d[1] * w[1] + d[2] * w[2]
        ab[0, r : r + 8, :] = ab1[0, r : r + 8, :] + TIME_STEP * change
        ab[1, r : r + 8, :] = ab1[1, r : r + 8, :] + change

    def vals(r):
        m = mass[r : r + 8, :]
        return [m, *[m * x2[c * ROWS + r : c * ROWS + r + 8, :] for c in range(3)]]

    acc[...] = jnp.zeros_like(acc)
    part_sums(part, vals, acc, True)
    moments = jnp.concatenate([acc[0:32, :] + acc[32:64, :], jnp.zeros((96, LANES), F32)], 0)
    dots[:, 256:384] = moments.T
    table[...] = jnp.zeros_like(table)
    for i in range(4):
        hits, pieces = [], []
        for t in range(4 * i, 4 * i + 4):
            here = slot[t : t + 1, :]
            rows = [ab[0, t : t + 1, :], ab[1, t : t + 1, :]]
            one, two = slotted(hits_of(here >> 6).astype(BF), (here & 63).astype(F32), rows)
            hits += one
            pieces += two
        table[...] += lax.dot_general(
            jnp.concatenate(hits, 1), jnp.concatenate(pieces, 1), NT, preferred_element_type=F32
        )
    left = lax.broadcasted_iota(jnp.int32, (64, LANES), 1) < 64
    one, two = ab[0, 16:80, :], ab[1, 16:80, :]
    dots[:, 0:128] = table[...]
    dots[0:64, 128:256] = jnp.where(left, one, pltpu.roll(two, 64, 1))
    dots[64:128, 128:256] = jnp.where(left, pltpu.roll(one, 64, 1), two)


def part_sums(part, vals, acc, by_device):
    it = iota_rows(LANES)
    it8 = (lax.broadcasted_iota(jnp.int32, (16, LANES), 0) & 7).astype(F32).astype(BF)
    one, zero = jnp.ones((LANES, LANES), BF), jnp.zeros((LANES, LANES), BF)
    for r in range(0, ROWS, 8):
        here = part[r : r + 8, :]
        lo = here & 127
        if by_device:
            lo = ((lo & 63) << 1) | (lo >> 6)
        lof, hif = lo.astype(F32), (here >> 7).astype(F32)
        val = vals(r)
        first = [x.astype(BF).astype(F32) for x in val]
        split = (first, [x - y for x, y in zip(val, first)])
        left, right = [], []
        for a in range(8):
            right.append(jnp.where(wide(lof, a, LANES) == it, one, zero))
            mask = wide(hif, a, 16) == it8
            rows = []
            for s in range(2):
                for k in range(0, len(val), 2):
                    two = [jnp.broadcast_to(split[s][k + d][a : a + 1, :], (8, LANES)) for d in range(2)]
                    rows.append(jnp.where(mask, jnp.concatenate(two, 0).astype(BF), zero[:16]))
            left.append(jnp.concatenate(rows, 0))
        acc[...] += lax.dot_general(
            jnp.concatenate(left, 1), jnp.concatenate(right, 1), NT, preferred_element_type=F32
        )


def contact_kernel(
    dots, got, slave, slot, nrm, midx, mnrm, x, net, part, contact, keep, give, acc, tot, acc2, push, mine
):
    acc[...] = jnp.zeros_like(acc)
    acc2[...] = jnp.zeros_like(acc2)
    left = lax.broadcasted_iota(jnp.int32, (LANES, LANES), 1) < 64
    as_slave = dots[:, 0:128] - got[:, 128:256]
    as_master = got[:, 0:128] - dots[:, 128:256]
    gap = jnp.where(left, as_slave, pltpu.roll(as_master, 64, 1))
    closing = jnp.where(left, pltpu.roll(as_slave, 64, 1), as_master)
    z = -gap / GAP_WIDTH
    soft = jnp.maximum(z, 0.0) + jnp.log1p(jnp.exp(-jnp.abs(z)))
    size = PENALTY * GAP_WIDTH * soft - CONTACT_DAMP * closing
    top, low = size[0:64, :], size[64:128, :]
    mine[...] = jnp.where(left[0:64, :], top, pltpu.roll(low, 64, 1))
    push[...] = -jnp.where(left[0:64, :], pltpu.roll(top, 64, 1), low)

    def step(i, carry):
        one, two = [], []
        for q in range(4):
            at = pl.ds(pl.multiple_of(i * 32 + q * 8, 8), 8)
            here, size = midx[at, :], push[at, :]
            pair = place(here & 127, here >> 7, [size * mnrm[c, at, :] for c in range(3)])
            one.append(pair[0])
            two.append(pair[1])
        acc[...] += lax.dot_general(
            jnp.concatenate(one, 1), jnp.concatenate(two, 1), NT, preferred_element_type=F32
        )
        return carry

    lax.fori_loop(0, 2, step, 0)
    one, two = [], []
    for r in (0, 8):
        here, at = slave[r : r + 8, :], slot[r : r + 8, :]
        (size,) = gather(mine, (0,), ((at >> 12) << 6) + (at & 63), (at >> 6) & 63, 64)
        pair = place(here & 127, here >> 7, [size * nrm[16 * c + r : 16 * c + r + 8, :] for c in range(3)])
        one.append(pair[0])
        two.append(pair[1])
    acc[...] += lax.dot_general(
        jnp.concatenate(one, 1), jnp.concatenate(two, 1), NT, preferred_element_type=F32
    )
    contact[...] = acc[0:96, :] + acc[96:192, :]
    tot[...] = net[...] + contact[...]

    def vals(r):
        p = [x[c * ROWS + r : c * ROWS + r + 8, :] for c in range(3)]
        n = [tot[c * ROWS + r : c * ROWS + r + 8, :] for c in range(3)]
        return [
            *n,
            p[1] * n[2] - p[2] * n[1],
            p[2] * n[0] - p[0] * n[2],
            p[0] * n[1] - p[1] * n[0],
        ]

    part_sums(part, vals, acc2, False)
    acc2[0:48, :] = acc2[0:48, :] + acc2[48:96, :]
    lane = lax.broadcasted_iota(jnp.int32, (8, LANES), 1)
    last = jnp.zeros((8, LANES), F32)
    for k in range(6):
        piece = jnp.where(lane < 16, acc2[8 * k : 8 * k + 8, :], 0.0)
        last = last + (pltpu.roll(piece, 16 * k, 1) if k else piece)
    even = lax.axis_index("dom") & 1 == 0
    pairs = [(acc2[8 * k : 8 * k + 1, :], acc2[8 * k + 2 : 8 * k + 3, :]) for k in range(6)]
    pairs += [(acc2[8 * k + 1 : 8 * k + 2, :], acc2[8 * k + 25 : 8 * k + 26, :]) for k in range(3)]
    pairs += [(jnp.zeros((1, LANES), F32), last[3:4, :])]
    for k, (low, high) in enumerate(pairs):
        keep[k : k + 1, :] = jnp.where(even, low, high)
        give[k : k + 1, :] = jnp.where(even, high, low)
    keep[10:16, :] = jnp.zeros((6, LANES), F32)
    give[10:16, :] = jnp.zeros((6, LANES), F32)
    moments = jnp.broadcast_to(jnp.sum(got[:, 256:384], axis=0, keepdims=True), (8, LANES))
    moments = jnp.where(lane < 96, 0.0, pltpu.roll(moments, 96, 1))
    keep[9:10, :] = keep[9:10, :] + moments[0:1, :]


def nodal_kernel(v, contact, mass, nodal):
    for c in range(3):
        at = slice(c * ROWS, (c + 1) * ROWS)
        speed = v[at, :] + TIME_STEP * contact[at, :] / mass[...]
        for h in range(ROWS):
            nodal[c : c + 1, h * LANES : (h + 1) * LANES] = speed[h : h + 1, :]


def spread_kernel(keep, given, out):
    tile = keep[...] + given[...]
    for k in range(10):
        out[:, k * LANES : (k + 1) * LANES] = jnp.broadcast_to(tile[k : k + 1, :], (64, LANES))


def total_kernel(got, out):
    for k in range(10):
        out[k : k + 1, :] = jnp.sum(got[:, k * LANES : (k + 1) * LANES], axis=0, keepdims=True)
    out[10:16, :] = jnp.zeros((6, LANES), F32)
    out[16:80, :] = pltpu.roll(got[:, 9 * LANES : 10 * LANES], 32, 1)


def motion_kernel(mine, other, rigid, out):
    even = lax.axis_index("dom") & 1 == 0
    low = jnp.where(even, mine[...], other[...])
    high = jnp.where(even, other[...], mine[...])
    by = jnp.concatenate([low[16:80, :], high[16:80, :]], 0).T
    moments = [by[8 * k : 8 * k + 4, :] for k in range(4)]
    sums = []
    for k in range(6):
        second = low[6 + k : 7 + k, :] if k < 3 else high[3 + k : 4 + k, :]
        last = pltpu.roll(high[8:16, :], LANES - 16 * k, 1) if k else high[8:16, :]
        sums.append(jnp.concatenate([low[k : k + 1, :], second, high[k : k + 1, :], last[1:2, :]], 0))
    own = rigid[0:4, :]
    mass = own + moments[0]
    centre = [(own * rigid[8 + 8 * c : 12 + 8 * c, :] + moments[1 + c]) / mass for c in range(3)]
    force, turn = sums[0:3], sums[3:6]
    rows = [y / mass for y in force]
    for c in range(3):
        a, b = (c + 1) % 3, (c + 2) % 3
        moment = turn[c] - (centre[a] * force[b] - centre[b] * force[a])
        rows.append(moment / rigid[32 + 8 * c : 36 + 8 * c, :])
    for r, row in enumerate(rows):
        for h, n in spans():
            out[r : r + 1, h * LANES : h * LANES + n] = row[h : h + 1, 0:n]


def partner(block, apart):
    count = lax.axis_size("dom")
    return lax.ppermute(block, "dom", [(i, i ^ (1 << apart)) for i in range(count)])


def in_hbm(*arrays):
    return [pltpu.with_memory_space_constraint(x, pltpu.HBM) for x in arrays]


def later(value, than):
    return lax.optimization_barrier((value, than))[0]


def swap(block, groups=None):
    return lax.all_to_all(block, "dom", 0, 0, tiled=True, axis_index_groups=groups)


def per_device(
    rest_pos,
    displacement,
    velocity,
    ext_force,
    node_mass,
    body_accel,
    connectivity,
    elem_material,
    stiffness,
    shared_nodes,
    contact_slave,
    contact_owner,
    contact_master,
    contact_normal,
    part_of_node,
    part_mass,
    part_center,
    part_inertia,
):
    state = ((96, LANES), F32)
    table = ((LANES, 5 * LANES), F32)
    own = [((3, LANES), F32)] * NBR
    work = [
        pltpu.VMEM((96, LANES), F32),
        pltpu.VMEM((24 * TOGETHER, LANES), F32),
        pltpu.VMEM((192, LANES), F32),
    ]
    inputs = (
        stiffness,
        contact_owner.reshape(16, LANES),
        contact_master.reshape(16, LANES),
        contact_normal,
        displacement,
        velocity,
        connectivity,
        elem_material,
        shared_nodes.transpose(1, 0, 2),
        ext_force,
        node_mass.reshape(ROWS, LANES),
        body_accel,
        contact_slave.reshape(16, LANES),
    )
    rows, ints = ((ROWS, LANES), F32), jnp.int32
    whole, map_rows = pltpu.VMEM((3, 4096), F32), ((ROWS, LANES), ints)
    u, v, fm, mass, idx, cols, shared, internal, send, slave, slot, normal = call(
        first_kernel,
        [
            state,
            state,
            state,
            rows,
            ((8, 4096), ints),
            ((192, 24, LANES), F32),
            ((8, LANES), ints),
            state,
            table,
            ((16, LANES), ints),
            ((16, LANES), ints),
            ((3, 2048), F32),
        ],
        [HBM] * 13,
        "first_cycle",
        [
            whole,
            whole,
            whole,
            pltpu.VMEM((NBR, 1, LANES), ints),
            pltpu.VMEM((16, LANES), ints),
            pltpu.VMEM((16, LANES), ints),
            pltpu.VMEM((8, 24, 24), F32),
            pltpu.SMEM((ROWS,), ints),
            pltpu.SMEM((3,), F32),
            pltpu.VMEM((8, 4096), ints),
            *work,
            pltpu.VMEM((LANES, 2 * LANES), F32),
            pltpu.SemaphoreType.DMA((13,)),
        ],
    )(*in_hbm(*inputs))
    got = swap(send)
    trio = ((3, PARTS_SIZE), F32)
    pos, part, inv, nrm, light, rigid = call(
        fixed_kernel,
        [state, map_rows, map_rows, ((48, LANES), F32), ((8, LANES), F32), ((56, LANES), F32)],
        [HBM] * 5 + [VMEM] * 3,
        "fixed_data",
        [
            whole,
            pltpu.VMEM((1, PARTS_SIZE), F32),
            pltpu.VMEM(*trio),
            pltpu.VMEM(*trio),
            pltpu.VMEM((LANES, LANES), F32),
            pltpu.SemaphoreType.DMA((5,)),
        ],
    )(
        *in_hbm(
            rest_pos,
            part_of_node.reshape(ROWS, LANES),
            part_mass.reshape(1, PARTS_SIZE),
            part_center,
            part_inertia,
        ),
        normal,
        shared,
        mass,
    )
    recv = [got]
    for n in range(CYCLES - 1):
        u, v, internal, *mine = call(
            functools.partial(next_kernel, n == 0),
            [state, state, state, *own],
            [VMEM] * 7 + [SMEM] + [VMEM] * (2 + len(recv)),
            "next_cycle",
            work,
        )(u, v, internal, inv, fm, mass, idx, elem_material, cols, shared, *recv)
        recv = [partner(mine[b], b) for b in range(NBR)]
        if n == 0:
            midx, mnrm, code = call(
                ends_kernel,
                [((64, LANES), ints), ((3, 64, LANES), F32), ((80, LANES), ints)],
                [VMEM] * 3,
                "contact_ends",
            )(later(got, mine), slave, inv)
            recv, code = lax.optimization_barrier((recv, code))
    both = ((2, 80, LANES), F32)
    x, v, ab = call(
        base_kernel,
        [state, state, both],
        [VMEM] * 10,
        "contact_base",
        [pltpu.VMEM((192, LANES), F32)],
    )(u, v, internal, fm, mass, pos, slave, nrm, midx, mnrm)
    x, v, net, dots = call(
        dots_kernel,
        [state, state, state, ((LANES, 3 * LANES), F32)],
        [VMEM] * 18,
        "contact_dots",
        [pltpu.VMEM((64, LANES), F32), pltpu.VMEM((LANES, LANES), F32), pltpu.VMEM(*both)],
    )(x, v, ab, internal, inv, light, fm, mass, part, slot, nrm, mnrm, code, *recv)
    half = ((16, LANES), F32)
    contact, keep, give = call(
        contact_kernel,
        [state, half, half],
        [VMEM] * 10,
        "contact_forces",
        [
            pltpu.VMEM((192, LANES), F32),
            pltpu.VMEM((96, LANES), F32),
            pltpu.VMEM((96, LANES), F32),
            pltpu.VMEM((64, LANES), F32),
            pltpu.VMEM((64, LANES), F32),
        ],
    )(dots, swap(dots), slave, slot, nrm, midx, mnrm, x, net, part)
    (nodal_velocity,) = call(nodal_kernel, [((3, 4096), F32)], [VMEM] * 3, "nodal_velocity")(v, contact, mass)
    (spread,) = call(spread_kernel, [((64, 10 * LANES), F32)], [VMEM] * 2, "part_spread")(keep, partner(give, 0))
    chips = lax.axis_size("dom") // 2
    groups = [[2 * i + core for i in range(chips)] for core in range(2)]
    (total,) = call(total_kernel, [((80, LANES), F32)], [VMEM], "part_totals")(swap(spread, groups))
    (motion,) = call(motion_kernel, [((6, PARTS_SIZE), F32)], [VMEM] * 3, "part_motion")(
        total, partner(total, 0), rigid
    )
    return nodal_velocity, motion


def solution(mesh):
    placed = (
        P(None, "dom"),
        P(None, "dom"),
        P(None, "dom"),
        P(None, "dom"),
        P("dom"),
        P(),
        P(None, "dom"),
        P("dom"),
        P(),
        P("dom", None, None),
        P("dom"),
        P("dom", None),
        P("dom"),
        P(None, "dom"),
        P("dom"),
        P(),
        P(),
        P(),
    )
    return jax.shard_map(
        per_device, mesh=mesh, in_specs=placed, out_specs=(P(None, "dom"), P()), check_vma=False
    )
```

```python
import functools

import jax
import jax.numpy as jnp
from jax import lax
from jax.experimental import pallas as pl
from jax.experimental.pallas import tpu as pltpu
from jax.sharding import PartitionSpec as P

CYCLES = 3
PARTS_SIZE = 400

TIME_STEP = 0.1
DAMP_RATIO = 0.05
PENALTY = 2.0
GAP_WIDTH = 0.5
CONTACT_DAMP = 0.2

BF = jnp.bfloat16
F32 = jnp.float32
NT = (((1,), (1,)), ((), ()))
LANES = 128
ROWS = 32
NBR = 5
TOGETHER = 4

VMEM = pl.BlockSpec(memory_space=pltpu.VMEM)
SMEM = pl.BlockSpec(memory_space=pltpu.SMEM)
HBM = pl.BlockSpec(memory_space=pltpu.HBM)


def call(body, outs, in_specs, name, scratch=(), flops=0, last=()):
    return pl.pallas_call(
        body,
        out_shape=[jax.ShapeDtypeStruct(s, d) for s, d in outs],
        in_specs=in_specs,
        out_specs=[VMEM] * (len(outs) - len(last)) + list(last),
        scratch_shapes=list(scratch),
        compiler_params=pltpu.CompilerParams(vmem_limit_bytes=40 << 20),
        cost_estimate=pl.CostEstimate(flops=flops, bytes_accessed=1 << 20, transcendentals=0),
        name=name,
    )


def lanes_of(row, idx):
    return jnp.take_along_axis(row, idx, axis=1, mode="promise_in_bounds")


def gather(tab, bases, lo, hi, rows=ROWS):
    acc = [None] * len(bases)
    for h in range(rows):
        here = hi == h
        for c, base in enumerate(bases):
            row = jnp.broadcast_to(tab[base + h : base + h + 1, :], (8, LANES))
            val = lanes_of(row, lo)
            acc[c] = val if h == 0 else jnp.where(here, val, acc[c])
    return acc


def halves(x):
    first = x.astype(BF)
    return first, (x - first.astype(F32)).astype(BF)


def wide(x, a, n):
    row = jnp.broadcast_to(x[a : a + 1, :].astype(F32), (16, LANES)).astype(BF)
    return jnp.concatenate([row] * (n // 16), 0)


def iota_rows(n):
    return lax.broadcasted_iota(jnp.int32, (n, LANES), 0).astype(F32).astype(BF)


def place(lo, hi, vals):
    lof, hif = lo.astype(F32), hi.astype(F32)
    it = iota_rows(LANES)
    split = [halves(v) for v in vals]
    one, zero = jnp.ones((LANES, LANES), BF), jnp.zeros((LANES, LANES), BF)
    left, right = [], []
    for a in range(8):
        right.append(jnp.where(wide(lof, a, LANES) == it, one, zero))
        mask = wide(hif, a, ROWS) == it[:ROWS]
        left.append(
            jnp.concatenate(
                [
                    jnp.where(mask, wide(split[c][s], a, ROWS), zero[:ROWS])
                    for s in range(2)
                    for c in range(len(vals))
                ],
                0,
            )
        )
    return jnp.concatenate(left, 1), jnp.concatenate(right, 1)


def add_placed(acc, lo, hi, vals):
    left, right = place(lo, hi, vals)
    acc[...] += lax.dot_general(left, right, NT, preferred_element_type=F32)


def to_rows(src, dst):
    for c in range(3):
        for h in range(ROWS):
            dst[c * ROWS + h : c * ROWS + h + 1, :] = src[c : c + 1, h * LANES : (h + 1) * LANES]


def elements(idx, mat, tab, cols, g, acc):
    acc[...] = jnp.zeros_like(acc)
    steps = ROWS // TOGETHER

    def corners(i, q):
        here = idx[:, pl.ds(pl.multiple_of((i * TOGETHER + q) * LANES, LANES), LANES)]
        return here & 127, here >> 7

    def fetch(i):
        vals = []
        for q in range(TOGETHER):
            vals += gather(tab, (0, ROWS, 2 * ROWS), *corners(i, q))
        return tuple(vals)

    def step(i, vals):
        upcoming = fetch((i + 1) & (steps - 1))
        left, right = [], []
        for q in range(TOGETHER):
            for c in range(3):
                g[q * 24 + 8 * c : q * 24 + 8 * c + 8, :] = vals[q * 3 + c]
            first = mat[i * TOGETHER + q] * 24
            force = [jnp.zeros((8, LANES), F32)] * 3
            for j in range(24):
                col = cols.at[first + j]
                row = jnp.broadcast_to(g[q * 24 + j : q * 24 + j + 1, :], (8, LANES))
                force = [force[c] + col[8 * c : 8 * c + 8, :] * row for c in range(3)]
            one, two = place(*corners(i, q), force)
            left.append(one)
            right.append(two)
        acc[...] += lax.dot_general(
            jnp.concatenate(left, 1), jnp.concatenate(right, 1), NT, preferred_element_type=F32
        )
        return upcoming

    lax.fori_loop(0, steps, step, fetch(0))


def finish_internal(acc, internal, shared):
    internal[...] = acc[0:96, :] + acc[96:192, :]
    return gather(internal, (0, ROWS, 2 * ROWS), shared[...] & 127, shared[...] >> 7)


def slotted(hitb, rank, vals):
    rows = lax.broadcasted_iota(jnp.int32, (64, LANES), 0).astype(F32)
    mine = jnp.broadcast_to(rank, (64, LANES)) == rows
    left = [jnp.broadcast_to(x, (64, LANES)) for x in vals]
    pieces = []
    for s in range(3):
        pieces.append(jnp.concatenate([jnp.where(mine, x, 0.0).astype(BF) for x in left], 0))
        left = [x - x.astype(BF).astype(F32) for x in left]
    return [hitb] * 3, pieces


def hits_of(owner_row):
    down = lax.broadcasted_iota(jnp.int32, (LANES, LANES), 0)
    return jnp.where(jnp.broadcast_to(owner_row, (LANES, LANES)) == down, 1.0, 0.0)


def slots(owner, master, normal, slot, acc, between):
    acc[...] = jnp.zeros_like(acc)
    down = lax.broadcasted_iota(jnp.int32, (LANES, LANES), 0)
    across = lax.broadcasted_iota(jnp.int32, (LANES, LANES), 1)
    before = jnp.where(down < across, 1.0, 0.0).astype(BF)
    hits = [hits_of(owner[t : t + 1, :]) for t in range(16)]
    counts = jnp.dot(jnp.concatenate([hit.astype(BF) for hit in hits], 0), before, preferred_element_type=F32)
    carry = jnp.zeros((LANES, 1), F32)
    for t, hit in enumerate(hits):
        count = counts[t * LANES : (t + 1) * LANES, :] + carry
        rank = jnp.sum(hit * count, axis=0, keepdims=True)
        carry = carry + jnp.sum(hit, axis=1, keepdims=True)
        slot[t : t + 1, :] = owner[t : t + 1, :] * 64 + rank.astype(jnp.int32)
    for four in range(4):
        hits, pieces = [], []
        for t in range(4 * four, 4 * four + 4):
            vals = [normal[c : c + 1, t * LANES : (t + 1) * LANES] for c in range(3)]
            rank = (slot[t : t + 1, :] & 63).astype(F32)
            one, two = slotted(
                hits_of(owner[t : t + 1, :]).astype(BF), rank, [*vals, master[t : t + 1, :].astype(F32)]
            )
            hits += one
            pieces += two
        between(2 * four)
        between(2 * four + 1)
        acc[...] += lax.dot_general(
            jnp.concatenate(hits, 1), jnp.concatenate(pieces, 1), NT, preferred_element_type=F32
        )


def spans():
    return [(h, min(LANES, PARTS_SIZE - h * LANES)) for h in range(4)]


def every(first, stride, count=LANES):
    return pl.ds(first, count, stride=stride)


def copy_all(srcs, dsts, sems):
    copies = [pltpu.make_async_copy(a, b, sems.at[i]) for i, (a, b) in enumerate(zip(srcs, dsts))]
    for copy in copies:
        copy.start()
    return copies


def first_kernel(*refs):
    srcs = refs[:13]
    u, v, fm, mass, idx, inv, cols, shared, internal, send, slave, slot, normal, mat = refs[13:27]
    disp0, vel0, force0, shared0, owner, master, stiff, accel, conn, tab, g, acc, small, table, sems = refs[27:]
    dsts = (stiff, owner, master, normal, disp0, vel0, conn, mat, shared0, force0, mass, accel, slave)
    copies = copy_all(srcs, dsts, sems)

    def columns(m):
        for j in range(24):
            cols[m * 24 + j] = jnp.broadcast_to(stiff[m, :, j : j + 1], (24, LANES))

    for copy in copies[:4]:
        copy.wait()
    slots(owner, master, normal, slot, table, columns)
    send[...] = jnp.zeros_like(send)
    send[every(0, 5), :] = table[:, 0:128]
    send[every(1, 5), :] = table[:, 128:256]
    for copy in copies[4:]:
        copy.wait()
    to_rows(disp0, u)
    to_rows(vel0, v)
    to_rows(force0, fm)
    tab[...] = u[...] + DAMP_RATIO * v[...]
    for c in range(3):
        at = slice(c * ROWS, (c + 1) * ROWS)
        fm[at, :] = fm[at, :] / mass[...] - accel[c]
    lane = lax.broadcasted_iota(jnp.int32, (8, LANES), 1)
    for b in range(ROWS):
        at = slice(b * LANES, (b + 1) * LANES)
        idx[:, at] = (conn[:, at] + lane + b * LANES) & 4095
    shared[...] = jnp.zeros_like(shared)
    for b in range(NBR):
        shared[b : b + 1, :] = shared0[b]
    small[...] = jnp.zeros_like(small)
    row = lax.broadcasted_iota(jnp.int32, (8, LANES), 0)
    held = row < NBR
    lo, hi = shared[...] & 127, shared[...] >> 7
    kept = [jnp.where(held, lane, 0).astype(F32), jnp.where(held, row + 1, 0).astype(F32)]
    add_placed(small, lo, hi, kept)
    found = (small[0:64, :] + small[64:128, :]).astype(jnp.int32)
    inv[...] = found[0:ROWS, :] + found[ROWS : 2 * ROWS, :] * LANES
    elements(idx, mat, tab, cols, g, acc)
    own = finish_internal(acc, internal, shared)
    me = lax.axis_index("dom")
    for b in range(NBR):
        for c in range(3):
            send[pl.ds(5 * (me ^ (1 << b)) + 2 + c, 1), :] = own[c][b : b + 1, :]


def fixed_kernel(*refs):
    pos0, part0, pmass0, pcenter0, pinertia0, normal, shared, mass, pos, part, nrm, light, rigid = refs[:13]
    pos1, pmass, pcenter, pinertia, sems = refs[13:]
    copies = copy_all(
        (pos0, part0, pmass0, pcenter0, pinertia0), (pos1, part, pmass, pcenter, pinertia), sems
    )
    (weight,) = gather(mass, (0,), shared[...] & 127, shared[...] >> 7)
    light[...] = -TIME_STEP / weight
    for t in range(16):
        for c in range(3):
            nrm[16 * c + t : 16 * c + t + 1, :] = normal[c : c + 1, t * LANES : (t + 1) * LANES]
    rigid[...] = jnp.ones_like(rigid)
    for copy in copies:
        copy.wait()
    to_rows(pos1, pos)
    for h, n in spans():
        at = slice(h * LANES, h * LANES + n)
        rigid[h : h + 1, 0:n] = pmass[0:1, at]
        for c in range(3):
            rigid[8 + 8 * c + h : 9 + 8 * c + h, 0:n] = pcenter[c : c + 1, at]
            rigid[32 + 8 * c + h : 33 + 8 * c + h, 0:n] = pinertia[c : c + 1, at]


def from_shared(code, rows):
    total = 0.0
    for b in range(NBR):
        row = jnp.broadcast_to(rows[b], (8, LANES))
        total = total + jnp.where(code >> 7 == b + 1, lanes_of(row, code & 127), 0.0)
    return total


def update(u, v, internal, inv, fm, mass, recv, c, r):
    at = slice(c * ROWS + r, c * ROWS + r + 8)
    total = internal[at, :] + from_shared(inv[r : r + 8, :], [recv[b][c] for b in range(NBR)])
    speed = v[at, :] + TIME_STEP * (fm[at, :] - total / mass[r : r + 8, :])
    return at, u[at, :] + TIME_STEP * speed, speed, total


def rows_of(refs):
    return [[ref[c : c + 1, :] for c in range(3)] for ref in refs]


def next_kernel(from_table, u, v, internal, inv, fm, mass, idx, mat, cols, shared, *rest):
    if from_table:
        got, rest = rest[0], rest[1:]
        me = lax.axis_index("dom")
        recv = [[got[pl.ds(5 * (me ^ (1 << b)) + 2 + c, 1), :] for c in range(3)] for b in range(NBR)]
    else:
        recv, rest = rows_of(rest[:NBR]), rest[NBR:]
    u2, v2, internal2 = rest[:3]
    own = rest[3:8]
    tab, g, acc = rest[8:]
    for c in range(3):
        for r in range(0, ROWS, 8):
            at, disp, speed, _ = update(u, v, internal, inv, fm, mass, recv, c, r)
            u2[at, :] = disp
            v2[at, :] = speed
            tab[at, :] = disp + DAMP_RATIO * speed
    elements(idx, mat, tab, cols, g, acc)
    vals = finish_internal(acc, internal2, shared)
    for b in range(NBR):
        for c in range(3):
            own[b][c : c + 1, :] = vals[c][b : b + 1, :]


def ends_kernel(got, slave, inv, midx, mnrm, code):
    left = lax.broadcasted_iota(jnp.int32, (64, LANES), 1) < 64
    for k, out in ((0, mnrm.at[0]), (1, mnrm.at[1]), (2, mnrm.at[2]), (3, midx)):
        top, low = got[every(k // 2, 5, 64), :], got[every(320 + k // 2, 5, 64), :]
        if k % 2:
            out[...] = jnp.where(left, pltpu.roll(top, 64, 1), low).astype(out.dtype)
        else:
            out[...] = jnp.where(left, top, pltpu.roll(low, 64, 1))
    for r in range(0, 80, 8):
        here = slave[r : r + 8, :] if r < 16 else midx[r - 16 : r - 8, :]
        (code[r : r + 8, :],) = gather(inv, (0,), here & 127, here >> 7)


def base_kernel(u, v, internal, fm, mass, pos, slave, nrm, midx, mnrm, x2, v2, ab, tab):
    for c in range(3):
        for r in range(0, ROWS, 8):
            at = slice(c * ROWS + r, c * ROWS + r + 8)
            speed = v[at, :] + TIME_STEP * (fm[at, :] - internal[at, :] / mass[r : r + 8, :])
            place_now = pos[at, :] + (u[at, :] + TIME_STEP * speed)
            x2[at, :] = place_now
            v2[at, :] = speed
            tab[at, :] = place_now
            tab[c * ROWS + 96 + r : c * ROWS + 96 + r + 8, :] = speed

    def both(here, w):
        y = gather(tab, tuple(range(0, 192, ROWS)), here & 127, here >> 7)
        return y[0] * w[0] + y[1] * w[1] + y[2] * w[2], y[3] * w[0] + y[4] * w[1] + y[5] * w[2]

    for r in (0, 8):
        w = [nrm[16 * c + r : 16 * c + r + 8, :] for c in range(3)]
        ab[0, r : r + 8, :], ab[1, r : r + 8, :] = both(slave[r : r + 8, :], w)

    def step(i, carry):
        for q in range(2):
            at = pl.ds(pl.multiple_of(i * 16 + q * 8, 8), 8)
            to = pl.ds(pl.multiple_of(i * 16 + q * 8 + 16, 8), 8)
            ab[0, to, :], ab[1, to, :] = both(midx[at, :], [mnrm[c, at, :] for c in range(3)])
        return carry

    lax.fori_loop(0, 4, step, 0)


def dots_kernel(x1, v1, ab1, internal, inv, light, fm, mass, part, slot, nrm, mnrm, code, *rest):
    recv = rows_of(rest[:5])
    x2, v2, net, dots, acc, table, ab = rest[5:]
    for c in range(3):
        for r in range(0, ROWS, 8):
            at = slice(c * ROWS + r, c * ROWS + r + 8)
            m = mass[r : r + 8, :]
            more = from_shared(inv[r : r + 8, :], [recv[b][c] for b in range(NBR)])
            change = -TIME_STEP * (more / m)
            x2[at, :] = x1[at, :] + TIME_STEP * change
            v2[at, :] = v1[at, :] + change
            net[at, :] = m * fm[at, :] - internal[at, :] - more
    moved = [[recv[b][c] * light[b : b + 1, :] for b in range(NBR)] for c in range(3)]
    for r in range(0, 80, 8):
        here = code[r : r + 8, :]
        if r < 16:
            w = [nrm[16 * c + r : 16 * c + r + 8, :] for c in range(3)]
        else:
            w = [mnrm[c, r - 16 : r - 8, :] for c in range(3)]
        d = [from_shared(here, moved[c]) for c in range(3)]
        change = d[0] * w[0] + d[1] * w[1] + d[2] * w[2]
        ab[0, r : r + 8, :] = ab1[0, r : r + 8, :] + TIME_STEP * change
        ab[1, r : r + 8, :] = ab1[1, r : r + 8, :] + change

    def vals(r):
        m = mass[r : r + 8, :]
        return [m, *[m * x2[c * ROWS + r : c * ROWS + r + 8, :] for c in range(3)]]

    acc[...] = jnp.zeros_like(acc)
    part_sums(part, vals, acc, True)
    moments = jnp.concatenate([acc[0:32, :] + acc[32:64, :], jnp.zeros((96, LANES), F32)], 0)
    dots[every(2, 3), :] = moments.T
    table[...] = jnp.zeros_like(table)
    for i in range(4):
        hits, pieces = [], []
        for t in range(4 * i, 4 * i + 4):
            here = slot[t : t + 1, :]
            rows = [ab[0, t : t + 1, :], ab[1, t : t + 1, :]]
            one, two = slotted(hits_of(here >> 6).astype(BF), (here & 63).astype(F32), rows)
            hits += one
            pieces += two
        table[...] += lax.dot_general(
            jnp.concatenate(hits, 1), jnp.concatenate(pieces, 1), NT, preferred_element_type=F32
        )
    left = lax.broadcasted_iota(jnp.int32, (64, LANES), 1) < 64
    one, two = ab[0, 16:80, :], ab[1, 16:80, :]
    dots[every(0, 3), :] = table[...]
    dots[every(1, 3, 64), :] = jnp.where(left, one, pltpu.roll(two, 64, 1))
    dots[every(193, 3, 64), :] = jnp.where(left, pltpu.roll(one, 64, 1), two)


def part_sums(part, vals, acc, by_device):
    it = iota_rows(LANES)
    it8 = (lax.broadcasted_iota(jnp.int32, (16, LANES), 0) & 7).astype(F32).astype(BF)
    one, zero = jnp.ones((LANES, LANES), BF), jnp.zeros((LANES, LANES), BF)
    for r in range(0, ROWS, 8):
        here = part[r : r + 8, :]
        lo = here & 127
        if by_device:
            lo = ((lo & 63) << 1) | (lo >> 6)
        lof, hif = lo.astype(F32), (here >> 7).astype(F32)
        val = vals(r)
        first = [x.astype(BF).astype(F32) for x in val]
        split = (first, [x - y for x, y in zip(val, first)])
        left, right = [], []
        for a in range(8):
            right.append(jnp.where(wide(lof, a, LANES) == it, one, zero))
            mask = wide(hif, a, 16) == it8
            rows = []
            for s in range(2):
                for k in range(0, len(val), 2):
                    two = [jnp.broadcast_to(split[s][k + d][a : a + 1, :], (8, LANES)) for d in range(2)]
                    rows.append(jnp.where(mask, jnp.concatenate(two, 0).astype(BF), zero[:16]))
            left.append(jnp.concatenate(rows, 0))
        acc[...] += lax.dot_general(
            jnp.concatenate(left, 1), jnp.concatenate(right, 1), NT, preferred_element_type=F32
        )


def contact_kernel(
    dots, got, slave, slot, nrm, midx, mnrm, x, net, part, contact, keep, give, acc, tot, acc2, push, mine
):
    acc[...] = jnp.zeros_like(acc)
    acc2[...] = jnp.zeros_like(acc2)
    left = lax.broadcasted_iota(jnp.int32, (LANES, LANES), 1) < 64
    as_slave = dots[every(0, 3), :] - got[every(1, 3), :]
    as_master = got[every(0, 3), :] - dots[every(1, 3), :]
    gap = jnp.where(left, as_slave, pltpu.roll(as_master, 64, 1))
    closing = jnp.where(left, pltpu.roll(as_slave, 64, 1), as_master)
    z = -gap / GAP_WIDTH
    soft = jnp.maximum(z, 0.0) + jnp.log1p(jnp.exp(-jnp.abs(z)))
    size = PENALTY * GAP_WIDTH * soft - CONTACT_DAMP * closing
    top, low = size[0:64, :], size[64:128, :]
    mine[...] = jnp.where(left[0:64, :], top, pltpu.roll(low, 64, 1))
    push[...] = -jnp.where(left[0:64, :], pltpu.roll(top, 64, 1), low)

    def step(i, carry):
        one, two = [], []
        for q in range(4):
            at = pl.ds(pl.multiple_of(i * 32 + q * 8, 8), 8)
            here, size = midx[at, :], push[at, :]
            pair = place(here & 127, here >> 7, [size * mnrm[c, at, :] for c in range(3)])
            one.append(pair[0])
            two.append(pair[1])
        acc[...] += lax.dot_general(
            jnp.concatenate(one, 1), jnp.concatenate(two, 1), NT, preferred_element_type=F32
        )
        return carry

    lax.fori_loop(0, 2, step, 0)
    one, two = [], []
    for r in (0, 8):
        here, at = slave[r : r + 8, :], slot[r : r + 8, :]
        (size,) = gather(mine, (0,), ((at >> 12) << 6) + (at & 63), (at >> 6) & 63, 64)
        pair = place(here & 127, here >> 7, [size * nrm[16 * c + r : 16 * c + r + 8, :] for c in range(3)])
        one.append(pair[0])
        two.append(pair[1])
    acc[...] += lax.dot_general(
        jnp.concatenate(one, 1), jnp.concatenate(two, 1), NT, preferred_element_type=F32
    )
    contact[...] = acc[0:96, :] + acc[96:192, :]
    tot[...] = net[...] + contact[...]

    def vals(r):
        p = [x[c * ROWS + r : c * ROWS + r + 8, :] for c in range(3)]
        n = [tot[c * ROWS + r : c * ROWS + r + 8, :] for c in range(3)]
        return [
            *n,
            p[1] * n[2] - p[2] * n[1],
            p[2] * n[0] - p[0] * n[2],
            p[0] * n[1] - p[1] * n[0],
        ]

    part_sums(part, vals, acc2, False)
    acc2[0:48, :] = acc2[0:48, :] + acc2[48:96, :]
    lane = lax.broadcasted_iota(jnp.int32, (8, LANES), 1)
    last = jnp.zeros((8, LANES), F32)
    for k in range(6):
        piece = jnp.where(lane < 16, acc2[8 * k : 8 * k + 8, :], 0.0)
        last = last + (pltpu.roll(piece, 16 * k, 1) if k else piece)
    even = lax.axis_index("dom") & 1 == 0
    pairs = [(acc2[8 * k : 8 * k + 1, :], acc2[8 * k + 2 : 8 * k + 3, :]) for k in range(6)]
    pairs += [(acc2[8 * k + 1 : 8 * k + 2, :], acc2[8 * k + 25 : 8 * k + 26, :]) for k in range(3)]
    pairs += [(jnp.zeros((1, LANES), F32), last[3:4, :])]
    for k, (low, high) in enumerate(pairs):
        keep[k : k + 1, :] = jnp.where(even, low, high)
        give[k : k + 1, :] = jnp.where(even, high, low)
    keep[10:16, :] = jnp.zeros((6, LANES), F32)
    give[10:16, :] = jnp.zeros((6, LANES), F32)
    moments = jnp.broadcast_to(jnp.sum(got[every(2, 3), :], axis=0, keepdims=True), (8, LANES))
    moments = jnp.where(lane < 96, 0.0, pltpu.roll(moments, 96, 1))
    keep[9:10, :] = keep[9:10, :] + moments[0:1, :]


def nodal_kernel(v, contact, mass, nodal):
    for c in range(3):
        at = slice(c * ROWS, (c + 1) * ROWS)
        speed = v[at, :] + TIME_STEP * contact[at, :] / mass[...]
        for h in range(ROWS):
            nodal[c : c + 1, h * LANES : (h + 1) * LANES] = speed[h : h + 1, :]


def spread_kernel(keep, given, out):
    tile = (keep[...] + given[...])[0:10, :]
    four = jnp.concatenate([tile] * 4, 0)
    for k in range(16):
        out[40 * k : 40 * k + 40, :] = four


def total_kernel(got, out):
    four = got[0:40, :]
    for k in range(1, 16):
        four = four + got[40 * k : 40 * k + 40, :]
    out[0:10, :] = four[0:10, :] + four[10:20, :] + four[20:30, :] + four[30:40, :]
    out[10:16, :] = jnp.zeros((6, LANES), F32)
    out[16:80, :] = pltpu.roll(got[every(9, 10, 64), :], 32, 1)


def motion_kernel(mine, other, rigid, out):
    even = lax.axis_index("dom") & 1 == 0
    low = jnp.where(even, mine[...], other[...])
    high = jnp.where(even, other[...], mine[...])
    by = jnp.concatenate([low[16:80, :], high[16:80, :]], 0).T
    moments = [by[8 * k : 8 * k + 4, :] for k in range(4)]
    sums = []
    for k in range(6):
        second = low[6 + k : 7 + k, :] if k < 3 else high[3 + k : 4 + k, :]
        last = pltpu.roll(high[8:16, :], LANES - 16 * k, 1) if k else high[8:16, :]
        sums.append(jnp.concatenate([low[k : k + 1, :], second, high[k : k + 1, :], last[1:2, :]], 0))
    own = rigid[0:4, :]
    mass = own + moments[0]
    centre = [(own * rigid[8 + 8 * c : 12 + 8 * c, :] + moments[1 + c]) / mass for c in range(3)]
    force, turn = sums[0:3], sums[3:6]
    rows = [y / mass for y in force]
    for c in range(3):
        a, b = (c + 1) % 3, (c + 2) % 3
        moment = turn[c] - (centre[a] * force[b] - centre[b] * force[a])
        rows.append(moment / rigid[32 + 8 * c : 36 + 8 * c, :])
    for r, row in enumerate(rows):
        for h, n in spans():
            out[r : r + 1, h * LANES : h * LANES + n] = row[h : h + 1, 0:n]


def partner(block, apart):
    count = lax.axis_size("dom")
    return lax.ppermute(block, "dom", [(i, i ^ (1 << apart)) for i in range(count)])


def in_hbm(*arrays):
    return [pltpu.with_memory_space_constraint(x, pltpu.HBM) for x in arrays]


def later(value, than):
    return lax.optimization_barrier((value, than))[0]


def swap(block, groups=None):
    peers = len(groups[0]) if groups else lax.axis_size("dom")
    flat = block.reshape(peers, 1, -1)
    return lax.all_to_all(flat, "dom", 0, 0, tiled=True, axis_index_groups=groups).reshape(block.shape)


def per_device(
    rest_pos,
    displacement,
    velocity,
    ext_force,
    node_mass,
    body_accel,
    connectivity,
    elem_material,
    stiffness,
    shared_nodes,
    contact_slave,
    contact_owner,
    contact_master,
    contact_normal,
    part_of_node,
    part_mass,
    part_center,
    part_inertia,
):
    state = ((96, LANES), F32)
    table = ((5 * LANES, LANES), F32)
    own = [((3, LANES), F32)] * NBR
    work = [
        pltpu.VMEM((96, LANES), F32),
        pltpu.VMEM((24 * TOGETHER, LANES), F32),
        pltpu.VMEM((192, LANES), F32),
    ]
    inputs = (
        stiffness,
        contact_owner.reshape(16, LANES),
        contact_master.reshape(16, LANES),
        contact_normal,
        displacement,
        velocity,
        connectivity,
        elem_material,
        shared_nodes.transpose(1, 0, 2),
        ext_force,
        node_mass.reshape(ROWS, LANES),
        body_accel,
        contact_slave.reshape(16, LANES),
    )
    rows, ints = ((ROWS, LANES), F32), jnp.int32
    whole, map_rows = pltpu.VMEM((3, 4096), F32), ((ROWS, LANES), ints)
    u, v, fm, mass, idx, inv, cols, shared, internal, send, slave, slot, normal, mat = call(
        first_kernel,
        [
            state,
            state,
            state,
            rows,
            ((8, 4096), ints),
            map_rows,
            ((192, 24, LANES), F32),
            ((8, LANES), ints),
            state,
            table,
            ((16, LANES), ints),
            ((16, LANES), ints),
            ((3, 2048), F32),
            ((ROWS,), ints),
        ],
        [HBM] * 13,
        "first_cycle",
        [
            whole,
            whole,
            whole,
            pltpu.VMEM((NBR, 1, LANES), ints),
            pltpu.VMEM((16, LANES), ints),
            pltpu.VMEM((16, LANES), ints),
            pltpu.VMEM((8, 24, 24), F32),
            pltpu.SMEM((3,), F32),
            pltpu.VMEM((8, 4096), ints),
            *work,
            pltpu.VMEM((LANES, LANES), F32),
            pltpu.VMEM((LANES, 2 * LANES), F32),
            pltpu.SemaphoreType.DMA((13,)),
        ],
        last=[SMEM],
    )(*in_hbm(*inputs))
    got = swap(send)
    trio = ((3, PARTS_SIZE), F32)
    recv = [got]
    for n in range(CYCLES - 1):
        u, v, internal, *mine = call(
            functools.partial(next_kernel, n == 0),
            [state, state, state, *own],
            [VMEM] * 7 + [SMEM] + [VMEM] * (2 + len(recv)),
            "next_cycle",
            work,
        )(u, v, internal, inv, fm, mass, idx, mat, cols, shared, *recv)
        recv = [partner(mine[b], b) for b in range(NBR)]
        if n == 0:
            midx, mnrm, code = call(
                ends_kernel,
                [((64, LANES), ints), ((3, 64, LANES), F32), ((80, LANES), ints)],
                [VMEM] * 3,
                "contact_ends",
            )(later(got, mine), slave, inv)
            pos, part, nrm, light, rigid = call(
                fixed_kernel,
                [state, map_rows, ((48, LANES), F32), ((8, LANES), F32), ((56, LANES), F32)],
                [HBM] * 5 + [VMEM] * 3,
                "fixed_data",
                [
                    whole,
                    pltpu.VMEM((1, PARTS_SIZE), F32),
                    pltpu.VMEM(*trio),
                    pltpu.VMEM(*trio),
                    pltpu.SemaphoreType.DMA((5,)),
                ],
            )(
                *in_hbm(
                    rest_pos,
                    part_of_node.reshape(ROWS, LANES),
                    part_mass.reshape(1, PARTS_SIZE),
                    part_center,
                    part_inertia,
                ),
                later(normal, mine),
                shared,
                mass,
            )
            recv, code, nrm = lax.optimization_barrier((recv, code, nrm))
    both = ((2, 80, LANES), F32)
    x, v, ab = call(
        base_kernel,
        [state, state, both],
        [VMEM] * 10,
        "contact_base",
        [pltpu.VMEM((192, LANES), F32)],
    )(u, v, internal, fm, mass, pos, slave, nrm, midx, mnrm)
    x, v, net, dots = call(
        dots_kernel,
        [state, state, state, ((3 * LANES, LANES), F32)],
        [VMEM] * 18,
        "contact_dots",
        [pltpu.VMEM((64, LANES), F32), pltpu.VMEM((LANES, LANES), F32), pltpu.VMEM(*both)],
    )(x, v, ab, internal, inv, light, fm, mass, part, slot, nrm, mnrm, code, *recv)
    half = ((16, LANES), F32)
    contact, keep, give = call(
        contact_kernel,
        [state, half, half],
        [VMEM] * 10,
        "contact_forces",
        [
            pltpu.VMEM((192, LANES), F32),
            pltpu.VMEM((96, LANES), F32),
            pltpu.VMEM((96, LANES), F32),
            pltpu.VMEM((64, LANES), F32),
            pltpu.VMEM((64, LANES), F32),
        ],
    )(dots, swap(dots), slave, slot, nrm, midx, mnrm, x, net, part)
    (nodal_velocity,) = call(nodal_kernel, [((3, 4096), F32)], [VMEM] * 3, "nodal_velocity")(v, contact, mass)
    (spread,) = call(spread_kernel, [((640, LANES), F32)], [VMEM] * 2, "part_spread")(keep, partner(give, 0))
    chips = lax.axis_size("dom") // 2
    groups = [[2 * i + core for i in range(chips)] for core in range(2)]
    (total,) = call(total_kernel, [((80, LANES), F32)], [VMEM], "part_totals")(swap(spread, groups))
    (motion,) = call(motion_kernel, [((6, PARTS_SIZE), F32)], [VMEM] * 3, "part_motion")(
        total, partner(total, 0), rigid
    )
    return nodal_velocity, motion


def solution(mesh):
    placed = (
        P(None, "dom"),
        P(None, "dom"),
        P(None, "dom"),
        P(None, "dom"),
        P("dom"),
        P(),
        P(None, "dom"),
        P("dom"),
        P(),
        P("dom", None, None),
        P("dom"),
        P("dom", None),
        P("dom"),
        P(None, "dom"),
        P("dom"),
        P(),
        P(),
        P(),
    )
    return jax.shard_map(
        per_device, mesh=mesh, in_specs=placed, out_specs=(P(None, "dom"), P()), check_vma=False
    )
```

```python
import functools

import jax
import jax.numpy as jnp
from jax import lax
from jax.experimental import pallas as pl
from jax.experimental.pallas import tpu as pltpu
from jax.sharding import PartitionSpec as P

CYCLES = 3
PARTS_SIZE = 400

TIME_STEP = 0.1
DAMP_RATIO = 0.05
PENALTY = 2.0
GAP_WIDTH = 0.5
CONTACT_DAMP = 0.2

BF = jnp.bfloat16
F32 = jnp.float32
NT = (((1,), (1,)), ((), ()))
LANES = 128
ROWS = 32
NBR = 5
TOGETHER = 8

VMEM = pl.BlockSpec(memory_space=pltpu.VMEM)
SMEM = pl.BlockSpec(memory_space=pltpu.SMEM)
HBM = pl.BlockSpec(memory_space=pltpu.HBM)


def call(body, outs, in_specs, name, scratch=(), flops=0):
    return pl.pallas_call(
        body,
        out_shape=[jax.ShapeDtypeStruct(s, d) for s, d in outs],
        in_specs=in_specs,
        out_specs=[VMEM] * len(outs),
        scratch_shapes=list(scratch),
        compiler_params=pltpu.CompilerParams(vmem_limit_bytes=40 << 20),
        cost_estimate=pl.CostEstimate(flops=flops, bytes_accessed=1 << 20, transcendentals=0),
        name=name,
    )


def lanes_of(row, idx):
    return jnp.take_along_axis(row, idx, axis=1, mode="promise_in_bounds")


def gather(tab, bases, lo, hi, rows=ROWS):
    acc = [None] * len(bases)
    for h in range(rows):
        here = hi == h
        for c, base in enumerate(bases):
            row = jnp.broadcast_to(tab[base + h : base + h + 1, :], (8, LANES))
            val = lanes_of(row, lo)
            acc[c] = val if h == 0 else jnp.where(here, val, acc[c])
    return acc


def wide(x, a, n):
    row = jnp.broadcast_to(x[a : a + 1, :].astype(F32), (16, LANES)).astype(BF)
    return jnp.concatenate([row] * (n // 16), 0)


def iota_rows(n):
    return lax.broadcasted_iota(jnp.int32, (n, LANES), 0).astype(F32).astype(BF)


def place(lo, hi, vals, held, base):
    it = iota_rows(LANES)
    one, zero = jnp.ones((LANES, LANES), BF), jnp.zeros((LANES, LANES), BF)
    first = [v.astype(BF).astype(F32) for v in vals]
    items = first + [v - x for v, x in zip(vals, first)] + [lo.astype(F32), hi.astype(F32)]
    for k, x in enumerate(items):
        held[base + 8 * k : base + 8 * k + 8, :] = x

    def spread(k, a, n):
        at = base + 8 * k + a
        row = jnp.broadcast_to(held[at : at + 1, :], (16, LANES)).astype(BF)
        return jnp.concatenate([row] * (n // 16), 0)

    left, right = [], []
    count = 2 * len(vals)
    for a in range(8):
        right.append(jnp.where(spread(count, a, LANES) == it, one, zero))
        mask = spread(count + 1, a, ROWS) == it[:ROWS]
        left.append(jnp.concatenate([jnp.where(mask, spread(k, a, ROWS), zero[:ROWS]) for k in range(count)], 0))
    return jnp.concatenate(left, 1), jnp.concatenate(right, 1)


def add_placed(acc, lo, hi, vals, held):
    left, right = place(lo, hi, vals, held, 0)
    acc[...] += lax.dot_general(left, right, NT, preferred_element_type=F32)


def to_rows(src, dst):
    for c in range(3):
        for h in range(ROWS):
            dst[c * ROWS + h : c * ROWS + h + 1, :] = src[c : c + 1, h * LANES : (h + 1) * LANES]


def elements(idx, mat, tab, cols, g, acc, held):
    acc[...] = jnp.zeros_like(acc)
    steps = ROWS // TOGETHER

    def corners(i, q):
        here = idx[:, pl.ds(pl.multiple_of((i * TOGETHER + q) * LANES, LANES), LANES)]
        return here & 127, here >> 7

    def fetch(i):
        vals = []
        for q in range(TOGETHER):
            vals += gather(tab, (0, ROWS, 2 * ROWS), *corners(i, q))
        return tuple(vals)

    def step(i, vals):
        upcoming = fetch((i + 1) & (steps - 1))
        left, right = [], []
        for q in range(TOGETHER):
            for c in range(3):
                g[q * 24 + 8 * c : q * 24 + 8 * c + 8, :] = vals[q * 3 + c]
            first = mat[i * TOGETHER + q] * 24
            force = [jnp.zeros((8, LANES), F32)] * 3
            for j in range(24):
                col = cols.at[first + j]
                row = jnp.broadcast_to(g[q * 24 + j : q * 24 + j + 1, :], (8, LANES))
                force = [force[c] + col[8 * c : 8 * c + 8, :] * row for c in range(3)]
            one, two = place(*corners(i, q), force, held, 64 * q)
            left.append(one)
            right.append(two)
        acc[...] += lax.dot_general(
            jnp.concatenate(left, 1), jnp.concatenate(right, 1), NT, preferred_element_type=F32
        )
        return upcoming

    lax.fori_loop(0, steps, step, fetch(0))


def finish_internal(acc, internal, shared):
    internal[...] = acc[0:96, :] + acc[96:192, :]
    return gather(internal, (0, ROWS, 2 * ROWS), shared[...] & 127, shared[...] >> 7)


def slotted(hitb, rank, vals):
    rows = lax.broadcasted_iota(jnp.int32, (64, LANES), 0).astype(F32)
    mine = jnp.broadcast_to(rank, (64, LANES)) == rows
    left = [jnp.broadcast_to(x, (64, LANES)) for x in vals]
    pieces = []
    for s in range(3):
        pieces.append(jnp.concatenate([jnp.where(mine, x, 0.0).astype(BF) for x in left], 0))
        left = [x - x.astype(BF).astype(F32) for x in left]
    return [hitb] * 3, pieces


def hits_of(owner_row):
    down = lax.broadcasted_iota(jnp.int32, (LANES, LANES), 0)
    return jnp.where(jnp.broadcast_to(owner_row, (LANES, LANES)) == down, 1.0, 0.0)


def slots(owner, master, normal, slot, acc, between):
    acc[...] = jnp.zeros_like(acc)
    down = lax.broadcasted_iota(jnp.int32, (LANES, LANES), 0)
    across = lax.broadcasted_iota(jnp.int32, (LANES, LANES), 1)
    before = jnp.where(down < across, 1.0, 0.0).astype(BF)
    hits = [hits_of(owner[t : t + 1, :]) for t in range(16)]
    counts = jnp.dot(jnp.concatenate([hit.astype(BF) for hit in hits], 0), before, preferred_element_type=F32)
    carry = jnp.zeros((LANES, 1), F32)
    for t, hit in enumerate(hits):
        count = counts[t * LANES : (t + 1) * LANES, :] + carry
        rank = jnp.sum(hit * count, axis=0, keepdims=True)
        carry = carry + jnp.sum(hit, axis=1, keepdims=True)
        slot[t : t + 1, :] = owner[t : t + 1, :] * 64 + rank.astype(jnp.int32)
    for four in range(4):
        hits, pieces = [], []
        for t in range(4 * four, 4 * four + 4):
            vals = [normal[c : c + 1, t * LANES : (t + 1) * LANES] for c in range(3)]
            rank = (slot[t : t + 1, :] & 63).astype(F32)
            one, two = slotted(
                hits_of(owner[t : t + 1, :]).astype(BF), rank, [*vals, master[t : t + 1, :].astype(F32)]
            )
            hits += one
            pieces += two
        between(2 * four)
        between(2 * four + 1)
        acc[...] += lax.dot_general(
            jnp.concatenate(hits, 1), jnp.concatenate(pieces, 1), NT, preferred_element_type=F32
        )


def spans():
    return [(h, min(LANES, PARTS_SIZE - h * LANES)) for h in range(4)]


def every(first, stride, count=LANES):
    return pl.ds(first, count, stride=stride)


def copy_all(srcs, dsts, sems):
    copies = [pltpu.make_async_copy(a, b, sems.at[i]) for i, (a, b) in enumerate(zip(srcs, dsts))]
    for copy in copies:
        copy.start()
    return copies


def first_kernel(*refs):
    srcs = [*refs[:13], refs[7]]
    u, v, fm, mass, idx, inv, cols, shared, internal, send, slave, slot, normal, matv = refs[13:27]
    disp0, vel0, force0, shared0, owner, master, stiff, accel, conn, mat, tab, g, acc, held, small, table, sems = refs[27:]
    dsts = (stiff, owner, master, normal, disp0, vel0, conn, mat, shared0, force0, mass, accel, slave, matv)
    copies = copy_all(srcs, dsts, sems)

    def columns(m):
        for j in range(24):
            cols[m * 24 + j] = jnp.broadcast_to(stiff[m, :, j : j + 1], (24, LANES))

    for copy in copies[:4]:
        copy.wait()
    slots(owner, master, normal, slot, table, columns)
    send[...] = jnp.zeros_like(send)
    send[every(0, 5), :] = table[:, 0:128]
    send[every(1, 5), :] = table[:, 128:256]
    for copy in copies[4:]:
        copy.wait()
    to_rows(disp0, u)
    to_rows(vel0, v)
    to_rows(force0, fm)
    tab[...] = u[...] + DAMP_RATIO * v[...]
    for c in range(3):
        at = slice(c * ROWS, (c + 1) * ROWS)
        fm[at, :] = fm[at, :] / mass[...] - accel[c]
    lane = lax.broadcasted_iota(jnp.int32, (8, LANES), 1)
    for b in range(ROWS):
        at = slice(b * LANES, (b + 1) * LANES)
        idx[:, at] = (conn[:, at] + lane + b * LANES) & 4095
    shared[...] = jnp.zeros_like(shared)
    for b in range(NBR):
        shared[b : b + 1, :] = shared0[b]
    small[...] = jnp.zeros_like(small)
    row = lax.broadcasted_iota(jnp.int32, (8, LANES), 0)
    listed = row < NBR
    lo, hi = shared[...] & 127, shared[...] >> 7
    kept = [jnp.where(listed, lane, 0).astype(F32), jnp.where(listed, row + 1, 0).astype(F32)]
    add_placed(small, lo, hi, kept, held)
    found = (small[0:64, :] + small[64:128, :]).astype(jnp.int32)
    inv[...] = found[0:ROWS, :] + found[ROWS : 2 * ROWS, :] * LANES
    elements(idx, mat, tab, cols, g, acc, held)
    own = finish_internal(acc, internal, shared)
    me = lax.axis_index("dom")
    for b in range(NBR):
        for c in range(3):
            send[pl.ds(5 * (me ^ (1 << b)) + 2 + c, 1), :] = own[c][b : b + 1, :]


def fixed_kernel(*refs):
    pos0, part0, pmass0, pcenter0, pinertia0, normal, shared, mass, pos, part, nrm, light, rigid = refs[:13]
    pos1, pmass, pcenter, pinertia, sems = refs[13:]
    copies = copy_all(
        (pos0, part0, pmass0, pcenter0, pinertia0), (pos1, part, pmass, pcenter, pinertia), sems
    )
    (weight,) = gather(mass, (0,), shared[...] & 127, shared[...] >> 7)
    light[...] = -TIME_STEP / weight
    for t in range(16):
        for c in range(3):
            nrm[16 * c + t : 16 * c + t + 1, :] = normal[c : c + 1, t * LANES : (t + 1) * LANES]
    rigid[...] = jnp.ones_like(rigid)
    for copy in copies:
        copy.wait()
    to_rows(pos1, pos)
    for h, n in spans():
        at = slice(h * LANES, h * LANES + n)
        rigid[h : h + 1, 0:n] = pmass[0:1, at]
        for c in range(3):
            rigid[8 + 8 * c + h : 9 + 8 * c + h, 0:n] = pcenter[c : c + 1, at]
            rigid[32 + 8 * c + h : 33 + 8 * c + h, 0:n] = pinertia[c : c + 1, at]


def from_shared(code, rows):
    total = 0.0
    for b in range(NBR):
        row = jnp.broadcast_to(rows[b], (8, LANES))
        total = total + jnp.where(code >> 7 == b + 1, lanes_of(row, code & 127), 0.0)
    return total


def update(u, v, internal, inv, fm, mass, recv, c, r):
    at = slice(c * ROWS + r, c * ROWS + r + 8)
    total = internal[at, :] + from_shared(inv[r : r + 8, :], [recv[b][c] for b in range(NBR)])
    speed = v[at, :] + TIME_STEP * (fm[at, :] - total / mass[r : r + 8, :])
    return at, u[at, :] + TIME_STEP * speed, speed, total


def rows_of(refs):
    return [[ref[c : c + 1, :] for c in range(3)] for ref in refs]


def next_kernel(from_table, u, v, internal, inv, fm, mass, idx, matv, cols, shared, *rest):
    if from_table:
        got, rest = rest[0], rest[1:]
        me = lax.axis_index("dom")
        recv = [[got[pl.ds(5 * (me ^ (1 << b)) + 2 + c, 1), :] for c in range(3)] for b in range(NBR)]
    else:
        recv, rest = rows_of(rest[:NBR]), rest[NBR:]
    u2, v2, internal2 = rest[:3]
    own = rest[3:8]
    tab, g, acc, held, mat, sem = rest[8:]
    numbers = pltpu.make_async_copy(matv, mat, sem)
    numbers.start()
    for c in range(3):
        for r in range(0, ROWS, 8):
            at, disp, speed, _ = update(u, v, internal, inv, fm, mass, recv, c, r)
            u2[at, :] = disp
            v2[at, :] = speed
            tab[at, :] = disp + DAMP_RATIO * speed
    numbers.wait()
    elements(idx, mat, tab, cols, g, acc, held)
    vals = finish_internal(acc, internal2, shared)
    for b in range(NBR):
        for c in range(3):
            own[b][c : c + 1, :] = vals[c][b : b + 1, :]


def ends_kernel(got, slave, inv, midx, mnrm, code):
    left = lax.broadcasted_iota(jnp.int32, (64, LANES), 1) < 64
    for k, out in ((0, mnrm.at[0]), (1, mnrm.at[1]), (2, mnrm.at[2]), (3, midx)):
        top, low = got[every(k // 2, 5, 64), :], got[every(320 + k // 2, 5, 64), :]
        if k % 2:
            out[...] = jnp.where(left, pltpu.roll(top, 64, 1), low).astype(out.dtype)
        else:
            out[...] = jnp.where(left, top, pltpu.roll(low, 64, 1))
    for r in range(0, 80, 8):
        here = slave[r : r + 8, :] if r < 16 else midx[r - 16 : r - 8, :]
        (code[r : r + 8, :],) = gather(inv, (0,), here & 127, here >> 7)


def base_kernel(u, v, internal, fm, mass, pos, slave, nrm, midx, mnrm, x2, v2, ab, tab):
    for c in range(3):
        for r in range(0, ROWS, 8):
            at = slice(c * ROWS + r, c * ROWS + r + 8)
            speed = v[at, :] + TIME_STEP * (fm[at, :] - internal[at, :] / mass[r : r + 8, :])
            place_now = pos[at, :] + (u[at, :] + TIME_STEP * speed)
            x2[at, :] = place_now
            v2[at, :] = speed
            tab[at, :] = place_now
            tab[c * ROWS + 96 + r : c * ROWS + 96 + r + 8, :] = speed

    def both(here, w):
        y = gather(tab, tuple(range(0, 192, ROWS)), here & 127, here >> 7)
        return y[0] * w[0] + y[1] * w[1] + y[2] * w[2], y[3] * w[0] + y[4] * w[1] + y[5] * w[2]

    for r in (0, 8):
        w = [nrm[16 * c + r : 16 * c + r + 8, :] for c in range(3)]
        ab[0, r : r + 8, :], ab[1, r : r + 8, :] = both(slave[r : r + 8, :], w)

    def step(i, carry):
        for q in range(2):
            at = pl.ds(pl.multiple_of(i * 16 + q * 8, 8), 8)
            to = pl.ds(pl.multiple_of(i * 16 + q * 8 + 16, 8), 8)
            ab[0, to, :], ab[1, to, :] = both(midx[at, :], [mnrm[c, at, :] for c in range(3)])
        return carry

    lax.fori_loop(0, 4, step, 0)


def dots_kernel(x1, v1, ab1, internal, inv, light, fm, mass, part, slot, nrm, mnrm, code, *rest):
    recv = rows_of(rest[:5])
    x2, v2, net, dots, acc, table, ab = rest[5:]
    for c in range(3):
        for r in range(0, ROWS, 8):
            at = slice(c * ROWS + r, c * ROWS + r + 8)
            m = mass[r : r + 8, :]
            more = from_shared(inv[r : r + 8, :], [recv[b][c] for b in range(NBR)])
            change = -TIME_STEP * (more / m)
            x2[at, :] = x1[at, :] + TIME_STEP * change
            v2[at, :] = v1[at, :] + change
            net[at, :] = m * fm[at, :] - internal[at, :] - more
    moved = [[recv[b][c] * light[b : b + 1, :] for b in range(NBR)] for c in range(3)]
    for r in range(0, 80, 8):
        here = code[r : r + 8, :]
        if r < 16:
            w = [nrm[16 * c + r : 16 * c + r + 8, :] for c in range(3)]
        else:
            w = [mnrm[c, r - 16 : r - 8, :] for c in range(3)]
        d = [from_shared(here, moved[c]) for c in range(3)]
        change = d[0] * w[0] + d[1] * w[1] + d[2] * w[2]
        ab[0, r : r + 8, :] = ab1[0, r : r + 8, :] + TIME_STEP * change
        ab[1, r : r + 8, :] = ab1[1, r : r + 8, :] + change

    def vals(r):
        m = mass[r : r + 8, :]
        return [m, *[m * x2[c * ROWS + r : c * ROWS + r + 8, :] for c in range(3)]]

    acc[...] = jnp.zeros_like(acc)
    part_sums(part, vals, acc, True)
    moments = jnp.concatenate([acc[0:32, :] + acc[32:64, :], jnp.zeros((96, LANES), F32)], 0)
    dots[every(2, 3), :] = moments.T
    table[...] = jnp.zeros_like(table)
    for i in range(4):
        hits, pieces = [], []
        for t in range(4 * i, 4 * i + 4):
            here = slot[t : t + 1, :]
            rows = [ab[0, t : t + 1, :], ab[1, t : t + 1, :]]
            one, two = slotted(hits_of(here >> 6).astype(BF), (here & 63).astype(F32), rows)
            hits += one
            pieces += two
        table[...] += lax.dot_general(
            jnp.concatenate(hits, 1), jnp.concatenate(pieces, 1), NT, preferred_element_type=F32
        )
    left = lax.broadcasted_iota(jnp.int32, (64, LANES), 1) < 64
    one, two = ab[0, 16:80, :], ab[1, 16:80, :]
    dots[every(0, 3), :] = table[...]
    dots[every(1, 3, 64), :] = jnp.where(left, one, pltpu.roll(two, 64, 1))
    dots[every(193, 3, 64), :] = jnp.where(left, pltpu.roll(one, 64, 1), two)


def part_sums(part, vals, acc, by_device):
    it = iota_rows(LANES)
    it8 = (lax.broadcasted_iota(jnp.int32, (16, LANES), 0) & 7).astype(F32).astype(BF)
    one, zero = jnp.ones((LANES, LANES), BF), jnp.zeros((LANES, LANES), BF)
    for r in range(0, ROWS, 8):
        here = part[r : r + 8, :]
        lo = here & 127
        if by_device:
            lo = ((lo & 63) << 1) | (lo >> 6)
        lof, hif = lo.astype(F32), (here >> 7).astype(F32)
        val = vals(r)
        first = [x.astype(BF).astype(F32) for x in val]
        split = (first, [x - y for x, y in zip(val, first)])
        left, right = [], []
        for a in range(8):
            right.append(jnp.where(wide(lof, a, LANES) == it, one, zero))
            mask = wide(hif, a, 16) == it8
            rows = []
            for s in range(2):
                for k in range(0, len(val), 2):
                    two = [jnp.broadcast_to(split[s][k + d][a : a + 1, :], (8, LANES)) for d in range(2)]
                    rows.append(jnp.where(mask, jnp.concatenate(two, 0).astype(BF), zero[:16]))
            left.append(jnp.concatenate(rows, 0))
        acc[...] += lax.dot_general(
            jnp.concatenate(left, 1), jnp.concatenate(right, 1), NT, preferred_element_type=F32
        )


def contact_kernel(
    dots, got, slave, slot, nrm, midx, mnrm, x, net, part, contact, keep, give, acc, tot, acc2, push, mine, held
):
    acc[...] = jnp.zeros_like(acc)
    acc2[...] = jnp.zeros_like(acc2)
    left = lax.broadcasted_iota(jnp.int32, (LANES, LANES), 1) < 64
    as_slave = dots[every(0, 3), :] - got[every(1, 3), :]
    as_master = got[every(0, 3), :] - dots[every(1, 3), :]
    gap = jnp.where(left, as_slave, pltpu.roll(as_master, 64, 1))
    closing = jnp.where(left, pltpu.roll(as_slave, 64, 1), as_master)
    z = -gap / GAP_WIDTH
    soft = jnp.maximum(z, 0.0) + jnp.log1p(jnp.exp(-jnp.abs(z)))
    size = PENALTY * GAP_WIDTH * soft - CONTACT_DAMP * closing
    top, low = size[0:64, :], size[64:128, :]
    mine[...] = jnp.where(left[0:64, :], top, pltpu.roll(low, 64, 1))
    push[...] = -jnp.where(left[0:64, :], pltpu.roll(top, 64, 1), low)

    def step(i, carry):
        one, two = [], []
        for q in range(4):
            at = pl.ds(pl.multiple_of(i * 32 + q * 8, 8), 8)
            here, size = midx[at, :], push[at, :]
            pair = place(here & 127, here >> 7, [size * mnrm[c, at, :] for c in range(3)], held, 64 * q)
            one.append(pair[0])
            two.append(pair[1])
        acc[...] += lax.dot_general(
            jnp.concatenate(one, 1), jnp.concatenate(two, 1), NT, preferred_element_type=F32
        )
        return carry

    lax.fori_loop(0, 2, step, 0)
    one, two = [], []
    for r in (0, 8):
        here, at = slave[r : r + 8, :], slot[r : r + 8, :]
        (size,) = gather(mine, (0,), ((at >> 12) << 6) + (at & 63), (at >> 6) & 63, 64)
        w = [size * nrm[16 * c + r : 16 * c + r + 8, :] for c in range(3)]
        pair = place(here & 127, here >> 7, w, held, 256 + 8 * r)
        one.append(pair[0])
        two.append(pair[1])
    acc[...] += lax.dot_general(
        jnp.concatenate(one, 1), jnp.concatenate(two, 1), NT, preferred_element_type=F32
    )
    contact[...] = acc[0:96, :] + acc[96:192, :]
    tot[...] = net[...] + contact[...]

    def vals(r):
        p = [x[c * ROWS + r : c * ROWS + r + 8, :] for c in range(3)]
        n = [tot[c * ROWS + r : c * ROWS + r + 8, :] for c in range(3)]
        return [
            *n,
            p[1] * n[2] - p[2] * n[1],
            p[2] * n[0] - p[0] * n[2],
            p[0] * n[1] - p[1] * n[0],
        ]

    part_sums(part, vals, acc2, False)
    acc2[0:48, :] = acc2[0:48, :] + acc2[48:96, :]
    lane = lax.broadcasted_iota(jnp.int32, (8, LANES), 1)
    last = jnp.zeros((8, LANES), F32)
    for k in range(6):
        piece = jnp.where(lane < 16, acc2[8 * k : 8 * k + 8, :], 0.0)
        last = last + (pltpu.roll(piece, 16 * k, 1) if k else piece)
    even = lax.axis_index("dom") & 1 == 0
    pairs = [(acc2[8 * k : 8 * k + 1, :], acc2[8 * k + 2 : 8 * k + 3, :]) for k in range(6)]
    pairs += [(acc2[8 * k + 1 : 8 * k + 2, :], acc2[8 * k + 25 : 8 * k + 26, :]) for k in range(3)]
    pairs += [(jnp.zeros((1, LANES), F32), last[3:4, :])]
    for k, (low, high) in enumerate(pairs):
        keep[k : k + 1, :] = jnp.where(even, low, high)
        give[k : k + 1, :] = jnp.where(even, high, low)
    keep[10:16, :] = jnp.zeros((6, LANES), F32)
    give[10:16, :] = jnp.zeros((6, LANES), F32)
    moments = jnp.broadcast_to(jnp.sum(got[every(2, 3), :], axis=0, keepdims=True), (8, LANES))
    moments = jnp.where(lane < 96, 0.0, pltpu.roll(moments, 96, 1))
    keep[9:10, :] = keep[9:10, :] + moments[0:1, :]


def nodal_kernel(v, contact, mass, nodal):
    for c in range(3):
        at = slice(c * ROWS, (c + 1) * ROWS)
        speed = v[at, :] + TIME_STEP * contact[at, :] / mass[...]
        for h in range(ROWS):
            nodal[c : c + 1, h * LANES : (h + 1) * LANES] = speed[h : h + 1, :]


def spread_kernel(keep, given, out):
    tile = (keep[...] + given[...])[0:10, :]
    four = jnp.concatenate([tile] * 4, 0)
    for k in range(16):
        out[40 * k : 40 * k + 40, :] = four


def total_kernel(got, out):
    four = got[0:40, :]
    for k in range(1, 16):
        four = four + got[40 * k : 40 * k + 40, :]
    out[0:10, :] = four[0:10, :] + four[10:20, :] + four[20:30, :] + four[30:40, :]
    out[10:16, :] = jnp.zeros((6, LANES), F32)
    out[16:80, :] = pltpu.roll(got[every(9, 10, 64), :], 32, 1)


def motion_kernel(mine, other, rigid, out):
    even = lax.axis_index("dom") & 1 == 0
    low = jnp.where(even, mine[...], other[...])
    high = jnp.where(even, other[...], mine[...])
    by = jnp.concatenate([low[16:80, :], high[16:80, :]], 0).T
    moments = [by[8 * k : 8 * k + 4, :] for k in range(4)]
    sums = []
    for k in range(6):
        second = low[6 + k : 7 + k, :] if k < 3 else high[3 + k : 4 + k, :]
        last = pltpu.roll(high[8:16, :], LANES - 16 * k, 1) if k else high[8:16, :]
        sums.append(jnp.concatenate([low[k : k + 1, :], second, high[k : k + 1, :], last[1:2, :]], 0))
    own = rigid[0:4, :]
    mass = own + moments[0]
    centre = [(own * rigid[8 + 8 * c : 12 + 8 * c, :] + moments[1 + c]) / mass for c in range(3)]
    force, turn = sums[0:3], sums[3:6]
    rows = [y / mass for y in force]
    for c in range(3):
        a, b = (c + 1) % 3, (c + 2) % 3
        moment = turn[c] - (centre[a] * force[b] - centre[b] * force[a])
        rows.append(moment / rigid[32 + 8 * c : 36 + 8 * c, :])
    for r, row in enumerate(rows):
        for h, n in spans():
            out[r : r + 1, h * LANES : h * LANES + n] = row[h : h + 1, 0:n]


def partner(block, apart):
    count = lax.axis_size("dom")
    return lax.ppermute(block, "dom", [(i, i ^ (1 << apart)) for i in range(count)])


def in_hbm(*arrays):
    return [pltpu.with_memory_space_constraint(x, pltpu.HBM) for x in arrays]


def later(value, than):
    return lax.optimization_barrier((value, than))[0]


def swap(block, groups=None):
    peers = len(groups[0]) if groups else lax.axis_size("dom")
    flat = block.reshape(peers, 1, -1)
    return lax.all_to_all(flat, "dom", 0, 0, tiled=True, axis_index_groups=groups).reshape(block.shape)


def per_device(
    rest_pos,
    displacement,
    velocity,
    ext_force,
    node_mass,
    body_accel,
    connectivity,
    elem_material,
    stiffness,
    shared_nodes,
    contact_slave,
    contact_owner,
    contact_master,
    contact_normal,
    part_of_node,
    part_mass,
    part_center,
    part_inertia,
):
    state = ((96, LANES), F32)
    table = ((5 * LANES, LANES), F32)
    own = [((3, LANES), F32)] * NBR
    work = [
        pltpu.VMEM((96, LANES), F32),
        pltpu.VMEM((24 * TOGETHER, LANES), F32),
        pltpu.VMEM((192, LANES), F32),
        pltpu.VMEM((64 * TOGETHER, LANES), F32),
    ]
    inputs = (
        stiffness,
        contact_owner.reshape(16, LANES),
        contact_master.reshape(16, LANES),
        contact_normal,
        displacement,
        velocity,
        connectivity,
        elem_material,
        shared_nodes.transpose(1, 0, 2),
        ext_force,
        node_mass.reshape(ROWS, LANES),
        body_accel,
        contact_slave.reshape(16, LANES),
    )
    rows, ints = ((ROWS, LANES), F32), jnp.int32
    whole, map_rows = pltpu.VMEM((3, 4096), F32), ((ROWS, LANES), ints)
    u, v, fm, mass, idx, inv, cols, shared, internal, send, slave, slot, normal, mat = call(
        first_kernel,
        [
            state,
            state,
            state,
            rows,
            ((8, 4096), ints),
            map_rows,
            ((192, 24, LANES), F32),
            ((8, LANES), ints),
            state,
            table,
            ((16, LANES), ints),
            ((16, LANES), ints),
            ((3, 2048), F32),
            ((ROWS,), ints),
        ],
        [HBM] * 13,
        "first_cycle",
        [
            whole,
            whole,
            whole,
            pltpu.VMEM((NBR, 1, LANES), ints),
            pltpu.VMEM((16, LANES), ints),
            pltpu.VMEM((16, LANES), ints),
            pltpu.VMEM((8, 24, 24), F32),
            pltpu.SMEM((3,), F32),
            pltpu.VMEM((8, 4096), ints),
            pltpu.SMEM((ROWS,), ints),
            *work,
            pltpu.VMEM((LANES, LANES), F32),
            pltpu.VMEM((LANES, 2 * LANES), F32),
            pltpu.SemaphoreType.DMA((14,)),
        ],
    )(*in_hbm(*inputs))
    got = swap(send)
    trio = ((3, PARTS_SIZE), F32)
    recv = [got]
    for n in range(CYCLES - 1):
        u, v, internal, *mine = call(
            functools.partial(next_kernel, n == 0),
            [state, state, state, *own],
            [VMEM] * (10 + len(recv)),
            "next_cycle",
            [*work, pltpu.SMEM((ROWS,), ints), pltpu.SemaphoreType.DMA],
        )(u, v, internal, inv, fm, mass, idx, mat, cols, shared, *recv)
        recv = [partner(mine[b], b) for b in range(NBR)]
        if n == 0:
            midx, mnrm, code = call(
                ends_kernel,
                [((64, LANES), ints), ((3, 64, LANES), F32), ((80, LANES), ints)],
                [VMEM] * 3,
                "contact_ends",
            )(later(got, mine), slave, inv)
            pos, part, nrm, light, rigid = call(
                fixed_kernel,
                [state, map_rows, ((48, LANES), F32), ((8, LANES), F32), ((56, LANES), F32)],
                [HBM] * 5 + [VMEM] * 3,
                "fixed_data",
                [
                    whole,
                    pltpu.VMEM((1, PARTS_SIZE), F32),
                    pltpu.VMEM(*trio),
                    pltpu.VMEM(*trio),
                    pltpu.SemaphoreType.DMA((5,)),
                ],
            )(
                *in_hbm(
                    rest_pos,
                    part_of_node.reshape(ROWS, LANES),
                    part_mass.reshape(1, PARTS_SIZE),
                    part_center,
                    part_inertia,
                ),
                later(normal, mine),
                shared,
                mass,
            )
            recv, code, nrm = lax.optimization_barrier((recv, code, nrm))
    both = ((2, 80, LANES), F32)
    x, v, ab = call(
        base_kernel,
        [state, state, both],
        [VMEM] * 10,
        "contact_base",
        [pltpu.VMEM((192, LANES), F32)],
    )(u, v, internal, fm, mass, pos, slave, nrm, midx, mnrm)
    x, v, net, dots = call(
        dots_kernel,
        [state, state, state, ((3 * LANES, LANES), F32)],
        [VMEM] * 18,
        "contact_dots",
        [pltpu.VMEM((64, LANES), F32), pltpu.VMEM((LANES, LANES), F32), pltpu.VMEM(*both)],
    )(x, v, ab, internal, inv, light, fm, mass, part, slot, nrm, mnrm, code, *recv)
    half = ((16, LANES), F32)
    contact, keep, give = call(
        contact_kernel,
        [state, half, half],
        [VMEM] * 10,
        "contact_forces",
        [
            pltpu.VMEM((192, LANES), F32),
            pltpu.VMEM((96, LANES), F32),
            pltpu.VMEM((96, LANES), F32),
            pltpu.VMEM((64, LANES), F32),
            pltpu.VMEM((64, LANES), F32),
            pltpu.VMEM((384, LANES), F32),
        ],
    )(dots, swap(dots), slave, slot, nrm, midx, mnrm, x, net, part)
    (nodal_velocity,) = call(nodal_kernel, [((3, 4096), F32)], [VMEM] * 3, "nodal_velocity")(v, contact, mass)
    (spread,) = call(spread_kernel, [((640, LANES), F32)], [VMEM] * 2, "part_spread")(keep, partner(give, 0))
    chips = lax.axis_size("dom") // 2
    groups = [[2 * i + core for i in range(chips)] for core in range(2)]
    (total,) = call(total_kernel, [((80, LANES), F32)], [VMEM], "part_totals")(swap(spread, groups))
    (motion,) = call(motion_kernel, [((6, PARTS_SIZE), F32)], [VMEM] * 3, "part_motion")(
        total, partner(total, 0), rigid
    )
    return nodal_velocity, motion


def solution(mesh):
    placed = (
        P(None, "dom"),
        P(None, "dom"),
        P(None, "dom"),
        P(None, "dom"),
        P("dom"),
        P(),
        P(None, "dom"),
        P("dom"),
        P(),
        P("dom", None, None),
        P("dom"),
        P("dom", None),
        P("dom"),
        P(None, "dom"),
        P("dom"),
        P(),
        P(),
        P(),
    )
    return jax.shard_map(
        per_device, mesh=mesh, in_specs=placed, out_specs=(P(None, "dom"), P()), check_vma=False
    )
```

```python
import functools

import jax
import jax.numpy as jnp
from jax import lax
from jax.experimental import pallas as pl
from jax.experimental.pallas import tpu as pltpu
from jax.sharding import PartitionSpec as P

CYCLES = 3
PARTS_SIZE = 400

TIME_STEP = 0.1
DAMP_RATIO = 0.05
PENALTY = 2.0
GAP_WIDTH = 0.5
CONTACT_DAMP = 0.2

BF = jnp.bfloat16
F32 = jnp.float32
NT = (((1,), (1,)), ((), ()))
LANES = 128
ROWS = 32
NBR = 5
TOGETHER = 8
AHEAD = 2

VMEM = pl.BlockSpec(memory_space=pltpu.VMEM)
SMEM = pl.BlockSpec(memory_space=pltpu.SMEM)
HBM = pl.BlockSpec(memory_space=pltpu.HBM)


def call(body, outs, in_specs, name, scratch=(), flops=0):
    return pl.pallas_call(
        body,
        out_shape=[jax.ShapeDtypeStruct(s, d) for s, d in outs],
        in_specs=in_specs,
        out_specs=[VMEM] * len(outs),
        scratch_shapes=list(scratch),
        compiler_params=pltpu.CompilerParams(vmem_limit_bytes=40 << 20),
        cost_estimate=pl.CostEstimate(flops=flops, bytes_accessed=1 << 20, transcendentals=0),
        name=name,
    )


def lanes_of(row, idx):
    return jnp.take_along_axis(row, idx, axis=1, mode="promise_in_bounds")


def gather(tab, bases, lo, hi, rows=ROWS):
    acc = [None] * len(bases)
    for h in range(rows):
        here = hi == h
        for c, base in enumerate(bases):
            row = jnp.broadcast_to(tab[base + h : base + h + 1, :], (8, LANES))
            val = lanes_of(row, lo)
            acc[c] = val if h == 0 else jnp.where(here, val, acc[c])
    return acc


def wide(x, a, n):
    row = jnp.broadcast_to(x[a : a + 1, :].astype(F32), (16, LANES)).astype(BF)
    return jnp.concatenate([row] * (n // 16), 0)


def iota_rows(n):
    return lax.broadcasted_iota(jnp.int32, (n, LANES), 0).astype(F32).astype(BF)


def place(lo, hi, vals, held, base):
    it = iota_rows(LANES)
    one, zero = jnp.ones((LANES, LANES), BF), jnp.zeros((LANES, LANES), BF)
    first = [v.astype(BF).astype(F32) for v in vals]
    items = first + [v - x for v, x in zip(vals, first)] + [lo.astype(F32), hi.astype(F32)]
    for k, x in enumerate(items):
        held[base + 8 * k : base + 8 * k + 8, :] = x

    def spread(k, a, n):
        at = base + 8 * k + a
        row = jnp.broadcast_to(held[at : at + 1, :], (16, LANES)).astype(BF)
        return jnp.concatenate([row] * (n // 16), 0)

    left, right = [], []
    count = 2 * len(vals)
    for a in range(8):
        right.append(jnp.where(spread(count, a, LANES) == it, one, zero))
        mask = spread(count + 1, a, ROWS) == it[:ROWS]
        left.append(jnp.concatenate([jnp.where(mask, spread(k, a, ROWS), zero[:ROWS]) for k in range(count)], 0))
    return jnp.concatenate(left, 1), jnp.concatenate(right, 1)


def add_placed(acc, lo, hi, vals, held):
    left, right = place(lo, hi, vals, held, 0)
    acc[...] += lax.dot_general(left, right, NT, preferred_element_type=F32)


def to_rows(src, dst):
    for c in range(3):
        for h in range(ROWS):
            dst[c * ROWS + h : c * ROWS + h + 1, :] = src[c : c + 1, h * LANES : (h + 1) * LANES]


def elements(idx, mat, tab, cols, g, acc, held):
    acc[...] = jnp.zeros_like(acc)

    def corners(b):
        here = idx[:, pl.ds(pl.multiple_of(b * LANES, LANES), LANES)]
        return here & 127, here >> 7

    def fetch(b):
        return gather(tab, (0, ROWS, 2 * ROWS), *corners(b & (ROWS - 1)))

    def step(i, vals):
        vals = list(vals)
        left, right = [], []
        for q in range(TOGETHER):
            b = i * TOGETHER + q
            vals += fetch(b + AHEAD)
            for c in range(3):
                g[q * 24 + 8 * c : q * 24 + 8 * c + 8, :] = vals[c]
            vals = vals[3:]
            first = mat[b] * 24
            force = [jnp.zeros((8, LANES), F32)] * 3
            for j in range(24):
                col = cols.at[first + j]
                row = jnp.broadcast_to(g[q * 24 + j : q * 24 + j + 1, :], (8, LANES))
                force = [force[c] + col[8 * c : 8 * c + 8, :] * row for c in range(3)]
            one, two = place(*corners(b), force, held, 64 * q)
            left.append(one)
            right.append(two)
        acc[...] += lax.dot_general(
            jnp.concatenate(left, 1), jnp.concatenate(right, 1), NT, preferred_element_type=F32
        )
        return tuple(vals)

    lax.fori_loop(0, ROWS // TOGETHER, step, tuple(x for b in range(AHEAD) for x in fetch(b)))


def finish_internal(acc, internal, shared):
    internal[...] = acc[0:96, :] + acc[96:192, :]
    return gather(internal, (0, ROWS, 2 * ROWS), shared[...] & 127, shared[...] >> 7)


def slotted(hitb, rank, vals):
    rows = lax.broadcasted_iota(jnp.int32, (64, LANES), 0).astype(F32)
    mine = jnp.broadcast_to(rank, (64, LANES)) == rows
    left = [jnp.broadcast_to(x, (64, LANES)) for x in vals]
    pieces = []
    for s in range(3):
        pieces.append(jnp.concatenate([jnp.where(mine, x, 0.0).astype(BF) for x in left], 0))
        left = [x - x.astype(BF).astype(F32) for x in left]
    return [hitb] * 3, pieces


def hits_of(owner_row):
    down = lax.broadcasted_iota(jnp.int32, (LANES, LANES), 0)
    return jnp.where(jnp.broadcast_to(owner_row, (LANES, LANES)) == down, 1.0, 0.0)


def slots(owner, master, normal, slot, acc, between):
    acc[...] = jnp.zeros_like(acc)
    down = lax.broadcasted_iota(jnp.int32, (LANES, LANES), 0)
    across = lax.broadcasted_iota(jnp.int32, (LANES, LANES), 1)
    before = jnp.where(down < across, 1.0, 0.0).astype(BF)
    hits = [hits_of(owner[t : t + 1, :]) for t in range(16)]
    counts = jnp.dot(jnp.concatenate([hit.astype(BF) for hit in hits], 0), before, preferred_element_type=F32)
    carry = jnp.zeros((LANES, 1), F32)
    for t, hit in enumerate(hits):
        count = counts[t * LANES : (t + 1) * LANES, :] + carry
        rank = jnp.sum(hit * count, axis=0, keepdims=True)
        carry = carry + jnp.sum(hit, axis=1, keepdims=True)
        slot[t : t + 1, :] = owner[t : t + 1, :] * 64 + rank.astype(jnp.int32)
    for four in range(4):
        hits, pieces = [], []
        for t in range(4 * four, 4 * four + 4):
            vals = [normal[c : c + 1, t * LANES : (t + 1) * LANES] for c in range(3)]
            rank = (slot[t : t + 1, :] & 63).astype(F32)
            one, two = slotted(
                hits_of(owner[t : t + 1, :]).astype(BF), rank, [*vals, master[t : t + 1, :].astype(F32)]
            )
            hits += one
            pieces += two
        between(2 * four)
        between(2 * four + 1)
        acc[...] += lax.dot_general(
            jnp.concatenate(hits, 1), jnp.concatenate(pieces, 1), NT, preferred_element_type=F32
        )


def spans():
    return [(h, min(LANES, PARTS_SIZE - h * LANES)) for h in range(4)]


def every(first, stride, count=LANES):
    return pl.ds(first, count, stride=stride)


def copy_all(srcs, dsts, sems):
    copies = [pltpu.make_async_copy(a, b, sems.at[i]) for i, (a, b) in enumerate(zip(srcs, dsts))]
    for copy in copies:
        copy.start()
    return copies


def first_kernel(*refs):
    srcs = [*refs[:13], refs[7]]
    u, v, fm, mass, idx, inv, cols, shared, internal, send, slave, slot, normal, matv = refs[13:27]
    disp0, vel0, force0, shared0, owner, master, stiff, accel, conn, mat, tab, g, acc, held, small, table, sems = refs[27:]
    dsts = (stiff, owner, master, normal, disp0, vel0, conn, mat, shared0, force0, mass, accel, slave, matv)
    copies = copy_all(srcs, dsts, sems)

    def columns(m):
        for j in range(24):
            cols[m * 24 + j] = jnp.broadcast_to(stiff[m, :, j : j + 1], (24, LANES))

    for copy in copies[:4]:
        copy.wait()
    slots(owner, master, normal, slot, table, columns)
    send[...] = jnp.zeros_like(send)
    send[every(0, 5), :] = table[:, 0:128]
    send[every(1, 5), :] = table[:, 128:256]
    for copy in copies[4:]:
        copy.wait()
    to_rows(disp0, u)
    to_rows(vel0, v)
    to_rows(force0, fm)
    tab[...] = u[...] + DAMP_RATIO * v[...]
    for c in range(3):
        at = slice(c * ROWS, (c + 1) * ROWS)
        fm[at, :] = fm[at, :] / mass[...] - accel[c]
    lane = lax.broadcasted_iota(jnp.int32, (8, LANES), 1)
    for b in range(ROWS):
        at = slice(b * LANES, (b + 1) * LANES)
        idx[:, at] = (conn[:, at] + lane + b * LANES) & 4095
    shared[...] = jnp.zeros_like(shared)
    for b in range(NBR):
        shared[b : b + 1, :] = shared0[b]
    small[...] = jnp.zeros_like(small)
    row = lax.broadcasted_iota(jnp.int32, (8, LANES), 0)
    listed = row < NBR
    lo, hi = shared[...] & 127, shared[...] >> 7
    kept = [jnp.where(listed, lane, 0).astype(F32), jnp.where(listed, row + 1, 0).astype(F32)]
    add_placed(small, lo, hi, kept, held)
    found = (small[0:64, :] + small[64:128, :]).astype(jnp.int32)
    inv[...] = found[0:ROWS, :] + found[ROWS : 2 * ROWS, :] * LANES
    elements(idx, mat, tab, cols, g, acc, held)
    own = finish_internal(acc, internal, shared)
    me = lax.axis_index("dom")
    for b in range(NBR):
        for c in range(3):
            send[pl.ds(5 * (me ^ (1 << b)) + 2 + c, 1), :] = own[c][b : b + 1, :]


def fixed_kernel(*refs):
    pos0, part0, pmass0, pcenter0, pinertia0, normal, shared, mass, pos, part, nrm, light, rigid = refs[:13]
    pos1, pmass, pcenter, pinertia, sems = refs[13:]
    copies = copy_all(
        (pos0, part0, pmass0, pcenter0, pinertia0), (pos1, part, pmass, pcenter, pinertia), sems
    )
    (weight,) = gather(mass, (0,), shared[...] & 127, shared[...] >> 7)
    light[...] = -TIME_STEP / weight
    for t in range(16):
        for c in range(3):
            nrm[16 * c + t : 16 * c + t + 1, :] = normal[c : c + 1, t * LANES : (t + 1) * LANES]
    rigid[...] = jnp.ones_like(rigid)
    for copy in copies:
        copy.wait()
    to_rows(pos1, pos)
    for h, n in spans():
        at = slice(h * LANES, h * LANES + n)
        rigid[h : h + 1, 0:n] = pmass[0:1, at]
        for c in range(3):
            rigid[8 + 8 * c + h : 9 + 8 * c + h, 0:n] = pcenter[c : c + 1, at]
            rigid[32 + 8 * c + h : 33 + 8 * c + h, 0:n] = pinertia[c : c + 1, at]


def from_shared(code, rows):
    total = 0.0
    for b in range(NBR):
        row = jnp.broadcast_to(rows[b], (8, LANES))
        total = total + jnp.where(code >> 7 == b + 1, lanes_of(row, code & 127), 0.0)
    return total


def update(u, v, internal, inv, fm, mass, recv, c, r):
    at = slice(c * ROWS + r, c * ROWS + r + 8)
    total = internal[at, :] + from_shared(inv[r : r + 8, :], [recv[b][c] for b in range(NBR)])
    speed = v[at, :] + TIME_STEP * (fm[at, :] - total / mass[r : r + 8, :])
    return at, u[at, :] + TIME_STEP * speed, speed, total


def rows_of(refs):
    return [[ref[c : c + 1, :] for c in range(3)] for ref in refs]


def next_kernel(from_table, u, v, internal, inv, fm, mass, idx, matv, cols, shared, *rest):
    if from_table:
        got, rest = rest[0], rest[1:]
        me = lax.axis_index("dom")
        recv = [[got[pl.ds(5 * (me ^ (1 << b)) + 2 + c, 1), :] for c in range(3)] for b in range(NBR)]
    else:
        recv, rest = rows_of(rest[:NBR]), rest[NBR:]
    u2, v2, internal2 = rest[:3]
    own = rest[3:8]
    tab, g, acc, held, mat, sem = rest[8:]
    numbers = pltpu.make_async_copy(matv, mat, sem)
    numbers.start()
    for c in range(3):
        for r in range(0, ROWS, 8):
            at, disp, speed, _ = update(u, v, internal, inv, fm, mass, recv, c, r)
            u2[at, :] = disp
            v2[at, :] = speed
            tab[at, :] = disp + DAMP_RATIO * speed
    numbers.wait()
    elements(idx, mat, tab, cols, g, acc, held)
    vals = finish_internal(acc, internal2, shared)
    for b in range(NBR):
        for c in range(3):
            own[b][c : c + 1, :] = vals[c][b : b + 1, :]


def ends_kernel(got, slave, inv, midx, mnrm, code):
    left = lax.broadcasted_iota(jnp.int32, (64, LANES), 1) < 64
    for k, out in ((0, mnrm.at[0]), (1, mnrm.at[1]), (2, mnrm.at[2]), (3, midx)):
        top, low = got[every(k // 2, 5, 64), :], got[every(320 + k // 2, 5, 64), :]
        if k % 2:
            out[...] = jnp.where(left, pltpu.roll(top, 64, 1), low).astype(out.dtype)
        else:
            out[...] = jnp.where(left, top, pltpu.roll(low, 64, 1))
    for r in range(0, 80, 8):
        here = slave[r : r + 8, :] if r < 16 else midx[r - 16 : r - 8, :]
        (code[r : r + 8, :],) = gather(inv, (0,), here & 127, here >> 7)


def base_kernel(u, v, internal, fm, mass, pos, slave, nrm, midx, mnrm, x2, v2, ab, tab):
    for c in range(3):
        for r in range(0, ROWS, 8):
            at = slice(c * ROWS + r, c * ROWS + r + 8)
            speed = v[at, :] + TIME_STEP * (fm[at, :] - internal[at, :] / mass[r : r + 8, :])
            place_now = pos[at, :] + (u[at, :] + TIME_STEP * speed)
            x2[at, :] = place_now
            v2[at, :] = speed
            tab[at, :] = place_now
            tab[c * ROWS + 96 + r : c * ROWS + 96 + r + 8, :] = speed

    def both(here, w):
        y = gather(tab, tuple(range(0, 192, ROWS)), here & 127, here >> 7)
        return y[0] * w[0] + y[1] * w[1] + y[2] * w[2], y[3] * w[0] + y[4] * w[1] + y[5] * w[2]

    for r in (0, 8):
        w = [nrm[16 * c + r : 16 * c + r + 8, :] for c in range(3)]
        ab[0, r : r + 8, :], ab[1, r : r + 8, :] = both(slave[r : r + 8, :], w)

    def step(i, carry):
        for q in range(2):
            at = pl.ds(pl.multiple_of(i * 16 + q * 8, 8), 8)
            to = pl.ds(pl.multiple_of(i * 16 + q * 8 + 16, 8), 8)
            ab[0, to, :], ab[1, to, :] = both(midx[at, :], [mnrm[c, at, :] for c in range(3)])
        return carry

    lax.fori_loop(0, 4, step, 0)


def dots_kernel(x1, v1, ab1, internal, inv, light, fm, mass, part, slot, nrm, mnrm, code, *rest):
    recv = rows_of(rest[:5])
    x2, v2, net, dots, acc, table, ab = rest[5:]
    for c in range(3):
        for r in range(0, ROWS, 8):
            at = slice(c * ROWS + r, c * ROWS + r + 8)
            m = mass[r : r + 8, :]
            more = from_shared(inv[r : r + 8, :], [recv[b][c] for b in range(NBR)])
            change = -TIME_STEP * (more / m)
            x2[at, :] = x1[at, :] + TIME_STEP * change
            v2[at, :] = v1[at, :] + change
            net[at, :] = m * fm[at, :] - internal[at, :] - more
    moved = [[recv[b][c] * light[b : b + 1, :] for b in range(NBR)] for c in range(3)]
    for r in range(0, 80, 8):
        here = code[r : r + 8, :]
        if r < 16:
            w = [nrm[16 * c + r : 16 * c + r + 8, :] for c in range(3)]
        else:
            w = [mnrm[c, r - 16 : r - 8, :] for c in range(3)]
        d = [from_shared(here, moved[c]) for c in range(3)]
        change = d[0] * w[0] + d[1] * w[1] + d[2] * w[2]
        ab[0, r : r + 8, :] = ab1[0, r : r + 8, :] + TIME_STEP * change
        ab[1, r : r + 8, :] = ab1[1, r : r + 8, :] + change

    def vals(r):
        m = mass[r : r + 8, :]
        return [m, *[m * x2[c * ROWS + r : c * ROWS + r + 8, :] for c in range(3)]]

    acc[...] = jnp.zeros_like(acc)
    part_sums(part, vals, acc, True)
    moments = jnp.concatenate([acc[0:32, :] + acc[32:64, :], jnp.zeros((96, LANES), F32)], 0)
    dots[every(2, 3), :] = moments.T
    table[...] = jnp.zeros_like(table)
    for i in range(4):
        hits, pieces = [], []
        for t in range(4 * i, 4 * i + 4):
            here = slot[t : t + 1, :]
            rows = [ab[0, t : t + 1, :], ab[1, t : t + 1, :]]
            one, two = slotted(hits_of(here >> 6).astype(BF), (here & 63).astype(F32), rows)
            hits += one
            pieces += two
        table[...] += lax.dot_general(
            jnp.concatenate(hits, 1), jnp.concatenate(pieces, 1), NT, preferred_element_type=F32
        )
    left = lax.broadcasted_iota(jnp.int32, (64, LANES), 1) < 64
    one, two = ab[0, 16:80, :], ab[1, 16:80, :]
    dots[every(0, 3), :] = table[...]
    dots[every(1, 3, 64), :] = jnp.where(left, one, pltpu.roll(two, 64, 1))
    dots[every(193, 3, 64), :] = jnp.where(left, pltpu.roll(one, 64, 1), two)


def part_sums(part, vals, acc, by_device):
    it = iota_rows(LANES)
    it8 = (lax.broadcasted_iota(jnp.int32, (16, LANES), 0) & 7).astype(F32).astype(BF)
    one, zero = jnp.ones((LANES, LANES), BF), jnp.zeros((LANES, LANES), BF)
    for r in range(0, ROWS, 8):
        here = part[r : r + 8, :]
        lo = here & 127
        if by_device:
            lo = ((lo & 63) << 1) | (lo >> 6)
        lof, hif = lo.astype(F32), (here >> 7).astype(F32)
        val = vals(r)
        first = [x.astype(BF).astype(F32) for x in val]
        split = (first, [x - y for x, y in zip(val, first)])
        left, right = [], []
        for a in range(8):
            right.append(jnp.where(wide(lof, a, LANES) == it, one, zero))
            mask = wide(hif, a, 16) == it8
            rows = []
            for s in range(2):
                for k in range(0, len(val), 2):
                    two = [jnp.broadcast_to(split[s][k + d][a : a + 1, :], (8, LANES)) for d in range(2)]
                    rows.append(jnp.where(mask, jnp.concatenate(two, 0).astype(BF), zero[:16]))
            left.append(jnp.concatenate(rows, 0))
        acc[...] += lax.dot_general(
            jnp.concatenate(left, 1), jnp.concatenate(right, 1), NT, preferred_element_type=F32
        )


def contact_kernel(
    dots, got, slave, slot, nrm, midx, mnrm, x, net, part, contact, keep, give, acc, tot, acc2, push, mine, held
):
    acc[...] = jnp.zeros_like(acc)
    acc2[...] = jnp.zeros_like(acc2)
    left = lax.broadcasted_iota(jnp.int32, (LANES, LANES), 1) < 64
    as_slave = dots[every(0, 3), :] - got[every(1, 3), :]
    as_master = got[every(0, 3), :] - dots[every(1, 3), :]
    gap = jnp.where(left, as_slave, pltpu.roll(as_master, 64, 1))
    closing = jnp.where(left, pltpu.roll(as_slave, 64, 1), as_master)
    z = -gap / GAP_WIDTH
    soft = jnp.maximum(z, 0.0) + jnp.log1p(jnp.exp(-jnp.abs(z)))
    size = PENALTY * GAP_WIDTH * soft - CONTACT_DAMP * closing
    top, low = size[0:64, :], size[64:128, :]
    mine[...] = jnp.where(left[0:64, :], top, pltpu.roll(low, 64, 1))
    push[...] = -jnp.where(left[0:64, :], pltpu.roll(top, 64, 1), low)

    def step(i, carry):
        one, two = [], []
        for q in range(4):
            at = pl.ds(pl.multiple_of(i * 32 + q * 8, 8), 8)
            here, size = midx[at, :], push[at, :]
            pair = place(here & 127, here >> 7, [size * mnrm[c, at, :] for c in range(3)], held, 64 * q)
            one.append(pair[0])
            two.append(pair[1])
        acc[...] += lax.dot_general(
            jnp.concatenate(one, 1), jnp.concatenate(two, 1), NT, preferred_element_type=F32
        )
        return carry

    lax.fori_loop(0, 2, step, 0)
    one, two = [], []
    for r in (0, 8):
        here, at = slave[r : r + 8, :], slot[r : r + 8, :]
        (size,) = gather(mine, (0,), ((at >> 12) << 6) + (at & 63), (at >> 6) & 63, 64)
        w = [size * nrm[16 * c + r : 16 * c + r + 8, :] for c in range(3)]
        pair = place(here & 127, here >> 7, w, held, 256 + 8 * r)
        one.append(pair[0])
        two.append(pair[1])
    acc[...] += lax.dot_general(
        jnp.concatenate(one, 1), jnp.concatenate(two, 1), NT, preferred_element_type=F32
    )
    contact[...] = acc[0:96, :] + acc[96:192, :]
    tot[...] = net[...] + contact[...]

    def vals(r):
        p = [x[c * ROWS + r : c * ROWS + r + 8, :] for c in range(3)]
        n = [tot[c * ROWS + r : c * ROWS + r + 8, :] for c in range(3)]
        return [
            *n,
            p[1] * n[2] - p[2] * n[1],
            p[2] * n[0] - p[0] * n[2],
            p[0] * n[1] - p[1] * n[0],
        ]

    part_sums(part, vals, acc2, False)
    acc2[0:48, :] = acc2[0:48, :] + acc2[48:96, :]
    lane = lax.broadcasted_iota(jnp.int32, (8, LANES), 1)
    last = jnp.zeros((8, LANES), F32)
    for k in range(6):
        piece = jnp.where(lane < 16, acc2[8 * k : 8 * k + 8, :], 0.0)
        last = last + (pltpu.roll(piece, 16 * k, 1) if k else piece)
    even = lax.axis_index("dom") & 1 == 0
    pairs = [(acc2[8 * k : 8 * k + 1, :], acc2[8 * k + 2 : 8 * k + 3, :]) for k in range(6)]
    pairs += [(acc2[8 * k + 1 : 8 * k + 2, :], acc2[8 * k + 25 : 8 * k + 26, :]) for k in range(3)]
    pairs += [(jnp.zeros((1, LANES), F32), last[3:4, :])]
    for k, (low, high) in enumerate(pairs):
        keep[k : k + 1, :] = jnp.where(even, low, high)
        give[k : k + 1, :] = jnp.where(even, high, low)
    keep[10:16, :] = jnp.zeros((6, LANES), F32)
    give[10:16, :] = jnp.zeros((6, LANES), F32)
    moments = jnp.broadcast_to(jnp.sum(got[every(2, 3), :], axis=0, keepdims=True), (8, LANES))
    moments = jnp.where(lane < 96, 0.0, pltpu.roll(moments, 96, 1))
    keep[9:10, :] = keep[9:10, :] + moments[0:1, :]


def nodal_kernel(v, contact, mass, nodal):
    for c in range(3):
        at = slice(c * ROWS, (c + 1) * ROWS)
        speed = v[at, :] + TIME_STEP * contact[at, :] / mass[...]
        for h in range(ROWS):
            nodal[c : c + 1, h * LANES : (h + 1) * LANES] = speed[h : h + 1, :]


def spread_kernel(keep, given, out):
    tile = (keep[...] + given[...])[0:10, :]
    four = jnp.concatenate([tile] * 4, 0)
    for k in range(16):
        out[40 * k : 40 * k + 40, :] = four


def total_kernel(got, out):
    four = got[0:40, :]
    for k in range(1, 16):
        four = four + got[40 * k : 40 * k + 40, :]
    out[0:10, :] = four[0:10, :] + four[10:20, :] + four[20:30, :] + four[30:40, :]
    out[10:16, :] = jnp.zeros((6, LANES), F32)
    out[16:80, :] = pltpu.roll(got[every(9, 10, 64), :], 32, 1)


def motion_kernel(mine, other, rigid, out):
    even = lax.axis_index("dom") & 1 == 0
    low = jnp.where(even, mine[...], other[...])
    high = jnp.where(even, other[...], mine[...])
    by = jnp.concatenate([low[16:80, :], high[16:80, :]], 0).T
    moments = [by[8 * k : 8 * k + 4, :] for k in range(4)]
    sums = []
    for k in range(6):
        second = low[6 + k : 7 + k, :] if k < 3 else high[3 + k : 4 + k, :]
        last = pltpu.roll(high[8:16, :], LANES - 16 * k, 1) if k else high[8:16, :]
        sums.append(jnp.concatenate([low[k : k + 1, :], second, high[k : k + 1, :], last[1:2, :]], 0))
    own = rigid[0:4, :]
    mass = own + moments[0]
    centre = [(own * rigid[8 + 8 * c : 12 + 8 * c, :] + moments[1 + c]) / mass for c in range(3)]
    force, turn = sums[0:3], sums[3:6]
    rows = [y / mass for y in force]
    for c in range(3):
        a, b = (c + 1) % 3, (c + 2) % 3
        moment = turn[c] - (centre[a] * force[b] - centre[b] * force[a])
        rows.append(moment / rigid[32 + 8 * c : 36 + 8 * c, :])
    for r, row in enumerate(rows):
        for h, n in spans():
            out[r : r + 1, h * LANES : h * LANES + n] = row[h : h + 1, 0:n]


def partner(block, apart):
    count = lax.axis_size("dom")
    return lax.ppermute(block, "dom", [(i, i ^ (1 << apart)) for i in range(count)])


def in_hbm(*arrays):
    return [pltpu.with_memory_space_constraint(x, pltpu.HBM) for x in arrays]


def later(value, than):
    return lax.optimization_barrier((value, than))[0]


def swap(block, groups=None):
    peers = len(groups[0]) if groups else lax.axis_size("dom")
    flat = block.reshape(peers, 1, -1)
    return lax.all_to_all(flat, "dom", 0, 0, tiled=True, axis_index_groups=groups).reshape(block.shape)


def per_device(
    rest_pos,
    displacement,
    velocity,
    ext_force,
    node_mass,
    body_accel,
    connectivity,
    elem_material,
    stiffness,
    shared_nodes,
    contact_slave,
    contact_owner,
    contact_master,
    contact_normal,
    part_of_node,
    part_mass,
    part_center,
    part_inertia,
):
    state = ((96, LANES), F32)
    table = ((5 * LANES, LANES), F32)
    own = [((3, LANES), F32)] * NBR
    work = [
        pltpu.VMEM((96, LANES), F32),
        pltpu.VMEM((24 * TOGETHER, LANES), F32),
        pltpu.VMEM((192, LANES), F32),
        pltpu.VMEM((64 * TOGETHER, LANES), F32),
    ]
    inputs = (
        stiffness,
        contact_owner.reshape(16, LANES),
        contact_master.reshape(16, LANES),
        contact_normal,
        displacement,
        velocity,
        connectivity,
        elem_material,
        shared_nodes.transpose(1, 0, 2),
        ext_force,
        node_mass.reshape(ROWS, LANES),
        body_accel,
        contact_slave.reshape(16, LANES),
    )
    rows, ints = ((ROWS, LANES), F32), jnp.int32
    whole, map_rows = pltpu.VMEM((3, 4096), F32), ((ROWS, LANES), ints)
    u, v, fm, mass, idx, inv, cols, shared, internal, send, slave, slot, normal, mat = call(
        first_kernel,
        [
            state,
            state,
            state,
            rows,
            ((8, 4096), ints),
            map_rows,
            ((192, 24, LANES), F32),
            ((8, LANES), ints),
            state,
            table,
            ((16, LANES), ints),
            ((16, LANES), ints),
            ((3, 2048), F32),
            ((ROWS,), ints),
        ],
        [HBM] * 13,
        "first_cycle",
        [
            whole,
            whole,
            whole,
            pltpu.VMEM((NBR, 1, LANES), ints),
            pltpu.VMEM((16, LANES), ints),
            pltpu.VMEM((16, LANES), ints),
            pltpu.VMEM((8, 24, 24), F32),
            pltpu.SMEM((3,), F32),
            pltpu.VMEM((8, 4096), ints),
            pltpu.SMEM((ROWS,), ints),
            *work,
            pltpu.VMEM((LANES, LANES), F32),
            pltpu.VMEM((LANES, 2 * LANES), F32),
            pltpu.SemaphoreType.DMA((14,)),
        ],
    )(*in_hbm(*inputs))
    got = swap(send)
    trio = ((3, PARTS_SIZE), F32)
    recv = [got]
    for n in range(CYCLES - 1):
        u, v, internal, *mine = call(
            functools.partial(next_kernel, n == 0),
            [state, state, state, *own],
            [VMEM] * (10 + len(recv)),
            "next_cycle",
            [*work, pltpu.SMEM((ROWS,), ints), pltpu.SemaphoreType.DMA],
        )(u, v, internal, inv, fm, mass, idx, mat, cols, shared, *recv)
        recv = [partner(mine[b], b) for b in range(NBR)]
        if n == 0:
            midx, mnrm, code = call(
                ends_kernel,
                [((64, LANES), ints), ((3, 64, LANES), F32), ((80, LANES), ints)],
                [VMEM] * 3,
                "contact_ends",
            )(later(got, mine), slave, inv)
            pos, part, nrm, light, rigid = call(
                fixed_kernel,
                [state, map_rows, ((48, LANES), F32), ((8, LANES), F32), ((56, LANES), F32)],
                [HBM] * 5 + [VMEM] * 3,
                "fixed_data",
                [
                    whole,
                    pltpu.VMEM((1, PARTS_SIZE), F32),
                    pltpu.VMEM(*trio),
                    pltpu.VMEM(*trio),
                    pltpu.SemaphoreType.DMA((5,)),
                ],
            )(
                *in_hbm(
                    rest_pos,
                    part_of_node.reshape(ROWS, LANES),
                    part_mass.reshape(1, PARTS_SIZE),
                    part_center,
                    part_inertia,
                ),
                later(normal, mine),
                shared,
                mass,
            )
            recv, code, nrm = lax.optimization_barrier((recv, code, nrm))
    both = ((2, 80, LANES), F32)
    x, v, ab = call(
        base_kernel,
        [state, state, both],
        [VMEM] * 10,
        "contact_base",
        [pltpu.VMEM((192, LANES), F32)],
    )(u, v, internal, fm, mass, pos, slave, nrm, midx, mnrm)
    x, v, net, dots = call(
        dots_kernel,
        [state, state, state, ((3 * LANES, LANES), F32)],
        [VMEM] * 18,
        "contact_dots",
        [pltpu.VMEM((64, LANES), F32), pltpu.VMEM((LANES, LANES), F32), pltpu.VMEM(*both)],
    )(x, v, ab, internal, inv, light, fm, mass, part, slot, nrm, mnrm, code, *recv)
    half = ((16, LANES), F32)
    contact, keep, give = call(
        contact_kernel,
        [state, half, half],
        [VMEM] * 10,
        "contact_forces",
        [
            pltpu.VMEM((192, LANES), F32),
            pltpu.VMEM((96, LANES), F32),
            pltpu.VMEM((96, LANES), F32),
            pltpu.VMEM((64, LANES), F32),
            pltpu.VMEM((64, LANES), F32),
            pltpu.VMEM((384, LANES), F32),
        ],
    )(dots, swap(dots), slave, slot, nrm, midx, mnrm, x, net, part)
    (nodal_velocity,) = call(nodal_kernel, [((3, 4096), F32)], [VMEM] * 3, "nodal_velocity")(v, contact, mass)
    (spread,) = call(spread_kernel, [((640, LANES), F32)], [VMEM] * 2, "part_spread")(keep, partner(give, 0))
    chips = lax.axis_size("dom") // 2
    groups = [[2 * i + core for i in range(chips)] for core in range(2)]
    (total,) = call(total_kernel, [((80, LANES), F32)], [VMEM], "part_totals")(swap(spread, groups))
    (motion,) = call(motion_kernel, [((6, PARTS_SIZE), F32)], [VMEM] * 3, "part_motion")(
        total, partner(total, 0), rigid
    )
    return nodal_velocity, motion


def solution(mesh):
    placed = (
        P(None, "dom"),
        P(None, "dom"),
        P(None, "dom"),
        P(None, "dom"),
        P("dom"),
        P(),
        P(None, "dom"),
        P("dom"),
        P(),
        P("dom", None, None),
        P("dom"),
        P("dom", None),
        P("dom"),
        P(None, "dom"),
        P("dom"),
        P(),
        P(),
        P(),
    )
    return jax.shard_map(
        per_device, mesh=mesh, in_specs=placed, out_specs=(P(None, "dom"), P()), check_vma=False
    )
```

```python
import functools

import jax
import jax.numpy as jnp
from jax import lax
from jax.experimental import pallas as pl
from jax.experimental.pallas import tpu as pltpu
from jax.sharding import PartitionSpec as P

CYCLES = 3
PARTS_SIZE = 400

TIME_STEP = 0.1
DAMP_RATIO = 0.05
PENALTY = 2.0
GAP_WIDTH = 0.5
CONTACT_DAMP = 0.2

BF = jnp.bfloat16
F32 = jnp.float32
NT = (((1,), (1,)), ((), ()))
LANES = 128
ROWS = 32
NBR = 5
TOGETHER = 16
AHEAD = 2

VMEM = pl.BlockSpec(memory_space=pltpu.VMEM)
SMEM = pl.BlockSpec(memory_space=pltpu.SMEM)
HBM = pl.BlockSpec(memory_space=pltpu.HBM)


def call(body, outs, in_specs, name, scratch=(), flops=0):
    return pl.pallas_call(
        body,
        out_shape=[jax.ShapeDtypeStruct(s, d) for s, d in outs],
        in_specs=in_specs,
        out_specs=[VMEM] * len(outs),
        scratch_shapes=list(scratch),
        compiler_params=pltpu.CompilerParams(vmem_limit_bytes=40 << 20),
        cost_estimate=pl.CostEstimate(flops=flops, bytes_accessed=1 << 20, transcendentals=0),
        name=name,
    )


def lanes_of(row, idx):
    return jnp.take_along_axis(row, idx, axis=1, mode="promise_in_bounds")


def gather(tab, bases, lo, hi, rows=ROWS):
    acc = [None] * len(bases)
    for h in range(rows):
        here = hi == h
        for c, base in enumerate(bases):
            row = jnp.broadcast_to(tab[base + h : base + h + 1, :], (8, LANES))
            val = lanes_of(row, lo)
            acc[c] = val if h == 0 else jnp.where(here, val, acc[c])
    return acc


def wide(x, a, n):
    row = jnp.broadcast_to(x[a : a + 1, :].astype(F32), (16, LANES)).astype(BF)
    return jnp.concatenate([row] * (n // 16), 0)


def iota_rows(n):
    return lax.broadcasted_iota(jnp.int32, (n, LANES), 0).astype(F32).astype(BF)


def place(lo, hi, vals, held, base):
    it = iota_rows(LANES)
    one, zero = jnp.ones((LANES, LANES), BF), jnp.zeros((LANES, LANES), BF)
    first = [v.astype(BF).astype(F32) for v in vals]
    items = first + [v - x for v, x in zip(vals, first)] + [lo.astype(F32), hi.astype(F32)]
    for k, x in enumerate(items):
        held[base + 8 * k : base + 8 * k + 8, :] = x

    def spread(k, a, n):
        at = base + 8 * k + a
        row = jnp.broadcast_to(held[at : at + 1, :], (16, LANES)).astype(BF)
        return jnp.concatenate([row] * (n // 16), 0)

    left, right = [], []
    count = 2 * len(vals)
    for a in range(8):
        right.append(jnp.where(spread(count, a, LANES) == it, one, zero))
        mask = spread(count + 1, a, ROWS) == it[:ROWS]
        left.append(jnp.concatenate([jnp.where(mask, spread(k, a, ROWS), zero[:ROWS]) for k in range(count)], 0))
    return jnp.concatenate(left, 1), jnp.concatenate(right, 1)


def add_placed(acc, lo, hi, vals, held):
    left, right = place(lo, hi, vals, held, 0)
    acc[...] += lax.dot_general(left, right, NT, preferred_element_type=F32)


def to_rows(src, dst):
    for c in range(3):
        for h in range(ROWS):
            dst[c * ROWS + h : c * ROWS + h + 1, :] = src[c : c + 1, h * LANES : (h + 1) * LANES]


def elements(idx, mat, tab, cols, g, acc, held):
    acc[...] = jnp.zeros_like(acc)

    def corners(b):
        here = idx[:, pl.ds(pl.multiple_of(b * LANES, LANES), LANES)]
        return here & 127, here >> 7

    def fetch(b):
        return gather(tab, (0, ROWS, 2 * ROWS), *corners(b & (ROWS - 1)))

    def step(i, vals):
        vals = list(vals)
        left, right = [], []
        for q in range(TOGETHER):
            b = i * TOGETHER + q
            vals += fetch(b + AHEAD)
            for c in range(3):
                g[q * 24 + 8 * c : q * 24 + 8 * c + 8, :] = vals[c]
            vals = vals[3:]
            first = mat[b] * 24
            force = [jnp.zeros((8, LANES), F32)] * 3
            for j in range(24):
                col = cols.at[first + j]
                row = jnp.broadcast_to(g[q * 24 + j : q * 24 + j + 1, :], (8, LANES))
                force = [force[c] + col[8 * c : 8 * c + 8, :] * row for c in range(3)]
            one, two = place(*corners(b), force, held, 64 * q)
            left.append(one)
            right.append(two)
        acc[...] += lax.dot_general(
            jnp.concatenate(left, 1), jnp.concatenate(right, 1), NT, preferred_element_type=F32
        )
        return tuple(vals)

    lax.fori_loop(0, ROWS // TOGETHER, step, tuple(x for b in range(AHEAD) for x in fetch(b)))


def finish_internal(acc, internal, shared):
    internal[...] = acc[0:96, :] + acc[96:192, :]
    return gather(internal, (0, ROWS, 2 * ROWS), shared[...] & 127, shared[...] >> 7)


def slotted(hitb, rank, vals):
    rows = lax.broadcasted_iota(jnp.int32, (64, LANES), 0).astype(F32)
    mine = jnp.broadcast_to(rank, (64, LANES)) == rows
    left = [jnp.broadcast_to(x, (64, LANES)) for x in vals]
    pieces = []
    for s in range(3):
        pieces.append(jnp.concatenate([jnp.where(mine, x, 0.0).astype(BF) for x in left], 0))
        left = [x - x.astype(BF).astype(F32) for x in left]
    return [hitb] * 3, pieces


def hits_of(owner_row):
    down = lax.broadcasted_iota(jnp.int32, (LANES, LANES), 0)
    return jnp.where(jnp.broadcast_to(owner_row, (LANES, LANES)) == down, 1.0, 0.0)


def slots(owner, master, normal, slot, acc, between):
    acc[...] = jnp.zeros_like(acc)
    down = lax.broadcasted_iota(jnp.int32, (LANES, LANES), 0)
    across = lax.broadcasted_iota(jnp.int32, (LANES, LANES), 1)
    before = jnp.where(down < across, 1.0, 0.0).astype(BF)
    hits = [hits_of(owner[t : t + 1, :]) for t in range(16)]
    counts = jnp.dot(jnp.concatenate([hit.astype(BF) for hit in hits], 0), before, preferred_element_type=F32)
    carry = jnp.zeros((LANES, 1), F32)
    for t, hit in enumerate(hits):
        count = counts[t * LANES : (t + 1) * LANES, :] + carry
        rank = jnp.sum(hit * count, axis=0, keepdims=True)
        carry = carry + jnp.sum(hit, axis=1, keepdims=True)
        slot[t : t + 1, :] = owner[t : t + 1, :] * 64 + rank.astype(jnp.int32)
    for four in range(4):
        hits, pieces = [], []
        for t in range(4 * four, 4 * four + 4):
            vals = [normal[c : c + 1, t * LANES : (t + 1) * LANES] for c in range(3)]
            rank = (slot[t : t + 1, :] & 63).astype(F32)
            one, two = slotted(
                hits_of(owner[t : t + 1, :]).astype(BF), rank, [*vals, master[t : t + 1, :].astype(F32)]
            )
            hits += one
            pieces += two
        between(2 * four)
        between(2 * four + 1)
        acc[...] += lax.dot_general(
            jnp.concatenate(hits, 1), jnp.concatenate(pieces, 1), NT, preferred_element_type=F32
        )


def spans():
    return [(h, min(LANES, PARTS_SIZE - h * LANES)) for h in range(4)]


def every(first, stride, count=LANES):
    return pl.ds(first, count, stride=stride)


def copy_all(srcs, dsts, sems):
    copies = [pltpu.make_async_copy(a, b, sems.at[i]) for i, (a, b) in enumerate(zip(srcs, dsts))]
    for copy in copies:
        copy.start()
    return copies


def first_kernel(*refs):
    srcs = [*refs[:13], refs[7]]
    u, v, fm, mass, idx, inv, cols, shared, internal, send, slave, slot, normal, matv = refs[13:27]
    disp0, vel0, force0, shared0, owner, master, stiff, accel, conn, mat, tab, g, acc, held, small, table, sems = refs[27:]
    dsts = (stiff, owner, master, normal, disp0, vel0, conn, mat, shared0, force0, mass, accel, slave, matv)
    copies = copy_all(srcs, dsts, sems)

    def columns(m):
        for j in range(24):
            cols[m * 24 + j] = jnp.broadcast_to(stiff[m, :, j : j + 1], (24, LANES))

    for copy in copies[:4]:
        copy.wait()
    slots(owner, master, normal, slot, table, columns)
    send[...] = jnp.zeros_like(send)
    send[every(0, 5), :] = table[:, 0:128]
    send[every(1, 5), :] = table[:, 128:256]
    for copy in copies[4:]:
        copy.wait()
    to_rows(disp0, u)
    to_rows(vel0, v)
    to_rows(force0, fm)
    tab[...] = u[...] + DAMP_RATIO * v[...]
    for c in range(3):
        at = slice(c * ROWS, (c + 1) * ROWS)
        fm[at, :] = fm[at, :] / mass[...] - accel[c]
    lane = lax.broadcasted_iota(jnp.int32, (8, LANES), 1)
    for b in range(ROWS):
        at = slice(b * LANES, (b + 1) * LANES)
        idx[:, at] = (conn[:, at] + lane + b * LANES) & 4095
    shared[...] = jnp.zeros_like(shared)
    for b in range(NBR):
        shared[b : b + 1, :] = shared0[b]
    small[...] = jnp.zeros_like(small)
    row = lax.broadcasted_iota(jnp.int32, (8, LANES), 0)
    listed = row < NBR
    lo, hi = shared[...] & 127, shared[...] >> 7
    kept = [jnp.where(listed, lane, 0).astype(F32), jnp.where(listed, row + 1, 0).astype(F32)]
    add_placed(small, lo, hi, kept, held)
    found = (small[0:64, :] + small[64:128, :]).astype(jnp.int32)
    inv[...] = found[0:ROWS, :] + found[ROWS : 2 * ROWS, :] * LANES
    elements(idx, mat, tab, cols, g, acc, held)
    own = finish_internal(acc, internal, shared)
    me = lax.axis_index("dom")
    for b in range(NBR):
        for c in range(3):
            send[pl.ds(5 * (me ^ (1 << b)) + 2 + c, 1), :] = own[c][b : b + 1, :]


def fixed_kernel(*refs):
    pos0, part0, pmass0, pcenter0, pinertia0, normal, shared, mass, pos, part, nrm, light, rigid = refs[:13]
    pos1, pmass, pcenter, pinertia, sems = refs[13:]
    copies = copy_all(
        (pos0, part0, pmass0, pcenter0, pinertia0), (pos1, part, pmass, pcenter, pinertia), sems
    )
    (weight,) = gather(mass, (0,), shared[...] & 127, shared[...] >> 7)
    light[...] = -TIME_STEP / weight
    for t in range(16):
        for c in range(3):
            nrm[16 * c + t : 16 * c + t + 1, :] = normal[c : c + 1, t * LANES : (t + 1) * LANES]
    rigid[...] = jnp.ones_like(rigid)
    for copy in copies:
        copy.wait()
    to_rows(pos1, pos)
    for h, n in spans():
        at = slice(h * LANES, h * LANES + n)
        rigid[h : h + 1, 0:n] = pmass[0:1, at]
        for c in range(3):
            rigid[8 + 8 * c + h : 9 + 8 * c + h, 0:n] = pcenter[c : c + 1, at]
            rigid[32 + 8 * c + h : 33 + 8 * c + h, 0:n] = pinertia[c : c + 1, at]


def from_shared(code, rows):
    total = 0.0
    for b in range(NBR):
        row = jnp.broadcast_to(rows[b], (8, LANES))
        total = total + jnp.where(code >> 7 == b + 1, lanes_of(row, code & 127), 0.0)
    return total


def update(u, v, internal, inv, fm, mass, recv, c, r):
    at = slice(c * ROWS + r, c * ROWS + r + 8)
    total = internal[at, :] + from_shared(inv[r : r + 8, :], [recv[b][c] for b in range(NBR)])
    speed = v[at, :] + TIME_STEP * (fm[at, :] - total / mass[r : r + 8, :])
    return at, u[at, :] + TIME_STEP * speed, speed, total


def rows_of(refs):
    return [[ref[c : c + 1, :] for c in range(3)] for ref in refs]


def next_kernel(from_table, u, v, internal, inv, fm, mass, idx, matv, cols, shared, *rest):
    if from_table:
        got, rest = rest[0], rest[1:]
        me = lax.axis_index("dom")
        recv = [[got[pl.ds(5 * (me ^ (1 << b)) + 2 + c, 1), :] for c in range(3)] for b in range(NBR)]
    else:
        recv, rest = rows_of(rest[:NBR]), rest[NBR:]
    u2, v2, internal2 = rest[:3]
    own = rest[3:8]
    tab, g, acc, held, mat, sem = rest[8:]
    numbers = pltpu.make_async_copy(matv, mat, sem)
    numbers.start()
    for c in range(3):
        for r in range(0, ROWS, 8):
            at, disp, speed, _ = update(u, v, internal, inv, fm, mass, recv, c, r)
            u2[at, :] = disp
            v2[at, :] = speed
            tab[at, :] = disp + DAMP_RATIO * speed
    numbers.wait()
    elements(idx, mat, tab, cols, g, acc, held)
    vals = finish_internal(acc, internal2, shared)
    for b in range(NBR):
        for c in range(3):
            own[b][c : c + 1, :] = vals[c][b : b + 1, :]


def ends_kernel(got, slave, inv, midx, mnrm, code):
    left = lax.broadcasted_iota(jnp.int32, (64, LANES), 1) < 64
    for k, out in ((0, mnrm.at[0]), (1, mnrm.at[1]), (2, mnrm.at[2]), (3, midx)):
        top, low = got[every(k // 2, 5, 64), :], got[every(320 + k // 2, 5, 64), :]
        if k % 2:
            out[...] = jnp.where(left, pltpu.roll(top, 64, 1), low).astype(out.dtype)
        else:
            out[...] = jnp.where(left, top, pltpu.roll(low, 64, 1))
    for r in range(0, 80, 8):
        here = slave[r : r + 8, :] if r < 16 else midx[r - 16 : r - 8, :]
        (code[r : r + 8, :],) = gather(inv, (0,), here & 127, here >> 7)


def base_kernel(u, v, internal, fm, mass, pos, slave, nrm, midx, mnrm, x2, v2, ab, tab):
    for c in range(3):
        for r in range(0, ROWS, 8):
            at = slice(c * ROWS + r, c * ROWS + r + 8)
            speed = v[at, :] + TIME_STEP * (fm[at, :] - internal[at, :] / mass[r : r + 8, :])
            place_now = pos[at, :] + (u[at, :] + TIME_STEP * speed)
            x2[at, :] = place_now
            v2[at, :] = speed
            tab[at, :] = place_now
            tab[c * ROWS + 96 + r : c * ROWS + 96 + r + 8, :] = speed

    def both(here, w):
        y = gather(tab, tuple(range(0, 192, ROWS)), here & 127, here >> 7)
        return y[0] * w[0] + y[1] * w[1] + y[2] * w[2], y[3] * w[0] + y[4] * w[1] + y[5] * w[2]

    for r in (0, 8):
        w = [nrm[16 * c + r : 16 * c + r + 8, :] for c in range(3)]
        ab[0, r : r + 8, :], ab[1, r : r + 8, :] = both(slave[r : r + 8, :], w)

    def step(i, carry):
        for q in range(2):
            at = pl.ds(pl.multiple_of(i * 16 + q * 8, 8), 8)
            to = pl.ds(pl.multiple_of(i * 16 + q * 8 + 16, 8), 8)
            ab[0, to, :], ab[1, to, :] = both(midx[at, :], [mnrm[c, at, :] for c in range(3)])
        return carry

    lax.fori_loop(0, 4, step, 0)


def dots_kernel(x1, v1, ab1, internal, inv, light, fm, mass, part, slot, nrm, mnrm, code, *rest):
    recv = rows_of(rest[:5])
    x2, v2, net, dots, acc, table, ab = rest[5:]
    for c in range(3):
        for r in range(0, ROWS, 8):
            at = slice(c * ROWS + r, c * ROWS + r + 8)
            m = mass[r : r + 8, :]
            more = from_shared(inv[r : r + 8, :], [recv[b][c] for b in range(NBR)])
            change = -TIME_STEP * (more / m)
            x2[at, :] = x1[at, :] + TIME_STEP * change
            v2[at, :] = v1[at, :] + change
            net[at, :] = m * fm[at, :] - internal[at, :] - more
    moved = [[recv[b][c] * light[b : b + 1, :] for b in range(NBR)] for c in range(3)]
    for r in range(0, 80, 8):
        here = code[r : r + 8, :]
        if r < 16:
            w = [nrm[16 * c + r : 16 * c + r + 8, :] for c in range(3)]
        else:
            w = [mnrm[c, r - 16 : r - 8, :] for c in range(3)]
        d = [from_shared(here, moved[c]) for c in range(3)]
        change = d[0] * w[0] + d[1] * w[1] + d[2] * w[2]
        ab[0, r : r + 8, :] = ab1[0, r : r + 8, :] + TIME_STEP * change
        ab[1, r : r + 8, :] = ab1[1, r : r + 8, :] + change

    def vals(r):
        m = mass[r : r + 8, :]
        return [m, *[m * x2[c * ROWS + r : c * ROWS + r + 8, :] for c in range(3)]]

    acc[...] = jnp.zeros_like(acc)
    part_sums(part, vals, acc, True)
    moments = jnp.concatenate([acc[0:32, :] + acc[32:64, :], jnp.zeros((96, LANES), F32)], 0)
    dots[every(2, 3), :] = moments.T
    table[...] = jnp.zeros_like(table)
    for i in range(4):
        hits, pieces = [], []
        for t in range(4 * i, 4 * i + 4):
            here = slot[t : t + 1, :]
            rows = [ab[0, t : t + 1, :], ab[1, t : t + 1, :]]
            one, two = slotted(hits_of(here >> 6).astype(BF), (here & 63).astype(F32), rows)
            hits += one
            pieces += two
        table[...] += lax.dot_general(
            jnp.concatenate(hits, 1), jnp.concatenate(pieces, 1), NT, preferred_element_type=F32
        )
    left = lax.broadcasted_iota(jnp.int32, (64, LANES), 1) < 64
    one, two = ab[0, 16:80, :], ab[1, 16:80, :]
    dots[every(0, 3), :] = table[...]
    dots[every(1, 3, 64), :] = jnp.where(left, one, pltpu.roll(two, 64, 1))
    dots[every(193, 3, 64), :] = jnp.where(left, pltpu.roll(one, 64, 1), two)


def part_sums(part, vals, acc, by_device):
    it = iota_rows(LANES)
    it8 = (lax.broadcasted_iota(jnp.int32, (16, LANES), 0) & 7).astype(F32).astype(BF)
    one, zero = jnp.ones((LANES, LANES), BF), jnp.zeros((LANES, LANES), BF)
    for r in range(0, ROWS, 8):
        here = part[r : r + 8, :]
        lo = here & 127
        if by_device:
            lo = ((lo & 63) << 1) | (lo >> 6)
        lof, hif = lo.astype(F32), (here >> 7).astype(F32)
        val = vals(r)
        first = [x.astype(BF).astype(F32) for x in val]
        split = (first, [x - y for x, y in zip(val, first)])
        left, right = [], []
        for a in range(8):
            right.append(jnp.where(wide(lof, a, LANES) == it, one, zero))
            mask = wide(hif, a, 16) == it8
            rows = []
            for s in range(2):
                for k in range(0, len(val), 2):
                    two = [jnp.broadcast_to(split[s][k + d][a : a + 1, :], (8, LANES)) for d in range(2)]
                    rows.append(jnp.where(mask, jnp.concatenate(two, 0).astype(BF), zero[:16]))
            left.append(jnp.concatenate(rows, 0))
        acc[...] += lax.dot_general(
            jnp.concatenate(left, 1), jnp.concatenate(right, 1), NT, preferred_element_type=F32
        )


def contact_kernel(
    dots, got, slave, slot, nrm, midx, mnrm, x, net, part, contact, keep, give, acc, tot, acc2, push, mine, held
):
    acc2[...] = jnp.zeros_like(acc2)
    left = lax.broadcasted_iota(jnp.int32, (LANES, LANES), 1) < 64
    as_slave = dots[every(0, 3), :] - got[every(1, 3), :]
    as_master = got[every(0, 3), :] - dots[every(1, 3), :]
    gap = jnp.where(left, as_slave, pltpu.roll(as_master, 64, 1))
    closing = jnp.where(left, pltpu.roll(as_slave, 64, 1), as_master)
    z = -gap / GAP_WIDTH
    soft = jnp.maximum(z, 0.0) + jnp.log1p(jnp.exp(-jnp.abs(z)))
    size = PENALTY * GAP_WIDTH * soft - CONTACT_DAMP * closing
    top, low = size[0:64, :], size[64:128, :]
    mine[...] = jnp.where(left[0:64, :], top, pltpu.roll(low, 64, 1))
    push[...] = -jnp.where(left[0:64, :], pltpu.roll(top, 64, 1), low)

    blocks = []
    for r in range(0, 64, 8):
        here, at = midx[r : r + 8, :], push[r : r + 8, :]
        blocks.append((here, [at * mnrm[c, r : r + 8, :] for c in range(3)]))
    for r in (0, 8):
        at = slot[r : r + 8, :]
        (size,) = gather(mine, (0,), ((at >> 12) << 6) + (at & 63), (at >> 6) & 63, 64)
        blocks.append((slave[r : r + 8, :], [size * nrm[16 * c + r : 16 * c + r + 8, :] for c in range(3)]))
    pairs = [place(here & 127, here >> 7, w, held, 64 * k) for k, (here, w) in enumerate(blocks)]
    acc[...] = lax.dot_general(
        jnp.concatenate([pair[0] for pair in pairs], 1),
        jnp.concatenate([pair[1] for pair in pairs], 1),
        NT,
        preferred_element_type=F32,
    )
    contact[...] = acc[0:96, :] + acc[96:192, :]
    tot[...] = net[...] + contact[...]

    def vals(r):
        p = [x[c * ROWS + r : c * ROWS + r + 8, :] for c in range(3)]
        n = [tot[c * ROWS + r : c * ROWS + r + 8, :] for c in range(3)]
        return [
            *n,
            p[1] * n[2] - p[2] * n[1],
            p[2] * n[0] - p[0] * n[2],
            p[0] * n[1] - p[1] * n[0],
        ]

    part_sums(part, vals, acc2, False)
    acc2[0:48, :] = acc2[0:48, :] + acc2[48:96, :]
    lane = lax.broadcasted_iota(jnp.int32, (8, LANES), 1)
    last = jnp.zeros((8, LANES), F32)
    for k in range(6):
        piece = jnp.where(lane < 16, acc2[8 * k : 8 * k + 8, :], 0.0)
        last = last + (pltpu.roll(piece, 16 * k, 1) if k else piece)
    even = lax.axis_index("dom") & 1 == 0
    pairs = [(acc2[8 * k : 8 * k + 1, :], acc2[8 * k + 2 : 8 * k + 3, :]) for k in range(6)]
    pairs += [(acc2[8 * k + 1 : 8 * k + 2, :], acc2[8 * k + 25 : 8 * k + 26, :]) for k in range(3)]
    pairs += [(jnp.zeros((1, LANES), F32), last[3:4, :])]
    for k, (low, high) in enumerate(pairs):
        keep[k : k + 1, :] = jnp.where(even, low, high)
        give[k : k + 1, :] = jnp.where(even, high, low)
    keep[10:16, :] = jnp.zeros((6, LANES), F32)
    give[10:16, :] = jnp.zeros((6, LANES), F32)
    moments = jnp.broadcast_to(jnp.sum(got[every(2, 3), :], axis=0, keepdims=True), (8, LANES))
    moments = jnp.where(lane < 96, 0.0, pltpu.roll(moments, 96, 1))
    keep[9:10, :] = keep[9:10, :] + moments[0:1, :]


def nodal_kernel(v, contact, mass, nodal):
    for c in range(3):
        at = slice(c * ROWS, (c + 1) * ROWS)
        speed = v[at, :] + TIME_STEP * contact[at, :] / mass[...]
        for h in range(ROWS):
            nodal[c : c + 1, h * LANES : (h + 1) * LANES] = speed[h : h + 1, :]


def spread_kernel(keep, given, out):
    tile = (keep[...] + given[...])[0:10, :]
    four = jnp.concatenate([tile] * 4, 0)
    for k in range(16):
        out[40 * k : 40 * k + 40, :] = four


def total_kernel(got, out):
    four = got[0:40, :]
    for k in range(1, 16):
        four = four + got[40 * k : 40 * k + 40, :]
    out[0:10, :] = four[0:10, :] + four[10:20, :] + four[20:30, :] + four[30:40, :]
    out[10:16, :] = jnp.zeros((6, LANES), F32)
    out[16:80, :] = pltpu.roll(got[every(9, 10, 64), :], 32, 1)


def motion_kernel(mine, other, rigid, out):
    even = lax.axis_index("dom") & 1 == 0
    low = jnp.where(even, mine[...], other[...])
    high = jnp.where(even, other[...], mine[...])
    by = jnp.concatenate([low[16:80, :], high[16:80, :]], 0).T
    moments = [by[8 * k : 8 * k + 4, :] for k in range(4)]
    sums = []
    for k in range(6):
        second = low[6 + k : 7 + k, :] if k < 3 else high[3 + k : 4 + k, :]
        last = pltpu.roll(high[8:16, :], LANES - 16 * k, 1) if k else high[8:16, :]
        sums.append(jnp.concatenate([low[k : k + 1, :], second, high[k : k + 1, :], last[1:2, :]], 0))
    own = rigid[0:4, :]
    mass = own + moments[0]
    centre = [(own * rigid[8 + 8 * c : 12 + 8 * c, :] + moments[1 + c]) / mass for c in range(3)]
    force, turn = sums[0:3], sums[3:6]
    rows = [y / mass for y in force]
    for c in range(3):
        a, b = (c + 1) % 3, (c + 2) % 3
        moment = turn[c] - (centre[a] * force[b] - centre[b] * force[a])
        rows.append(moment / rigid[32 + 8 * c : 36 + 8 * c, :])
    for r, row in enumerate(rows):
        for h, n in spans():
            out[r : r + 1, h * LANES : h * LANES + n] = row[h : h + 1, 0:n]


def partner(block, apart):
    count = lax.axis_size("dom")
    return lax.ppermute(block, "dom", [(i, i ^ (1 << apart)) for i in range(count)])


def in_hbm(*arrays):
    return [pltpu.with_memory_space_constraint(x, pltpu.HBM) for x in arrays]


def later(value, than):
    return lax.optimization_barrier((value, than))[0]


def swap(block, groups=None):
    peers = len(groups[0]) if groups else lax.axis_size("dom")
    flat = block.reshape(peers, 1, -1)
    return lax.all_to_all(flat, "dom", 0, 0, tiled=True, axis_index_groups=groups).reshape(block.shape)


def per_device(
    rest_pos,
    displacement,
    velocity,
    ext_force,
    node_mass,
    body_accel,
    connectivity,
    elem_material,
    stiffness,
    shared_nodes,
    contact_slave,
    contact_owner,
    contact_master,
    contact_normal,
    part_of_node,
    part_mass,
    part_center,
    part_inertia,
):
    state = ((96, LANES), F32)
    table = ((5 * LANES, LANES), F32)
    own = [((3, LANES), F32)] * NBR
    work = [
        pltpu.VMEM((96, LANES), F32),
        pltpu.VMEM((24 * TOGETHER, LANES), F32),
        pltpu.VMEM((192, LANES), F32),
        pltpu.VMEM((64 * TOGETHER, LANES), F32),
    ]
    inputs = (
        stiffness,
        contact_owner.reshape(16, LANES),
        contact_master.reshape(16, LANES),
        contact_normal,
        displacement,
        velocity,
        connectivity,
        elem_material,
        shared_nodes.transpose(1, 0, 2),
        ext_force,
        node_mass.reshape(ROWS, LANES),
        body_accel,
        contact_slave.reshape(16, LANES),
    )
    rows, ints = ((ROWS, LANES), F32), jnp.int32
    whole, map_rows = pltpu.VMEM((3, 4096), F32), ((ROWS, LANES), ints)
    u, v, fm, mass, idx, inv, cols, shared, internal, send, slave, slot, normal, mat = call(
        first_kernel,
        [
            state,
            state,
            state,
            rows,
            ((8, 4096), ints),
            map_rows,
            ((192, 24, LANES), F32),
            ((8, LANES), ints),
            state,
            table,
            ((16, LANES), ints),
            ((16, LANES), ints),
            ((3, 2048), F32),
            ((ROWS,), ints),
        ],
        [HBM] * 13,
        "first_cycle",
        [
            whole,
            whole,
            whole,
            pltpu.VMEM((NBR, 1, LANES), ints),
            pltpu.VMEM((16, LANES), ints),
            pltpu.VMEM((16, LANES), ints),
            pltpu.VMEM((8, 24, 24), F32),
            pltpu.SMEM((3,), F32),
            pltpu.VMEM((8, 4096), ints),
            pltpu.SMEM((ROWS,), ints),
            *work,
            pltpu.VMEM((LANES, LANES), F32),
            pltpu.VMEM((LANES, 2 * LANES), F32),
            pltpu.SemaphoreType.DMA((14,)),
        ],
    )(*in_hbm(*inputs))
    got = swap(send)
    trio = ((3, PARTS_SIZE), F32)
    recv = [got]
    for n in range(CYCLES - 1):
        u, v, internal, *mine = call(
            functools.partial(next_kernel, n == 0),
            [state, state, state, *own],
            [VMEM] * (10 + len(recv)),
            "next_cycle",
            [*work, pltpu.SMEM((ROWS,), ints), pltpu.SemaphoreType.DMA],
        )(u, v, internal, inv, fm, mass, idx, mat, cols, shared, *recv)
        recv = [partner(mine[b], b) for b in range(NBR)]
        if n == 0:
            midx, mnrm, code = call(
                ends_kernel,
                [((64, LANES), ints), ((3, 64, LANES), F32), ((80, LANES), ints)],
                [VMEM] * 3,
                "contact_ends",
            )(later(got, mine), slave, inv)
            pos, part, nrm, light, rigid = call(
                fixed_kernel,
                [state, map_rows, ((48, LANES), F32), ((8, LANES), F32), ((56, LANES), F32)],
                [HBM] * 5 + [VMEM] * 3,
                "fixed_data",
                [
                    whole,
                    pltpu.VMEM((1, PARTS_SIZE), F32),
                    pltpu.VMEM(*trio),
                    pltpu.VMEM(*trio),
                    pltpu.SemaphoreType.DMA((5,)),
                ],
            )(
                *in_hbm(
                    rest_pos,
                    part_of_node.reshape(ROWS, LANES),
                    part_mass.reshape(1, PARTS_SIZE),
                    part_center,
                    part_inertia,
                ),
                later(normal, mine),
                shared,
                mass,
            )
            recv, code, nrm = lax.optimization_barrier((recv, code, nrm))
    both = ((2, 80, LANES), F32)
    x, v, ab = call(
        base_kernel,
        [state, state, both],
        [VMEM] * 10,
        "contact_base",
        [pltpu.VMEM((192, LANES), F32)],
    )(u, v, internal, fm, mass, pos, slave, nrm, midx, mnrm)
    x, v, net, dots = call(
        dots_kernel,
        [state, state, state, ((3 * LANES, LANES), F32)],
        [VMEM] * 18,
        "contact_dots",
        [pltpu.VMEM((64, LANES), F32), pltpu.VMEM((LANES, LANES), F32), pltpu.VMEM(*both)],
    )(x, v, ab, internal, inv, light, fm, mass, part, slot, nrm, mnrm, code, *recv)
    half = ((16, LANES), F32)
    contact, keep, give = call(
        contact_kernel,
        [state, half, half],
        [VMEM] * 10,
        "contact_forces",
        [
            pltpu.VMEM((192, LANES), F32),
            pltpu.VMEM((96, LANES), F32),
            pltpu.VMEM((96, LANES), F32),
            pltpu.VMEM((64, LANES), F32),
            pltpu.VMEM((64, LANES), F32),
            pltpu.VMEM((640, LANES), F32),
        ],
    )(dots, swap(dots), slave, slot, nrm, midx, mnrm, x, net, part)
    (nodal_velocity,) = call(nodal_kernel, [((3, 4096), F32)], [VMEM] * 3, "nodal_velocity")(v, contact, mass)
    (spread,) = call(spread_kernel, [((640, LANES), F32)], [VMEM] * 2, "part_spread")(keep, partner(give, 0))
    chips = lax.axis_size("dom") // 2
    groups = [[2 * i + core for i in range(chips)] for core in range(2)]
    (total,) = call(total_kernel, [((80, LANES), F32)], [VMEM], "part_totals")(swap(spread, groups))
    (motion,) = call(motion_kernel, [((6, PARTS_SIZE), F32)], [VMEM] * 3, "part_motion")(
        total, partner(total, 0), rigid
    )
    return nodal_velocity, motion


def solution(mesh):
    placed = (
        P(None, "dom"),
        P(None, "dom"),
        P(None, "dom"),
        P(None, "dom"),
        P("dom"),
        P(),
        P(None, "dom"),
        P("dom"),
        P(),
        P("dom", None, None),
        P("dom"),
        P("dom", None),
        P("dom"),
        P(None, "dom"),
        P("dom"),
        P(),
        P(),
        P(),
    )
    return jax.shard_map(
        per_device, mesh=mesh, in_specs=placed, out_specs=(P(None, "dom"), P()), check_vma=False
    )
```
